32 devices in a mesh: dp: 16 (over z, y, core), tensor: 2 (over x).
Axes of the slice: x: 2, y: 2, z: 4, core: 2. Of those that a mesh axis runs over, the one named last changes fastest.
Arguments:
- tokens: bfloat16 [8192, 2048], P('dp'), may hold values from -6 to 6
- w_query: float32 [2048, 1536], P('dp', 'tensor'), may hold values from -0.125 to 0.125
- w_keyval: float32 [2048, 768], P('dp'), may hold values from -0.125 to 0.125
- w_out: float32 [1536, 2048], P('tensor', 'dp'), may hold values from -2.5 to 2.5
- w_gateup: float32 [2048, 2, 5120], P('dp', None, 'tensor'), may hold values from -0.125 to 0.125
- w_down: float32 [5120, 2048], P('tensor', 'dp'), may hold values from -0.15625 to 0.15625
- attn_gain: float32 [2048], P('dp'), may hold values from 0.1 to 1.9
- ffn_gain: float32 [2048], P('dp'), may hold values from 0.1 to 1.9
- qk_gain: float32 [2, 64], P(None, 'dp'), may hold values from 1 to 2
- segments: int32 [8192], P('dp'), may hold values from 0 to 3, as said below
- positions: int32 [8192], P('dp'), may hold values from 0 to 8191, as said below
- cotangent: bfloat16 [8192, 2048], P('dp'), may hold values from -6 to 6
Outputs:
- output: bfloat16 [8192, 2048], P('dp')
- input_grad: bfloat16 [8192, 2048], P('dp')
- grad_query: float32 [2048, 1536], P('dp', 'tensor')
- grad_keyval: float32 [2048, 768], P('dp')
- grad_out: float32 [1536, 2048], P('tensor', 'dp')
- grad_gateup: float32 [2048, 2, 5120], P('dp', None, 'tensor')
- grad_down: float32 [5120, 2048], P('tensor', 'dp')
- grad_attn_gain: float32 [2048], P('dp')
- grad_ffn_gain: float32 [2048], P('dp')
- grad_qk_gain: float32 [2, 64], P(None, 'dp')
The draws below stay inside these ranges and needn't reach their ends.
Inputs may be any that keep to these rules, and one draw needn't show every extreme that they name: `segments`: each sequence of 8192 tokens holds 4 documents, contiguous runs of tokens numbered 0, 1, 2 ... in order; the numbering starts again in each sequence. Within a document each token has the position of the one before plus one. A document's first position is below 1024 and at most 8192 minus its length, except the last document of each sequence, whose positions are the tokens' places in their sequence.
All inputs are finite; a program needn't handle non-finite values.
Results may differ from the reference program's by a relative error of at most 0.02.
The reference program's roundings to bfloat16 on the way count: a program that leaves them out, or rounds other values in their place, can miss the bound.
Values may be sent and summed in bfloat16 or wider, within the bound.
No kernel may reach another device: no remote copies, remote signals or barrier semaphores. Data moves between devices by JAX's collectives and lax.ppermute only.
A program may use at most 320 MiB of HBM per device.

```python
import math
import jax
import jax.numpy as jnp
from jax import lax

D = 2048
QH = 24
KVH = 6
HD = 64
FF = 5120
WINDOW = 1024
QW = 1536
KVW = 384
TOKENS = 8192
SEQ = 8192
DOCS = 4


def doc_starts(key):
    seq_keys = jax.random.split(key, TOKENS // SEQ)

    def one_sequence(seq_key):
        shuffled = jax.random.permutation(seq_key, SEQ - 1)
        return shuffled[:DOCS - 1].astype(jnp.int32) + 1
    return jax.vmap(one_sequence)(seq_keys)


def draw_segments(key, part):
    cut_points = doc_starts(key)
    places = jnp.arange(SEQ, dtype=jnp.int32)
    counted = jnp.sum((places[None, :, None] >= cut_points[:, None, :]).astype(jnp.int32), axis=2)
    return counted.reshape(TOKENS)


def sequence_positions(cut_points, shift_key):
    places = jnp.arange(SEQ, dtype=jnp.int32)
    past_cut = places[:, None] >= cut_points[None, :]
    doc_index = jnp.sum(past_cut.astype(jnp.int32), axis=1)
    begins = jnp.max(jnp.where(past_cut, cut_points[None, :], 0), axis=1)
    ordered = jnp.sort(cut_points)
    doc_begin = jnp.concatenate([jnp.zeros((1,), jnp.int32), ordered])
    doc_end = jnp.concatenate([ordered, jnp.full((1,), SEQ, jnp.int32)])
    doc_length = doc_end - doc_begin
    upper = jnp.minimum(1024, SEQ - doc_length + 1).astype(jnp.int32)
    shifts = jax.random.randint(shift_key, (DOCS,), 0, upper, dtype=jnp.int32)
    shifts = shifts.at[DOCS - 1].set(doc_begin[DOCS - 1])
    return shifts[doc_index] + places - begins


def draw_positions(key, part):
    cut_points = doc_starts(key)
    key = jax.random.fold_in(key, 5)
    shift_keys = jax.random.split(key, TOKENS // SEQ)
    return jax.vmap(sequence_positions)(cut_points, shift_keys).reshape(TOKENS)


def block_scale(rng, shape, cuts, low, top_value):
    level = 1.0
    for axis_at, parts in cuts:
        steps = jax.random.uniform(jax.random.fold_in(jax.random.fold_in(rng, 6), axis_at), (parts,), jnp.float32, low / len(cuts), top_value / len(cuts))
        level = level * jnp.repeat(jnp.exp(steps), shape[axis_at] // parts).reshape((-1,) + (1,) * (len(shape) - 1 - axis_at))
    return level


def normal_values(key, dims, spread, most, shards=(), kind=jnp.bfloat16):
    array = jax.random.normal(key, dims, jnp.float32) * spread
    if len(shards) > 0:
        array = block_scale(key, dims, shards, -0.22, 0.18) * array
    return jnp.clip(array, min=-most, max=most).astype(kind)


def setup_inputs(seed: int = 0) -> dict:
    streams_of = jax.random.split(jax.random.key(seed), 13)
    tokens = normal_values(streams_of[0], (TOKENS, D), 1.0, 6.0, ((0, 16),))
    w_query = normal_values(streams_of[1], (D, QW), D ** -0.5, 0.125, ((0, 16), (1, 2)), jnp.float32)
    w_keyval = normal_values(streams_of[2], (D, 2 * KVW), D ** -0.5, 0.125, ((0, 16),), jnp.float32)
    w_out = normal_values(streams_of[3], (QW, D), (max(QW // 256, 1)) ** -0.5, 2.5, ((0, 2), (1, 16)), jnp.float32)
    w_gateup = normal_values(streams_of[4], (D, 2, FF), D ** -0.5, 0.125, ((0, 16), (2, 2)), jnp.float32)
    w_down = normal_values(streams_of[5], (FF, D), (FF // 3) ** -0.5, 0.15625, ((0, 2), (1, 16)), jnp.float32)
    attn_gain = jnp.clip(1.0 + 0.18 * jax.random.normal(streams_of[6], (D,), jnp.float32), 0.1, 1.9)
    ffn_gain = jnp.clip(1.0 + 0.18 * jax.random.normal(streams_of[7], (D,), jnp.float32), 0.1, 1.9)
    qk_gain = jnp.clip(1.0 + 1.0 * jax.random.uniform(streams_of[8], (2, HD), jnp.float32) ** block_scale(streams_of[8], (2, HD), ((1, 16),), -0.2, 0.2), 1.0, 2.0)
    segments = draw_segments(jax.random.fold_in(streams_of[12], 71), 0)
    positions = draw_positions(jax.random.fold_in(streams_of[12], 71), 0)
    cotangent = normal_values(streams_of[11], (TOKENS, D), 1.0, 6.0, ((0, 16),))
    return {"tokens": tokens, "w_query": w_query, "w_keyval": w_keyval, "w_out": w_out, "w_gateup": w_gateup, "w_down": w_down, "attn_gain": attn_gain, "ffn_gain": ffn_gain, "qk_gain": qk_gain, "segments": segments, "positions": positions, "cotangent": cotangent}


EPSILON = 1e-06
SCORE_SCALE = 0.125
MASKED = -1e+30
ROPE_BASE = 10000.0
HIGHEST = lax.Precision.HIGHEST

@jax.custom_vjp
def low(v):
    return lax.optimization_barrier(v.astype(jnp.bfloat16)).astype(jnp.float32)

@jax.custom_vjp
def low_back(v):
    return v

def low_keep(v):
    return (low(v), None)

def low_pass(kept, grad):
    return (grad,)

def back_keep(v):
    return (v, None)

def back_low(kept, grad):
    return (low(grad),)
low.defvjp(low_keep, low_pass)
low_back.defvjp(back_keep, back_low)

def rms_norm(values, weight):
    return values * lax.rsqrt(lax.optimization_barrier(jnp.mean(values * values, axis=-1, keepdims=True)) + EPSILON) * weight

def rotate(values, cos_table, sin_table):
    half_width = values.shape[-1] // 2
    first_half = values[..., :half_width]
    second_half = values[..., half_width:]
    return jnp.concatenate([first_half * cos_table - second_half * sin_table, second_half * cos_table + first_half * sin_table], axis=-1)

def angles_of(positions):
    half_width = HD // 2
    frequency = jnp.exp(jnp.arange(half_width, dtype=jnp.float32) * (-math.log(ROPE_BASE) / half_width))
    phases = positions.astype(jnp.float32)[:, None] * frequency[None, :]
    return (jnp.cos(phases)[:, None, :], jnp.sin(phases)[:, None, :])

def attention(queries, keys, values, segments):
    group = QH // KVH
    block_rows = min(TOKENS, 512)
    block_count = TOKENS // block_rows
    seq_marks = (segments.astype(jnp.int32) + jnp.arange(TOKENS, dtype=jnp.int32) // SEQ * DOCS).astype(jnp.int32)
    query_groups = queries.reshape(TOKENS, KVH, group, HD)
    key_padded = jnp.concatenate([jnp.zeros((WINDOW, KVH, HD), keys.dtype), keys])
    value_padded = jnp.concatenate([jnp.zeros((WINDOW, KVH, HD), values.dtype), values])
    seg_padded = jnp.concatenate([jnp.full((WINDOW,), -1, jnp.int32), seq_marks])

    def attend_block(block_index):
        block_start = (block_index * block_rows).astype(jnp.int32)
        query_block = lax.dynamic_slice_in_dim(query_groups, block_start, block_rows, 0)
        key_block = lax.dynamic_slice_in_dim(key_padded, block_start, WINDOW + block_rows, 0)
        value_block = lax.dynamic_slice_in_dim(value_padded, block_start, WINDOW + block_rows, 0)
        seg_query = lax.dynamic_slice_in_dim(seq_marks, block_start, block_rows, 0)
        seg_key = lax.dynamic_slice_in_dim(seg_padded, block_start, WINDOW + block_rows, 0)
        scores = low_back(jnp.einsum('qhgd,khd->hgqk', query_block, key_block, precision=HIGHEST) * SCORE_SCALE)
        distance = jnp.arange(block_rows, dtype=jnp.int32)[:, None] + WINDOW - jnp.arange(WINDOW + block_rows, dtype=jnp.int32)[None, :]
        allowed = (distance >= 0) & (distance < WINDOW) & (seg_query[:, None] == seg_key[None, :])
        scores = jnp.where(allowed[None, None], scores, MASKED)
        row_max = lax.optimization_barrier(jnp.max(scores, axis=-1, keepdims=True))
        scaled = jnp.exp(scores - row_max)
        probability = low(scaled / lax.optimization_barrier(jnp.sum(scaled, axis=-1, keepdims=True)))
        return jnp.einsum('hgqk,khd->qhgd', probability, value_block, precision=HIGHEST)
    result = lax.map(jax.checkpoint(attend_block), jnp.arange(block_count, dtype=jnp.int32))
    return result.reshape(TOKENS, QW)

def feed_forward(mid, ffn_weight, gateup_weight, down_weight):
    block_rows = math.gcd(TOKENS, 4096)

    def ffn_block(mid_block):
        normed2 = low(rms_norm(mid_block, ffn_weight))
        gate_up = low_back(jnp.einsum('td,dcf->tcf', normed2, gateup_weight, precision=HIGHEST))
        act = low(jax.nn.silu(gate_up[:, 0]) * gate_up[:, 1])
        return mid_block + low_back(jnp.dot(act, down_weight, precision=HIGHEST))
    result = lax.map(jax.checkpoint(ffn_block), mid.reshape(TOKENS // block_rows, block_rows, D))
    return result.reshape(TOKENS, D)

def layer(inputs, w_query, w_keyval, w_out, w_gateup, w_down, attn_gain, ffn_gain, qk_gain, segments, cos_table, sin_table):
    query_weight = low(w_query)
    keyval_weight = low(w_keyval)
    out_weight = low(w_out)
    gateup_weight = low(w_gateup)
    down_weight = low(w_down)
    attn_weight = low(attn_gain)
    ffn_weight = low(ffn_gain)
    head_gains = low(qk_gain)
    normed = low(rms_norm(inputs, attn_weight))
    query_raw = low_back(jnp.dot(normed, query_weight, precision=HIGHEST))
    keyval_raw = low_back(jnp.dot(normed, keyval_weight, precision=HIGHEST))
    queries = low(rotate(rms_norm(query_raw.reshape(TOKENS, QH, HD), head_gains[0]), cos_table, sin_table))
    keys = low(rotate(rms_norm(keyval_raw[:, :KVW].reshape(TOKENS, KVH, HD), head_gains[1]), cos_table, sin_table))
    values = low(keyval_raw[:, KVW:].reshape(TOKENS, KVH, HD))
    attended = low_back(low(attention(queries, keys, values, segments)))
    mid = inputs + low_back(jnp.dot(attended, out_weight, precision=HIGHEST))
    return feed_forward(mid, ffn_weight, gateup_weight, down_weight)

def reference(tokens, w_query, w_keyval, w_out, w_gateup, w_down, attn_gain, ffn_gain, qk_gain, segments, positions, cotangent):
    cos_table, sin_table = angles_of(positions)

    def forward(inputs, query_w, keyval_w, out_w, gateup_w, down_w, attn_w, ffn_w, head_w):
        return layer(inputs, query_w, keyval_w, out_w, gateup_w, down_w, attn_w, ffn_w, head_w, segments, cos_table, sin_table)
    result, pull = jax.vjp(forward, tokens.astype(jnp.float32), w_query, w_keyval, w_out, w_gateup, w_down, attn_gain, ffn_gain, qk_gain)
    grads = pull(cotangent.astype(jnp.float32))
    return (result.astype(jnp.bfloat16), grads[0].astype(jnp.bfloat16), grads[1], grads[2], grads[3], grads[4], grads[5], grads[6], grads[7], grads[8])
```

```python
import math

import jax
import jax.numpy as jnp
from jax import lax
from jax.sharding import PartitionSpec as P

QH = 24
KVH = 6
HD = 64
GROUP = QH // KVH
WINDOW = 1024
SEQ_LEN = 8192
LANES = 128

EPSILON = 1e-06
SCORE_SCALE = 0.125
MASKED = -1e30
ROPE_BASE = 10000.0

bf16 = jnp.bfloat16
f32 = jnp.float32


def angles_of(positions):
    half_width = HD // 2
    frequency = jnp.exp(
        jnp.arange(half_width, dtype=f32) * (-math.log(ROPE_BASE) / half_width)
    )
    phases = positions.astype(f32)[:, None] * frequency[None, :]
    return jnp.cos(phases)[:, None, :], jnp.sin(phases)[:, None, :]


def rotate(values, cos_table, sin_table):
    half_width = values.shape[-1] // 2
    first_half = values[..., :half_width]
    second_half = values[..., half_width:]
    return jnp.concatenate(
        [
            first_half * cos_table - second_half * sin_table,
            second_half * cos_table + first_half * sin_table,
        ],
        axis=-1,
    )


def inverse_rms(values):
    return lax.rsqrt(jnp.mean(values * values, axis=-1, keepdims=True) + EPSILON)


def rms_back(values, scale, weight, d_out):
    weighted = d_out * weight
    pull = jnp.mean(weighted * values, axis=-1, keepdims=True)
    return scale * weighted - values * (scale * scale * scale * pull)


class Ring:
    def __init__(self):
        self.count = lax.axis_size("dp")
        self.outer = self.count // 4
        index = lax.axis_index("dp")
        self.index = index
        self.core = index % 2
        self.mid = (index // 2) % 2
        self.place = index // 4
        self.core_pairs = [(i, i ^ 1) for i in range(self.count)]
        self.mid_pairs = [(i, i ^ 2) for i in range(self.count)]

    def pick(self, array, bit, axis):
        return lax.dynamic_index_in_dim(array, bit, axis, keepdims=False)

    def columns(self, array):
        tokens, width = array.shape
        blocks = array.reshape(tokens, self.outer, 2, 2, width // self.count)
        halves = []
        for bit in (1 - self.core, self.core):
            half = self.pick(blocks, bit, 3)
            both = [self.pick(half, self.mid, 2), self.pick(half, 1 - self.mid, 2)]
            halves.append([part.reshape(tokens, width // 4) for part in both])
        return halves

    def rows(self, array):
        width, count = array.shape
        blocks = array.reshape(self.outer, 2, 2, width // self.count, count)
        halves = []
        for bit in (1 - self.core, self.core):
            half = self.pick(blocks, bit, 2)
            both = [self.pick(half, self.mid, 1), self.pick(half, 1 - self.mid, 1)]
            halves.append([part.reshape(width // 4, count) for part in both])
        return halves

    def chain(self, blocks):
        outer = self.outer
        from_above = None
        from_below = None
        for step in range(outer - 1):
            down_block = jnp.clip(step - outer + 1 + self.place, 0, outer - 1)
            up_block = jnp.clip(self.place + outer - 1 - step, 0, outer - 1)
            down = self.pick(blocks, down_block, 0)
            up = self.pick(blocks, up_block, 0)
            if step > 0:
                down = (down.astype(f32) + from_above.astype(f32)).astype(bf16)
                up = (up.astype(f32) + from_below.astype(f32)).astype(bf16)
            down_pairs = []
            up_pairs = []
            for i in range(self.count):
                place = i // 4
                if place >= max(1, outer - 1 - step):
                    down_pairs.append((i, i - 4))
                if place <= min(outer - 2, step):
                    up_pairs.append((i, i + 4))
            from_above = lax.ppermute(down, "dp", down_pairs)
            from_below = lax.ppermute(up, "dp", up_pairs)
        total = self.pick(blocks, self.place, 0).astype(f32)
        if outer > 1:
            total = total + (from_above.astype(f32) + from_below.astype(f32))
        return total

    def scatter(self, make):
        to_core = [make(0, part).astype(bf16) for part in (1, 0)]
        got = [lax.ppermute(part, "dp", self.core_pairs) for part in to_core]
        to_mid = (make(1, 1) + got[0].astype(f32)).astype(bf16)
        got_mid = lax.ppermute(to_mid, "dp", self.mid_pairs)
        kept = (make(1, 0) + got[1].astype(f32) + got_mid.astype(f32)).astype(bf16)
        return self.chain(kept.reshape((self.outer, -1) + kept.shape[1:]))


def other_tensor(array):
    count = lax.axis_size("tensor")
    return lax.ppermute(array, "tensor", [(i, (i + 1) % count) for i in range(count)])


def tensor_sum(partial):
    low = partial.astype(bf16)
    return low.astype(f32) + other_tensor(low).astype(f32)


def from_behind(shard, by):
    length = lax.axis_size("dp")
    pairs = [(i, i + by) for i in range(length) if 0 <= i + by < length]
    return lax.ppermute(shard, "dp", pairs)


def tn_dot(left, right):
    return lax.dot_general(left, right, (((0,), (0,)), ((), ())), preferred_element_type=f32)


def nt_dot(left, right):
    return lax.dot_general(left, right, (((1,), (1,)), ((), ())), preferred_element_type=f32)


def nn_dot(left, right):
    return jnp.dot(left, right, preferred_element_type=f32)


def shards(
    tokens,
    w_query,
    w_keyval,
    w_out,
    w_gateup,
    w_down,
    attn_gain,
    ffn_gain,
    qk_gain,
    segments,
    positions,
    cotangent,
):
    ring = Ring()
    row_count = tokens.shape[0]
    depth = w_query.shape[0]
    model = tokens.shape[1]
    hidden = w_gateup.shape[2]
    tensor = lax.axis_index("tensor")
    query_width = w_query.shape[1]
    local_heads = query_width // HD
    local_kv = local_heads // GROUP
    kv_width = local_kv * HD
    all_kv = w_keyval.shape[1] // 2
    gain_count = 2 * qk_gain.shape[1]

    own_keyval = lax.dynamic_index_in_dim(
        w_keyval.reshape(depth, 2, all_kv // kv_width, kv_width), tensor, 2, keepdims=False
    ).reshape(depth, 2 * kv_width)
    head_gain_column = jnp.pad(qk_gain.reshape(gain_count), (0, depth - gain_count))
    gains = jnp.stack([attn_gain, ffn_gain, head_gain_column], axis=1)
    gains = jnp.pad(gains, ((0, 0), (0, LANES - gains.shape[1])))
    attn_pack = jnp.concatenate([w_query, own_keyval, w_out.T, gains], axis=1).astype(bf16)
    attn_full = lax.all_gather(attn_pack, "dp", axis=0, tiled=True)
    gateup_full = lax.all_gather(
        w_gateup.reshape(depth, 2 * hidden).astype(bf16), "dp", axis=0, tiled=True
    )
    down_full = lax.all_gather(w_down.T.astype(bf16), "dp", axis=0, tiled=True)

    marks = (segments + 1).astype(bf16)
    seq_devices = min(SEQ_LEN // row_count, ring.count)
    own_sequence = ring.index // seq_devices
    reach_count = -(-WINDOW // row_count)
    halo_marks = []
    for step_back in range(reach_count, 0, -1):
        same_sequence = ((ring.index - step_back) // seq_devices == own_sequence).astype(bf16)
        halo_marks.append(from_behind(marks, step_back) * same_sequence)
    key_marks = jnp.concatenate(halo_marks + [marks], axis=0)
    key_count = key_marks.shape[0]
    cos_table, sin_table = angles_of(positions)

    residual = tokens.astype(f32)
    attn_scale = inverse_rms(residual)

    qkv_full = attn_full[:, : query_width + 2 * kv_width]
    query_full = qkv_full[:, :query_width]
    keyval_full = qkv_full[:, query_width:]
    out_start = query_width + 2 * kv_width
    out_full = attn_full[:, out_start : out_start + query_width]
    gain_start = out_start + query_width
    gain_columns = attn_full[:, gain_start : gain_start + 3].astype(f32)
    attn_weight = gain_columns[:, 0]
    ffn_weight = gain_columns[:, 1]
    head_gains = gain_columns[:, 2].reshape(ring.count, depth)[:, :gain_count]
    head_gains = head_gains.reshape(ring.count, 2, qk_gain.shape[1]).transpose(1, 0, 2).reshape(2, HD)
    gain_query = head_gains[0]
    gain_key = head_gains[1]

    normed_low = (residual * attn_scale * attn_weight).astype(bf16)
    query_raw = nn_dot(normed_low, query_full).reshape(row_count, local_heads, HD)
    keyval_raw = nn_dot(normed_low, keyval_full)
    key_raw = keyval_raw[:, :kv_width].reshape(row_count, local_kv, HD)
    query_scale = inverse_rms(query_raw)
    key_scale = inverse_rms(key_raw)
    query_low = rotate(query_raw * query_scale * gain_query, cos_table, sin_table).astype(bf16)
    key_low = rotate(key_raw * key_scale * gain_key, cos_table, sin_table).astype(bf16)
    keyval_low = jnp.concatenate(
        [key_low.reshape(row_count, kv_width), keyval_raw[:, kv_width:].astype(bf16)], axis=1
    )
    halo = [from_behind(keyval_low, step_back) for step_back in range(reach_count, 0, -1)]
    key_keyval = jnp.concatenate(halo + [keyval_low], axis=0)
    keys = key_keyval[:, :kv_width].reshape(key_count, local_kv, HD)
    values = key_keyval[:, kv_width:].reshape(key_count, local_kv, HD)
    query_groups = query_low.reshape(row_count, local_kv, GROUP, HD)
    distance = (jnp.arange(row_count, dtype=jnp.int32) + reach_count * row_count)[
        :, None
    ] - jnp.arange(key_count, dtype=jnp.int32)[None, :]
    allowed = (distance >= 0) & (distance < WINDOW) & (marks[:, None] == key_marks[None, :])

    def masked_scores():
        scores = jnp.einsum("qhgd,khd->hgqk", query_groups, keys, preferred_element_type=f32)
        return jnp.where(allowed[None, None], scores * SCORE_SCALE, MASKED)

    scores = masked_scores()
    row_max = jnp.max(scores, axis=-1, keepdims=True)
    scaled = jnp.exp(scores - row_max)
    row_total = jnp.sum(scaled, axis=-1, keepdims=True)
    probability = (scaled / row_total).astype(bf16)
    attended = jnp.einsum("hgqk,khd->qhgd", probability, values, preferred_element_type=f32)
    row_lse = row_max + jnp.log(row_total)
    attended_low = attended.reshape(row_count, query_width).astype(bf16)
    mid = residual + tensor_sum(nt_dot(attended_low, out_full))

    ffn_scale = inverse_rms(mid)
    normed2_low = (mid * ffn_scale * ffn_weight).astype(bf16)
    gate = nn_dot(normed2_low, gateup_full[:, :hidden])
    up = nn_dot(normed2_low, gateup_full[:, hidden:])
    gate_sigmoid = jax.nn.sigmoid(gate)
    gate_silu = gate * gate_sigmoid
    act_low = (gate_silu * up).astype(bf16)
    cotangent_parts = ring.columns(cotangent)
    grad_down = ring.scatter(lambda core, mid_at: tn_dot(cotangent_parts[core][mid_at], act_low)).T

    d_act = nn_dot(cotangent, down_full)
    d_gate = (d_act * up * gate_sigmoid * (1.0 + gate * (1.0 - gate_sigmoid))).astype(bf16)
    d_up = (d_act * gate_silu).astype(bf16)
    d_normed2 = tensor_sum(
        nt_dot(d_gate, gateup_full[:, :hidden]) + nt_dot(d_up, gateup_full[:, hidden:])
    )
    normed2_parts = ring.columns(normed2_low)
    grad_gate = ring.scatter(lambda core, mid_at: tn_dot(normed2_parts[core][mid_at], d_gate))
    grad_up = ring.scatter(lambda core, mid_at: tn_dot(normed2_parts[core][mid_at], d_up))
    grad_gateup = jnp.stack([grad_gate, grad_up], axis=1)
    result = mid + tensor_sum(nt_dot(act_low, down_full))
    output = result.astype(bf16)
    d_ffn_weight = jnp.sum(d_normed2 * mid * ffn_scale, axis=0)
    d_mid = cotangent.astype(f32) + rms_back(mid, ffn_scale, ffn_weight, d_normed2)

    d_mid_low = d_mid.astype(bf16)
    d_mid_parts = ring.columns(d_mid_low)
    grad_out = ring.scatter(lambda core, mid_at: tn_dot(d_mid_parts[core][mid_at], attended_low)).T
    d_attended = nn_dot(d_mid_low, out_full).astype(bf16)
    d_groups = d_attended.reshape(row_count, local_kv, GROUP, HD)
    probability = jnp.exp(masked_scores() - row_lse)
    d_prob = jnp.einsum("qhgd,khd->hgqk", d_groups, values, preferred_element_type=f32)
    row_delta = jnp.sum(d_prob * probability, axis=-1, keepdims=True)
    d_scores = (probability * (d_prob - row_delta)).astype(bf16)
    d_query = jnp.einsum("hgqk,khd->qhgd", d_scores, keys, preferred_element_type=f32) * SCORE_SCALE
    d_keys = (
        jnp.einsum("hgqk,qhgd->khd", d_scores, query_groups, preferred_element_type=f32)
        * SCORE_SCALE
    )
    d_values = jnp.einsum(
        "hgqk,qhgd->khd", probability.astype(bf16), d_groups, preferred_element_type=f32
    )
    d_keyval_all = jnp.concatenate(
        [d_keys.reshape(key_count, kv_width), d_values.reshape(key_count, kv_width)], axis=1
    )
    own_grad = d_keyval_all[reach_count * row_count :]
    for step_back in range(1, reach_count + 1):
        piece_start = (reach_count - step_back) * row_count
        piece = d_keyval_all[piece_start : piece_start + row_count].astype(bf16)
        own_grad = own_grad + from_behind(piece, -step_back).astype(f32)

    def head_back(raw, scale, gain, d_rotated):
        d_normed_head = rotate(d_rotated, cos_table, -sin_table)
        d_gain = jnp.sum(d_normed_head * raw * scale, axis=(0, 1))
        return rms_back(raw, scale, gain, d_normed_head), d_gain

    d_query_raw, d_gain_query = head_back(
        query_raw, query_scale, gain_query, d_query.reshape(row_count, local_heads, HD)
    )
    d_key_raw, d_gain_key = head_back(
        key_raw, key_scale, gain_key, own_grad[:, :kv_width].reshape(row_count, local_kv, HD)
    )
    d_qkv_low = jnp.concatenate(
        [
            d_query_raw.reshape(row_count, query_width),
            d_key_raw.reshape(row_count, kv_width),
            own_grad[:, kv_width:],
        ],
        axis=1,
    ).astype(bf16)
    d_normed_part = nt_dot(d_qkv_low, qkv_full)
    d_normed = tensor_sum(d_normed_part)
    d_attn_part = jnp.sum(d_normed_part * residual * attn_scale, axis=0)

    head_rows = jnp.stack([d_gain_query, d_gain_key], axis=0).reshape(2, ring.count, gain_count // 2)
    head_rows = head_rows.transpose(1, 0, 2).reshape(ring.count, gain_count)
    head_column = jnp.pad(head_rows, ((0, 0), (0, depth - gain_count))).reshape(model)
    gain_grads = jnp.stack([d_attn_part, d_ffn_weight, head_column], axis=1)
    gain_grads = jnp.pad(gain_grads, ((0, 0), (0, LANES - gain_grads.shape[1])))
    gain_parts = ring.rows(gain_grads)
    normed_parts = ring.columns(normed_low)
    grad_qkv = ring.scatter(
        lambda core, mid_at: jnp.concatenate(
            [tn_dot(normed_parts[core][mid_at], d_qkv_low), gain_parts[core][mid_at]], axis=1
        )
    )
    grad_query = grad_qkv[:, :query_width]
    shared = grad_qkv[:, query_width:].astype(bf16)
    shared_other = other_tensor(shared).astype(f32)
    shared = shared.astype(f32)
    first = tensor == 0
    keyval_mine = shared[:, : 2 * kv_width].reshape(depth, 2, 1, kv_width)
    keyval_theirs = shared_other[:, : 2 * kv_width].reshape(depth, 2, 1, kv_width)
    grad_keyval = jnp.concatenate(
        [
            jnp.where(first, keyval_mine, keyval_theirs),
            jnp.where(first, keyval_theirs, keyval_mine),
        ],
        axis=2,
    ).reshape(depth, 2 * all_kv)
    gains_mine = shared[:, 2 * kv_width :]
    gains_sum = gains_mine + shared_other[:, 2 * kv_width :]
    grad_attn_gain = gains_sum[:, 0]
    grad_ffn_gain = gains_mine[:, 1]
    grad_heads = gains_sum[:gain_count, 2].reshape(2, gain_count // 2)
    input_grad = (d_mid + rms_back(residual, attn_scale, attn_weight, d_normed)).astype(bf16)
    return (
        output,
        input_grad,
        grad_query,
        grad_keyval,
        grad_out,
        grad_gateup,
        grad_down,
        grad_attn_gain,
        grad_ffn_gain,
        grad_heads,
    )


def solution(mesh):
    in_specs = (
        P("dp", None),
        P("dp", "tensor"),
        P("dp", None),
        P("tensor", "dp"),
        P("dp", None, "tensor"),
        P("tensor", "dp"),
        P("dp"),
        P("dp"),
        P(None, "dp"),
        P("dp"),
        P("dp"),
        P("dp", None),
    )
    out_specs = (
        P("dp", None),
        P("dp", None),
        P("dp", "tensor"),
        P("dp", None),
        P("tensor", "dp"),
        P("dp", None, "tensor"),
        P("tensor", "dp"),
        P("dp"),
        P("dp"),
        P(None, "dp"),
    )
    return jax.shard_map(shards, mesh=mesh, in_specs=in_specs, out_specs=out_specs, check_vma=False)
```

```python
import functools
import math

import jax
import jax.numpy as jnp
from jax import lax
from jax.experimental import pallas as pl
from jax.experimental.pallas import tpu as pltpu
from jax.sharding import PartitionSpec as P

QH = 24
KVH = 6
HD = 64
GROUP = QH // KVH
WINDOW = 1024
SEQ_LEN = 8192
LANES = 128

EPSILON = 1e-06
SCORE_SCALE = 0.125
MASKED = -1e30
ROPE_BASE = 10000.0
EXP2_SCALE = SCORE_SCALE * math.log2(math.e)
TILE = 256
SUM_ROWS = 16

bf16 = jnp.bfloat16
f32 = jnp.float32


def angles_of(positions):
    half_width = HD // 2
    frequency = jnp.exp(
        jnp.arange(half_width, dtype=f32) * (-math.log(ROPE_BASE) / half_width)
    )
    phases = frequency[:, None] * positions.astype(f32)[None, :]
    return jnp.cos(phases)[None], jnp.sin(phases)[None]


def rotate(values, cos_table, sin_table):
    half_width = values.shape[1] // 2
    first_half = values[:, :half_width]
    second_half = values[:, half_width:]
    return jnp.concatenate(
        [
            first_half * cos_table - second_half * sin_table,
            second_half * cos_table + first_half * sin_table,
        ],
        axis=1,
    )


def inverse_rms(values, axis):
    return lax.rsqrt(jnp.mean(values * values, axis=axis, keepdims=True) + EPSILON)


def rms_back(values, scale, weight, d_out, axis):
    weighted = d_out * weight
    pull = jnp.mean(weighted * values, axis=axis, keepdims=True)
    return scale * weighted - values * (scale * scale * scale * pull)


class Ring:
    def __init__(self):
        self.count = lax.axis_size("dp")
        self.outer = self.count // 4
        index = lax.axis_index("dp")
        self.index = index
        self.core = index % 2
        self.mid = (index // 2) % 2
        self.place = index // 4
        self.core_pairs = [(i, i ^ 1) for i in range(self.count)]
        self.mid_pairs = [(i, i ^ 2) for i in range(self.count)]

    def pick(self, array, bit, axis):
        return lax.dynamic_index_in_dim(array, bit, axis, keepdims=False)

    def rows(self, array):
        width, count = array.shape
        blocks = array.reshape(self.outer, 2, 2, width // self.count, count)
        halves = []
        for bit in (1 - self.core, self.core):
            half = self.pick(blocks, bit, 2)
            both = [self.pick(half, self.mid, 1), self.pick(half, 1 - self.mid, 1)]
            halves.append(jnp.concatenate([part.reshape(width // 4, count) for part in both]))
        return halves

    def chain(self, blocks):
        total = self.pick(blocks, self.place, 0).astype(f32)
        for shift in range(1, self.outer):
            pairs = [(i, (i + 4 * shift) % self.count) for i in range(self.count)]
            sent = self.pick(blocks, (self.place + shift) % self.outer, 0)
            total = total + lax.ppermute(sent, "dp", pairs).astype(f32)
        return total

    def scatter(self, make):
        got = lax.ppermute(make(0).astype(bf16), "dp", self.core_pairs)
        both = make(1) + got.astype(f32)
        half = both.shape[0] // 2
        got_mid = lax.ppermute(both[half:].astype(bf16), "dp", self.mid_pairs)
        kept = (both[:half] + got_mid.astype(f32)).astype(bf16)
        return self.chain(kept.reshape((self.outer, -1) + kept.shape[1:]))


def other_tensor(array):
    count = lax.axis_size("tensor")
    return lax.ppermute(array, "tensor", [(i, (i + 1) % count) for i in range(count)])


def tensor_sum(partial):
    low = partial.astype(bf16)
    return low.astype(f32) + other_tensor(low).astype(f32)


def from_behind(shard, by):
    length = lax.axis_size("dp")
    pairs = [(i, i + by) for i in range(length) if 0 <= i + by < length]
    return lax.ppermute(shard, "dp", pairs)


def tn_dot(left, right):
    return lax.dot_general(left, right, (((0,), (0,)), ((), ())), preferred_element_type=f32)


def nt_dot(left, right):
    return lax.dot_general(left, right, (((1,), (1,)), ((), ())), preferred_element_type=f32)


def nn_dot(left, right):
    return jnp.dot(left, right, preferred_element_type=f32)


def attend_kernel(shift, q_ref, k_ref, v_ref, bias_ref, out_ref, inverse_ref):
    rows = q_ref.shape[1]
    for first in range(0, rows, TILE):
        at = slice(first, first + TILE)
        for head in range(GROUP):
            of = slice(head * HD, (head + 1) * HD)
            query = q_ref[of, at]
            total = jnp.zeros((HD + SUM_ROWS, TILE), f32)
            for start in range(first + shift, first + shift + WINDOW + TILE, TILE):
                near = slice(start, start + TILE)
                scores = nn_dot(k_ref[0, near, :], query)
                weight = jnp.exp2(scores * EXP2_SCALE + bias_ref[near, at]).astype(bf16)
                total = total + nn_dot(v_ref[0, :, near], weight)
            inverse = 1.0 / total[HD : HD + 1]
            out_ref[of, at] = (total[:HD] * inverse).astype(bf16)
            inverse_ref[0, head : head + 1, at] = inverse


def attend_back_kernel(shift, q_ref, k_ref, kt_ref, v_ref, d_ref, o_ref, inverse_ref, bias_ref, dq_ref, dk_ref, dv_ref):
    rows = q_ref.shape[1]
    dk_ref[...] = jnp.zeros_like(dk_ref)
    dv_ref[...] = jnp.zeros_like(dv_ref)
    for first in range(0, rows, TILE):
        at = slice(first, first + TILE)
        deltas = []
        for head in range(GROUP):
            of = slice(head * HD, (head + 1) * HD)
            deltas.append(jnp.sum(d_ref[of, at].astype(f32) * o_ref[of, at].astype(f32), axis=0, keepdims=True))
        d_query = [jnp.zeros((HD, TILE), f32) for _ in range(GROUP)]
        for start in range(first + shift, first + shift + WINDOW + TILE, TILE):
            near = slice(start, start + TILE)
            d_key = jnp.zeros((HD, TILE), f32)
            d_value = jnp.zeros((HD, TILE), f32)
            for head in range(GROUP):
                of = slice(head * HD, (head + 1) * HD)
                query = q_ref[of, at]
                d_out = d_ref[of, at]
                scores = nn_dot(k_ref[0, near, :], query)
                prob = jnp.exp2(scores * EXP2_SCALE + bias_ref[near, at]) * inverse_ref[0, head : head + 1, at]
                d_prob = nn_dot(v_ref[0, near, :], d_out)
                d_scores = (prob * (d_prob - deltas[head])).astype(bf16)
                d_query[head] = d_query[head] + nn_dot(kt_ref[:, near], d_scores)
                d_key = d_key + nt_dot(query, d_scores)
                d_value = d_value + nt_dot(d_out, prob.astype(bf16))
            dk_ref[:, near] += d_key
            dv_ref[:, near] += d_value
        for head in range(GROUP):
            dq_ref[head * HD : (head + 1) * HD, at] = d_query[head]


def attend(q_t, k, v_t, bias):
    kv, keys, _ = k.shape
    rows = q_t.shape[1]
    ones = jnp.ones((kv, SUM_ROWS, keys), bf16)
    v_ones = jnp.concatenate([v_t.reshape(kv, HD, keys), ones], axis=1)
    return pl.pallas_call(
        functools.partial(attend_kernel, keys - rows - WINDOW),
        grid=(kv,),
        in_specs=[
            pl.BlockSpec((GROUP * HD, rows), lambda h: (h, 0)),
            pl.BlockSpec((1, keys, HD), lambda h: (h, 0, 0)),
            pl.BlockSpec((1, HD + SUM_ROWS, keys), lambda h: (h, 0, 0)),
            pl.BlockSpec((keys, rows), lambda h: (0, 0)),
        ],
        out_specs=[
            pl.BlockSpec((GROUP * HD, rows), lambda h: (h, 0)),
            pl.BlockSpec((1, 8, rows), lambda h: (h, 0, 0)),
        ],
        out_shape=[jax.ShapeDtypeStruct((kv * GROUP * HD, rows), bf16), jax.ShapeDtypeStruct((kv, 8, rows), f32)],
        compiler_params=pltpu.CompilerParams(vmem_limit_bytes=40 * 2**20),
        cost_estimate=pl.CostEstimate(flops=4 * kv * GROUP * HD * rows * (WINDOW + TILE), bytes_accessed=8 * 2**20, transcendentals=kv * GROUP * rows * (WINDOW + TILE)),
    )(q_t, k, v_ones, bias)


def attend_back(q_t, k, k_t, v, d_t, o_t, inverse, bias):
    kv, keys, _ = k.shape
    rows = q_t.shape[1]
    head_block = pl.BlockSpec((GROUP * HD, rows), lambda h: (h, 0))
    key_block = pl.BlockSpec((1, keys, HD), lambda h: (h, 0, 0))
    key_t_block = pl.BlockSpec((HD, keys), lambda h: (h, 0))
    return pl.pallas_call(
        functools.partial(attend_back_kernel, keys - rows - WINDOW),
        grid=(kv,),
        in_specs=[head_block, key_block, key_t_block, key_block, head_block, head_block,
            pl.BlockSpec((1, 8, rows), lambda h: (h, 0, 0)),
            pl.BlockSpec((keys, rows), lambda h: (0, 0)),
        ],
        out_specs=[head_block, key_t_block, key_t_block],
        out_shape=[jax.ShapeDtypeStruct((kv * GROUP * HD, rows), f32), jax.ShapeDtypeStruct((kv * HD, keys), f32), jax.ShapeDtypeStruct((kv * HD, keys), f32)],
        compiler_params=pltpu.CompilerParams(vmem_limit_bytes=40 * 2**20),
        cost_estimate=pl.CostEstimate(flops=10 * kv * GROUP * HD * rows * (WINDOW + TILE), bytes_accessed=12 * 2**20, transcendentals=kv * GROUP * rows * (WINDOW + TILE)),
    )(q_t, k, k_t, v, d_t, o_t, inverse, bias)


def shards(
    tokens,
    w_query,
    w_keyval,
    w_out,
    w_gateup,
    w_down,
    attn_gain,
    ffn_gain,
    qk_gain,
    segments,
    positions,
    cotangent,
):
    ring = Ring()
    row_count = tokens.shape[0]
    depth = w_query.shape[0]
    model = tokens.shape[1]
    hidden = w_gateup.shape[2]
    tensor = lax.axis_index("tensor")
    query_width = w_query.shape[1]
    local_heads = query_width // HD
    local_kv = local_heads // GROUP
    kv_width = local_kv * HD
    all_kv = w_keyval.shape[1] // 2
    qkv_width = query_width + 2 * kv_width
    gain_count = 2 * qk_gain.shape[1]

    own_keyval = lax.dynamic_index_in_dim(
        w_keyval.reshape(depth, 2, all_kv // kv_width, kv_width), tensor, 2, keepdims=False
    ).reshape(depth, 2 * kv_width)
    head_gain_column = jnp.pad(qk_gain.reshape(gain_count), (0, depth - gain_count))
    gains = jnp.stack([attn_gain, ffn_gain, head_gain_column], axis=1)
    gains = jnp.pad(gains, ((0, 0), (0, LANES - gains.shape[1])))
    first_pack = jnp.concatenate([w_query, own_keyval, w_out.T, gains, w_down.T], axis=1)
    first_full = lax.all_gather(first_pack.astype(bf16), "dp", axis=0, tiled=True)
    gateup_full = lax.all_gather(
        w_gateup.reshape(depth, 2 * hidden).astype(bf16), "dp", axis=0, tiled=True
    )
    qkv_full = first_full[:, :qkv_width]
    gain_start = qkv_width + query_width
    out_full = first_full[:, qkv_width:gain_start]
    down_full = first_full[:, gain_start + LANES :]
    gain_columns = first_full[:, gain_start : gain_start + 3].astype(f32)
    attn_weight = gain_columns[:, 0]
    ffn_weight = gain_columns[:, 1]
    head_gains = gain_columns[:, 2].reshape(ring.count, depth)[:, :gain_count]
    head_gains = head_gains.reshape(ring.count, 2, qk_gain.shape[1]).transpose(1, 0, 2).reshape(2, HD)
    gain_query = head_gains[0][:, None]
    gain_key = head_gains[1][:, None]

    marks = (segments + 1).astype(bf16)
    seq_devices = min(SEQ_LEN // row_count, ring.count)
    own_sequence = ring.index // seq_devices
    reach_count = -(-WINDOW // row_count)
    halo_marks = []
    for step_back in range(reach_count, 0, -1):
        same_sequence = ((ring.index - step_back) // seq_devices == own_sequence).astype(bf16)
        halo_marks.append(from_behind(marks, step_back) * same_sequence)
    key_marks = jnp.concatenate(halo_marks + [marks], axis=0)
    key_count = key_marks.shape[0]
    distance = (jnp.arange(row_count, dtype=jnp.int32) + reach_count * row_count)[
        None, :
    ] - jnp.arange(key_count, dtype=jnp.int32)[:, None]
    allowed = (distance >= 0) & (distance < WINDOW) & (key_marks[:, None] == marks[None, :])
    bias = jnp.where(allowed, 0.0, MASKED).astype(f32)
    cos_table, sin_table = angles_of(positions)

    residual = tokens.astype(f32)
    attn_scale = inverse_rms(residual, 1)

    normed_low = (residual * attn_scale * attn_weight).astype(bf16)
    qkv_raw = lax.dot_general(
        qkv_full, normed_low, (((0,), (1,)), ((), ())), preferred_element_type=f32
    )
    query_raw = qkv_raw[:query_width].reshape(local_heads, HD, row_count)
    key_raw = qkv_raw[query_width : query_width + kv_width].reshape(local_kv, HD, row_count)
    query_scale = inverse_rms(query_raw, 1)
    key_scale = inverse_rms(key_raw, 1)
    query_low = rotate(query_raw * query_scale * gain_query, cos_table, sin_table).astype(bf16)
    key_low = rotate(key_raw * key_scale * gain_key, cos_table, sin_table).astype(bf16)
    query_low = query_low.reshape(query_width, row_count)
    keyval_low = jnp.concatenate(
        [key_low.reshape(kv_width, row_count), qkv_raw[query_width + kv_width :].astype(bf16)], axis=0
    )
    halo = [from_behind(keyval_low, step_back) for step_back in range(reach_count, 0, -1)]
    key_keyval = jnp.concatenate(halo + [keyval_low], axis=1)
    keys_t = key_keyval[:kv_width]
    values_t = key_keyval[kv_width:]
    keys = keys_t.reshape(local_kv, HD, key_count).transpose(0, 2, 1)
    values = values_t.reshape(local_kv, HD, key_count).transpose(0, 2, 1)
    attended, inverse_total = attend(query_low, keys, values_t, bias)
    mid_part = lax.dot_general(
        attended, out_full, (((0,), (1,)), ((), ())), preferred_element_type=f32
    )
    mid = residual + tensor_sum(mid_part)

    d_act = nn_dot(cotangent, down_full)
    ffn_scale = inverse_rms(mid, 1)
    normed2_low = (mid * ffn_scale * ffn_weight).astype(bf16)
    gate = nn_dot(normed2_low, gateup_full[:, :hidden])
    up = nn_dot(normed2_low, gateup_full[:, hidden:])
    gate_sigmoid = jax.nn.sigmoid(gate)
    gate_silu = gate * gate_sigmoid
    act_low = (gate_silu * up).astype(bf16)
    d_gate = (d_act * up * gate_sigmoid * (1.0 + gate * (1.0 - gate_sigmoid))).astype(bf16)
    d_up = (d_act * gate_silu).astype(bf16)
    d_normed2 = tensor_sum(
        nt_dot(d_gate, gateup_full[:, :hidden]) + nt_dot(d_up, gateup_full[:, hidden:])
    )
    grad_down = lax.psum_scatter(
        tn_dot(cotangent, act_low).astype(bf16), "dp", scatter_dimension=0, tiled=True
    )
    grad_down = grad_down.astype(f32).T
    normed2_rows = ring.rows(normed2_low.T)
    pieces = []
    piece_width = hidden // 2
    for source in (d_gate, d_up):
        for start in range(0, hidden, piece_width):
            piece = source[:, start : start + piece_width]
            pieces.append(ring.scatter(lambda part, piece=piece: nn_dot(normed2_rows[part], piece)))
    grad_gateup = jnp.concatenate(pieces, axis=1).reshape(depth, 2, hidden)
    result = mid + tensor_sum(nt_dot(act_low, down_full))
    output = result.astype(bf16)
    d_ffn_weight = jnp.sum(d_normed2 * mid * ffn_scale, axis=0)
    d_mid = cotangent.astype(f32) + rms_back(mid, ffn_scale, ffn_weight, d_normed2, 1)

    d_mid_low = d_mid.astype(bf16)
    d_mid_rows = ring.rows(d_mid_low.T)
    grad_out = ring.scatter(lambda part: nt_dot(d_mid_rows[part], attended)).T
    d_attended = lax.dot_general(
        out_full, d_mid_low, (((0,), (1,)), ((), ())), preferred_element_type=f32
    ).astype(bf16)
    d_query, d_keys, d_values = attend_back(
        query_low, keys, keys_t, values, d_attended, attended, inverse_total, bias
    )
    d_keyval_all = jnp.concatenate([d_keys * SCORE_SCALE, d_values], axis=0)
    own_grad = d_keyval_all[:, reach_count * row_count :]
    for step_back in range(1, reach_count + 1):
        piece_start = (reach_count - step_back) * row_count
        piece = d_keyval_all[:, piece_start : piece_start + row_count].astype(bf16)
        own_grad = own_grad + from_behind(piece, -step_back).astype(f32)

    def head_back(raw, scale, gain, d_rotated):
        d_normed_head = rotate(d_rotated, cos_table, -sin_table)
        d_gain = jnp.sum(d_normed_head * raw * scale, axis=(0, 2))
        return rms_back(raw, scale, gain, d_normed_head, 1), d_gain

    d_query_raw, d_gain_query = head_back(
        query_raw,
        query_scale,
        gain_query,
        d_query.reshape(local_heads, HD, row_count) * SCORE_SCALE,
    )
    d_key_raw, d_gain_key = head_back(
        key_raw, key_scale, gain_key, own_grad[:kv_width].reshape(local_kv, HD, row_count)
    )
    d_qkv_low = jnp.concatenate(
        [
            d_query_raw.reshape(query_width, row_count),
            d_key_raw.reshape(kv_width, row_count),
            own_grad[kv_width:],
        ],
        axis=0,
    ).astype(bf16)
    d_normed_part = lax.dot_general(
        d_qkv_low, qkv_full, (((0,), (1,)), ((), ())), preferred_element_type=f32
    )
    d_normed = tensor_sum(d_normed_part)
    d_attn_part = jnp.sum(d_normed_part * residual * attn_scale, axis=0)

    head_rows = jnp.stack([d_gain_query, d_gain_key], axis=0).reshape(2, ring.count, gain_count // 2)
    head_rows = head_rows.transpose(1, 0, 2).reshape(ring.count, gain_count)
    head_column = jnp.pad(head_rows, ((0, 0), (0, depth - gain_count))).reshape(model)
    gain_grads = jnp.stack([d_attn_part, d_ffn_weight, head_column], axis=1)
    gain_grads = jnp.pad(gain_grads, ((0, 0), (0, LANES - gain_grads.shape[1])))
    grad_qkv = lax.dot_general(
        normed_low, d_qkv_low, (((0,), (1,)), ((), ())), preferred_element_type=f32
    )
    grad_qkv = lax.psum_scatter(
        jnp.concatenate([grad_qkv, gain_grads], axis=1).astype(bf16),
        "dp",
        scatter_dimension=0,
        tiled=True,
    )
    grad_query = grad_qkv[:, :query_width].astype(f32)
    shared = grad_qkv[:, query_width:]
    shared_other = other_tensor(shared).astype(f32)
    shared = shared.astype(f32)
    first = tensor == 0
    keyval_mine = shared[:, : 2 * kv_width].reshape(depth, 2, 1, kv_width)
    keyval_theirs = shared_other[:, : 2 * kv_width].reshape(depth, 2, 1, kv_width)
    grad_keyval = jnp.concatenate(
        [
            jnp.where(first, keyval_mine, keyval_theirs),
            jnp.where(first, keyval_theirs, keyval_mine),
        ],
        axis=2,
    ).reshape(depth, 2 * all_kv)
    gains_mine = shared[:, 2 * kv_width :]
    gains_sum = gains_mine + shared_other[:, 2 * kv_width :]
    grad_attn_gain = gains_sum[:, 0]
    grad_ffn_gain = gains_mine[:, 1]
    grad_heads = gains_sum[:gain_count, 2].reshape(2, gain_count // 2)
    input_grad = (d_mid + rms_back(residual, attn_scale, attn_weight, d_normed, 1)).astype(bf16)
    return (
        output,
        input_grad,
        grad_query,
        grad_keyval,
        grad_out,
        grad_gateup,
        grad_down,
        grad_attn_gain,
        grad_ffn_gain,
        grad_heads,
    )


def solution(mesh):
    in_specs = (
        P("dp", None),
        P("dp", "tensor"),
        P("dp", None),
        P("tensor", "dp"),
        P("dp", None, "tensor"),
        P("tensor", "dp"),
        P("dp"),
        P("dp"),
        P(None, "dp"),
        P("dp"),
        P("dp"),
        P("dp", None),
    )
    out_specs = (
        P("dp", None),
        P("dp", None),
        P("dp", "tensor"),
        P("dp", None),
        P("tensor", "dp"),
        P("dp", None, "tensor"),
        P("tensor", "dp"),
        P("dp"),
        P("dp"),
        P(None, "dp"),
    )
    return jax.shard_map(shards, mesh=mesh, in_specs=in_specs, out_specs=out_specs, check_vma=False)
```

```python
import functools
import math

import jax
import jax.numpy as jnp
from jax import lax
from jax.experimental import pallas as pl
from jax.experimental.pallas import tpu as pltpu
from jax.sharding import PartitionSpec as P

QH = 24
KVH = 6
HD = 64
GROUP = QH // KVH
WINDOW = 1024
SEQ_LEN = 8192
LANES = 128

EPSILON = 1e-06
SCORE_SCALE = 0.125
MASKED = -1e30
ROPE_BASE = 10000.0
EXP2_SCALE = SCORE_SCALE * math.log2(math.e)
TILE = 256
SUM_ROWS = 16

bf16 = jnp.bfloat16
f32 = jnp.float32


def angles_of(positions):
    half_width = HD // 2
    frequency = jnp.exp(
        jnp.arange(half_width, dtype=f32) * (-math.log(ROPE_BASE) / half_width)
    )
    phases = frequency[:, None] * positions.astype(f32)[None, :]
    return jnp.cos(phases)[None], jnp.sin(phases)[None]


def rotate(values, cos_table, sin_table):
    half_width = values.shape[1] // 2
    first_half = values[:, :half_width]
    second_half = values[:, half_width:]
    return jnp.concatenate(
        [
            first_half * cos_table - second_half * sin_table,
            second_half * cos_table + first_half * sin_table,
        ],
        axis=1,
    )


def inverse_rms(values, axis):
    return lax.rsqrt(jnp.mean(values * values, axis=axis, keepdims=True) + EPSILON)


def rms_back(values, scale, weight, d_out, axis):
    weighted = d_out * weight
    pull = jnp.mean(weighted * values, axis=axis, keepdims=True)
    return scale * weighted - values * (scale * scale * scale * pull)


class Ring:
    def __init__(self):
        self.count = lax.axis_size("dp")
        self.outer = self.count // 4
        index = lax.axis_index("dp")
        self.index = index
        self.core = index % 2
        self.mid = (index // 2) % 2
        self.place = index // 4
        self.core_pairs = [(i, i ^ 1) for i in range(self.count)]
        self.mid_pairs = [(i, i ^ 2) for i in range(self.count)]

    def pick(self, array, bit, axis):
        return lax.dynamic_index_in_dim(array, bit, axis, keepdims=False)

    def rows(self, array):
        width, count = array.shape
        blocks = array.reshape(self.outer, 2, 2, width // self.count, count)
        halves = []
        for bit in (1 - self.core, self.core):
            half = self.pick(blocks, bit, 2)
            both = [self.pick(half, self.mid, 1), self.pick(half, 1 - self.mid, 1)]
            halves.append(jnp.concatenate([part.reshape(width // 4, count) for part in both]))
        return halves

    def chosen(self, array):
        depth = array.shape[1] // self.count
        if depth % LANES:
            return self.rows(array.T)
        order = []
        for core in (1 - self.core, self.core):
            for mid in (self.mid, 1 - self.mid):
                order += [4 * place + 2 * mid + core for place in range(self.outer)]
        return transposed_blocks(jnp.stack(order).astype(jnp.int32), array, depth)

    def to_core(self, lefts, right):
        got = lax.ppermute(nn_dot(lefts[0], right).astype(bf16), "dp", self.core_pairs)
        return got

    def to_mid(self, lefts, right, got):
        both = nn_dot(lefts[1], right) + got.astype(f32)
        half = both.shape[0] // 2
        kept = both[:half]
        return kept, lax.ppermute(both[half:].astype(bf16), "dp", self.mid_pairs)

    def to_outer(self, kept, got):
        blocks = (kept + got.astype(f32)).astype(bf16)
        blocks = blocks.reshape((self.outer, -1) + blocks.shape[1:])
        own = self.pick(blocks, self.place, 0)
        others = []
        for shift in range(1, self.outer):
            pairs = [(i, (i + 4 * shift) % self.count) for i in range(self.count)]
            sent = self.pick(blocks, (self.place + shift) % self.outer, 0)
            others.append(lax.ppermute(sent, "dp", pairs))
        return own, others

    def total(self, own, others):
        total = own.astype(f32)
        for other in others:
            total = total + other.astype(f32)
        return total


def other_tensor(array):
    count = lax.axis_size("tensor")
    return lax.ppermute(array, "tensor", [(i, (i + 1) % count) for i in range(count)])


def tensor_sum(partial, *before):
    low = partial.astype(bf16)
    other = other_tensor(low)
    if before:
        other = tie(other, *before)
    return low.astype(f32) + other.astype(f32)


def from_behind(shard, by):
    length = lax.axis_size("dp")
    pairs = [(i, i + by) for i in range(length) if 0 <= i + by < length]
    return lax.ppermute(shard, "dp", pairs)


def tn_dot(left, right):
    return lax.dot_general(left, right, (((0,), (0,)), ((), ())), preferred_element_type=f32)


def nt_dot(left, right):
    return lax.dot_general(left, right, (((1,), (1,)), ((), ())), preferred_element_type=f32)


def nn_dot(left, right):
    return jnp.dot(left, right, preferred_element_type=f32)


def tie(array, *others):
    def kernel(*refs):
        del refs

    return pl.pallas_call(
        kernel,
        in_specs=[pl.BlockSpec(memory_space=pl.ANY)] * (1 + len(others)),
        out_specs=pl.BlockSpec(memory_space=pl.ANY),
        out_shape=jax.ShapeDtypeStruct(array.shape, array.dtype),
        input_output_aliases={0: 0},
    )(array, *others)


def transposed_blocks(order, array, depth):
    tokens, width = array.shape
    half = width // depth // 2

    def kernel(order_ref, in_ref, first_ref, second_ref):
        del order_ref
        block = in_ref[...].astype(f32).T.astype(in_ref.dtype)

        @pl.when(pl.program_id(0) < half)
        def _():
            first_ref[...] = block

        @pl.when(pl.program_id(0) >= half)
        def _():
            second_ref[...] = block

    out = jax.ShapeDtypeStruct((width // 2, tokens), array.dtype)
    return pl.pallas_call(
        kernel,
        grid_spec=pltpu.PrefetchScalarGridSpec(
            num_scalar_prefetch=1,
            grid=(2 * half,),
            in_specs=[pl.BlockSpec((tokens, depth), lambda i, order: (0, order[i]))],
            out_specs=[
                pl.BlockSpec((depth, tokens), lambda i, order: (jnp.minimum(i, half - 1), 0)),
                pl.BlockSpec((depth, tokens), lambda i, order: (jnp.maximum(i - half, 0), 0)),
            ],
        ),
        out_shape=[out, out],
        cost_estimate=pl.CostEstimate(flops=0, bytes_accessed=4 * tokens * width, transcendentals=0),
    )(order, array)


def attend_kernel(shift, q_ref, k_ref, v_ref, bias_ref, out_ref, inverse_ref):
    rows = q_ref.shape[1]
    for first in range(0, rows, TILE):
        at = slice(first, first + TILE)
        for head in range(GROUP):
            of = slice(head * HD, (head + 1) * HD)
            query = q_ref[of, at]
            total = jnp.zeros((HD + SUM_ROWS, TILE), f32)
            for start in range(first + shift, first + shift + WINDOW + TILE, TILE):
                near = slice(start, start + TILE)
                scores = nn_dot(k_ref[0, near, :], query)
                weight = jnp.exp2(scores * EXP2_SCALE + bias_ref[near, at]).astype(bf16)
                total = total + nn_dot(v_ref[0, :, near], weight)
            inverse = 1.0 / total[HD : HD + 1]
            out_ref[of, at] = (total[:HD] * inverse).astype(bf16)
            inverse_ref[0, head : head + 1, at] = inverse


def attend_back_kernel(shift, q_ref, k_ref, kt_ref, v_ref, d_ref, o_ref, inverse_ref, bias_ref, dq_ref, dk_ref, dv_ref):
    rows = q_ref.shape[1]
    dk_ref[...] = jnp.zeros_like(dk_ref)
    dv_ref[...] = jnp.zeros_like(dv_ref)
    for first in range(0, rows, TILE):
        at = slice(first, first + TILE)
        deltas = []
        for head in range(GROUP):
            of = slice(head * HD, (head + 1) * HD)
            deltas.append(jnp.sum(d_ref[of, at].astype(f32) * o_ref[of, at].astype(f32), axis=0, keepdims=True))
        d_query = [jnp.zeros((HD, TILE), f32) for _ in range(GROUP)]
        for start in range(first + shift, first + shift + WINDOW + TILE, TILE):
            near = slice(start, start + TILE)
            d_key = jnp.zeros((HD, TILE), f32)
            d_value = jnp.zeros((HD, TILE), f32)
            for head in range(GROUP):
                of = slice(head * HD, (head + 1) * HD)
                query = q_ref[of, at]
                d_out = d_ref[of, at]
                scores = nn_dot(k_ref[0, near, :], query)
                prob = jnp.exp2(scores * EXP2_SCALE + bias_ref[near, at]) * inverse_ref[0, head : head + 1, at]
                d_prob = nn_dot(v_ref[0, near, :], d_out)
                d_scores = (prob * (d_prob - deltas[head])).astype(bf16)
                d_query[head] = d_query[head] + nn_dot(kt_ref[:, near], d_scores)
                d_key = d_key + nt_dot(query, d_scores)
                d_value = d_value + nt_dot(d_out, prob.astype(bf16))
            dk_ref[:, near] += d_key
            dv_ref[:, near] += d_value
        for head in range(GROUP):
            dq_ref[head * HD : (head + 1) * HD, at] = d_query[head]


def attend(q_t, k, v_t, bias):
    kv, keys, _ = k.shape
    rows = q_t.shape[1]
    ones = jnp.ones((kv, SUM_ROWS, keys), bf16)
    v_ones = jnp.concatenate([v_t.reshape(kv, HD, keys), ones], axis=1)
    return pl.pallas_call(
        functools.partial(attend_kernel, keys - rows - WINDOW),
        grid=(kv,),
        in_specs=[
            pl.BlockSpec((GROUP * HD, rows), lambda h: (h, 0)),
            pl.BlockSpec((1, keys, HD), lambda h: (h, 0, 0)),
            pl.BlockSpec((1, HD + SUM_ROWS, keys), lambda h: (h, 0, 0)),
            pl.BlockSpec((keys, rows), lambda h: (0, 0)),
        ],
        out_specs=[
            pl.BlockSpec((GROUP * HD, rows), lambda h: (h, 0)),
            pl.BlockSpec((1, 8, rows), lambda h: (h, 0, 0)),
        ],
        out_shape=[jax.ShapeDtypeStruct((kv * GROUP * HD, rows), bf16), jax.ShapeDtypeStruct((kv, 8, rows), f32)],
        compiler_params=pltpu.CompilerParams(vmem_limit_bytes=40 * 2**20),
        cost_estimate=pl.CostEstimate(flops=4 * kv * GROUP * HD * rows * (WINDOW + TILE), bytes_accessed=8 * 2**20, transcendentals=kv * GROUP * rows * (WINDOW + TILE)),
    )(q_t, k, v_ones, bias)


def attend_back(q_t, k, k_t, v, d_t, o_t, inverse, bias):
    kv, keys, _ = k.shape
    rows = q_t.shape[1]
    head_block = pl.BlockSpec((GROUP * HD, rows), lambda h: (h, 0))
    key_block = pl.BlockSpec((1, keys, HD), lambda h: (h, 0, 0))
    key_t_block = pl.BlockSpec((HD, keys), lambda h: (h, 0))
    return pl.pallas_call(
        functools.partial(attend_back_kernel, keys - rows - WINDOW),
        grid=(kv,),
        in_specs=[head_block, key_block, key_t_block, key_block, head_block, head_block,
            pl.BlockSpec((1, 8, rows), lambda h: (h, 0, 0)),
            pl.BlockSpec((keys, rows), lambda h: (0, 0)),
        ],
        out_specs=[head_block, key_t_block, key_t_block],
        out_shape=[jax.ShapeDtypeStruct((kv * GROUP * HD, rows), f32), jax.ShapeDtypeStruct((kv * HD, keys), f32), jax.ShapeDtypeStruct((kv * HD, keys), f32)],
        compiler_params=pltpu.CompilerParams(vmem_limit_bytes=40 * 2**20),
        cost_estimate=pl.CostEstimate(flops=10 * kv * GROUP * HD * rows * (WINDOW + TILE), bytes_accessed=12 * 2**20, transcendentals=kv * GROUP * rows * (WINDOW + TILE)),
    )(q_t, k, k_t, v, d_t, o_t, inverse, bias)


def shards(
    tokens,
    w_query,
    w_keyval,
    w_out,
    w_gateup,
    w_down,
    attn_gain,
    ffn_gain,
    qk_gain,
    segments,
    positions,
    cotangent,
):
    ring = Ring()
    row_count = tokens.shape[0]
    depth = w_query.shape[0]
    model = tokens.shape[1]
    hidden = w_gateup.shape[2]
    tensor = lax.axis_index("tensor")
    query_width = w_query.shape[1]
    local_heads = query_width // HD
    local_kv = local_heads // GROUP
    kv_width = local_kv * HD
    all_kv = w_keyval.shape[1] // 2
    qkv_width = query_width + 2 * kv_width
    gain_count = 2 * qk_gain.shape[1]

    own_keyval = lax.dynamic_index_in_dim(
        w_keyval.reshape(depth, 2, all_kv // kv_width, kv_width), tensor, 2, keepdims=False
    ).reshape(depth, 2 * kv_width)
    head_gain_column = jnp.pad(qk_gain.reshape(gain_count), (0, depth - gain_count))
    gains = jnp.stack([attn_gain, ffn_gain, head_gain_column], axis=1)
    gains = jnp.pad(gains, ((0, 0), (0, LANES - gains.shape[1])))
    first_pack = jnp.concatenate([w_query, own_keyval, w_out.T, gains, w_down.T], axis=1)
    first_full = lax.all_gather(first_pack.astype(bf16), "dp", axis=0, tiled=True)
    gateup_full = lax.all_gather(
        w_gateup.reshape(depth, 2 * hidden).astype(bf16), "dp", axis=0, tiled=True
    )
    qkv_full = first_full[:, :qkv_width]
    gain_start = qkv_width + query_width
    out_full = first_full[:, qkv_width:gain_start]
    down_full = first_full[:, gain_start + LANES :]
    gain_columns = first_full[:, gain_start : gain_start + 3].astype(f32)
    attn_weight = gain_columns[:, 0]
    ffn_weight = gain_columns[:, 1]
    head_gains = gain_columns[:, 2].reshape(ring.count, depth)[:, :gain_count]
    head_gains = head_gains.reshape(ring.count, 2, qk_gain.shape[1]).transpose(1, 0, 2).reshape(2, HD)
    gain_query = head_gains[0][:, None]
    gain_key = head_gains[1][:, None]

    marks = (segments + 1).astype(bf16)
    seq_devices = min(SEQ_LEN // row_count, ring.count)
    own_sequence = ring.index // seq_devices
    reach_count = -(-WINDOW // row_count)
    halo_marks = []
    for step_back in range(reach_count, 0, -1):
        same_sequence = ((ring.index - step_back) // seq_devices == own_sequence).astype(bf16)
        halo_marks.append(from_behind(marks, step_back) * same_sequence)
    key_marks = jnp.concatenate(halo_marks + [marks], axis=0)
    key_count = key_marks.shape[0]
    distance = (jnp.arange(row_count, dtype=jnp.int32) + reach_count * row_count)[
        None, :
    ] - jnp.arange(key_count, dtype=jnp.int32)[:, None]
    allowed = (distance >= 0) & (distance < WINDOW) & (key_marks[:, None] == marks[None, :])
    bias = jnp.where(allowed, 0.0, MASKED).astype(f32)
    cos_table, sin_table = angles_of(positions)

    residual = tokens.astype(f32)
    attn_scale = inverse_rms(residual, 1)

    normed_low = (residual * attn_scale * attn_weight).astype(bf16)
    qkv_raw = lax.dot_general(
        qkv_full, normed_low, (((0,), (1,)), ((), ())), preferred_element_type=f32
    )
    query_raw = qkv_raw[:query_width].reshape(local_heads, HD, row_count)
    key_raw = qkv_raw[query_width : query_width + kv_width].reshape(local_kv, HD, row_count)
    query_scale = inverse_rms(query_raw, 1)
    key_scale = inverse_rms(key_raw, 1)
    query_low = rotate(query_raw * query_scale * gain_query, cos_table, sin_table).astype(bf16)
    key_low = rotate(key_raw * key_scale * gain_key, cos_table, sin_table).astype(bf16)
    query_low = query_low.reshape(query_width, row_count)
    keyval_low = jnp.concatenate(
        [key_low.reshape(kv_width, row_count), qkv_raw[query_width + kv_width :].astype(bf16)], axis=0
    )
    halo = [from_behind(keyval_low, step_back) for step_back in range(reach_count, 0, -1)]
    key_keyval = jnp.concatenate(halo + [keyval_low], axis=1)
    keys_t = key_keyval[:kv_width]
    values_t = key_keyval[kv_width:]
    keys = keys_t.reshape(local_kv, HD, key_count).transpose(0, 2, 1)
    values = values_t.reshape(local_kv, HD, key_count).transpose(0, 2, 1)
    attended, inverse_total = attend(query_low, keys, values_t, bias)
    mid_part = lax.dot_general(
        attended, out_full, (((0,), (1,)), ((), ())), preferred_element_type=f32
    )
    mid = residual + tensor_sum(mid_part)

    d_act = nn_dot(cotangent, down_full)
    ffn_scale = inverse_rms(mid, 1)
    normed2_low = (mid * ffn_scale * ffn_weight).astype(bf16)
    gate = nn_dot(normed2_low, gateup_full[:, :hidden])
    up = nn_dot(normed2_low, gateup_full[:, hidden:])
    gate_sigmoid = jax.nn.sigmoid(gate)
    gate_silu = gate * gate_sigmoid
    act_low = (gate_silu * up).astype(bf16)
    d_gate = (d_act * up * gate_sigmoid * (1.0 + gate * (1.0 - gate_sigmoid))).astype(bf16)
    d_up = (d_act * gate_silu).astype(bf16)
    d_normed2_part = nt_dot(d_gate, gateup_full[:, :hidden]) + nt_dot(
        d_up, gateup_full[:, hidden:]
    )
    down_part = tn_dot(cotangent, act_low).astype(bf16)
    grad_down = lax.psum_scatter(down_part, "dp", scatter_dimension=0, tiled=True)
    normed2_rows = ring.chosen(normed2_low)
    piece_width = hidden // 2
    rights = [
        source[:, start : start + piece_width]
        for source in (d_gate, d_up)
        for start in range(0, hidden, piece_width)
    ]
    core_got = [ring.to_core(normed2_rows, right) for right in rights]
    d_normed2 = tensor_sum(d_normed2_part, *[got[: 2 * 8, :LANES] for got in core_got])
    mid_got = [
        ring.to_mid(normed2_rows, right, got) for right, got in zip(rights, core_got, strict=True)
    ]
    outer_got = [ring.to_outer(kept, got) for kept, got in mid_got]
    result = mid + tensor_sum(nt_dot(act_low, down_full))
    output = result.astype(bf16)
    d_ffn_weight = jnp.sum(d_normed2 * mid * ffn_scale, axis=0)
    d_mid = cotangent.astype(f32) + rms_back(mid, ffn_scale, ffn_weight, d_normed2, 1)

    d_mid_low = d_mid.astype(bf16)
    d_mid_rows = ring.chosen(d_mid_low)
    attended_back = attended.T
    out_core = ring.to_core(d_mid_rows, attended_back)
    out_kept, out_mid = ring.to_mid(d_mid_rows, attended_back, out_core)
    out_own, out_others = ring.to_outer(out_kept, out_mid)
    grad_out = ring.total(out_own, out_others).T
    d_attended = lax.dot_general(
        out_full, d_mid_low, (((0,), (1,)), ((), ())), preferred_element_type=f32
    ).astype(bf16)
    d_attended = tie(d_attended, mid_got[0][1])
    d_query, d_keys, d_values = attend_back(
        query_low, keys, keys_t, values, d_attended, attended, inverse_total, bias
    )
    d_keys = tie(d_keys, mid_got[1][1], *outer_got[0][1])
    d_keyval_all = jnp.concatenate([d_keys * SCORE_SCALE, d_values], axis=0)
    own_grad = d_keyval_all[:, reach_count * row_count :]
    for step_back in range(1, reach_count + 1):
        piece_start = (reach_count - step_back) * row_count
        piece = d_keyval_all[:, piece_start : piece_start + row_count].astype(bf16)
        own_grad = own_grad + from_behind(piece, -step_back).astype(f32)

    def head_back(raw, scale, gain, d_rotated):
        d_normed_head = rotate(d_rotated, cos_table, -sin_table)
        d_gain = jnp.sum(d_normed_head * raw * scale, axis=(0, 2))
        return rms_back(raw, scale, gain, d_normed_head, 1), d_gain

    d_query_raw, d_gain_query = head_back(
        query_raw,
        query_scale,
        gain_query,
        d_query.reshape(local_heads, HD, row_count) * SCORE_SCALE,
    )
    d_key_raw, d_gain_key = head_back(
        key_raw, key_scale, gain_key, own_grad[:kv_width].reshape(local_kv, HD, row_count)
    )
    d_qkv_low = jnp.concatenate(
        [
            d_query_raw.reshape(query_width, row_count),
            d_key_raw.reshape(kv_width, row_count),
            own_grad[kv_width:],
        ],
        axis=0,
    ).astype(bf16)
    d_qkv_low = tie(d_qkv_low, mid_got[2][1], *outer_got[1][1])
    d_normed_part = lax.dot_general(
        d_qkv_low, qkv_full, (((0,), (1,)), ((), ())), preferred_element_type=f32
    )
    d_normed = tensor_sum(d_normed_part)
    d_attn_part = jnp.sum(d_normed_part * residual * attn_scale, axis=0)

    head_rows = jnp.stack([d_gain_query, d_gain_key], axis=0).reshape(2, ring.count, gain_count // 2)
    head_rows = head_rows.transpose(1, 0, 2).reshape(ring.count, gain_count)
    head_column = jnp.pad(head_rows, ((0, 0), (0, depth - gain_count))).reshape(model)
    gain_grads = jnp.stack([d_attn_part, d_ffn_weight, head_column], axis=1)
    gain_grads = jnp.pad(gain_grads, ((0, 0), (0, LANES - gain_grads.shape[1])))
    grad_qkv = lax.dot_general(
        normed_low, d_qkv_low, (((0,), (1,)), ((), ())), preferred_element_type=f32
    )
    grad_qkv = lax.psum_scatter(
        jnp.concatenate([grad_qkv, gain_grads], axis=1).astype(bf16),
        "dp",
        scatter_dimension=0,
        tiled=True,
    )
    grad_query = grad_qkv[:, :query_width].astype(f32)
    shared = grad_qkv[:, query_width:]
    shared_other = other_tensor(shared).astype(f32)
    shared = shared.astype(f32)
    first = tensor == 0
    keyval_mine = shared[:, : 2 * kv_width].reshape(depth, 2, 1, kv_width)
    keyval_theirs = shared_other[:, : 2 * kv_width].reshape(depth, 2, 1, kv_width)
    grad_keyval = jnp.concatenate(
        [
            jnp.where(first, keyval_mine, keyval_theirs),
            jnp.where(first, keyval_theirs, keyval_mine),
        ],
        axis=2,
    ).reshape(depth, 2 * all_kv)
    gains_mine = shared[:, 2 * kv_width :]
    gains_sum = gains_mine + shared_other[:, 2 * kv_width :]
    grad_attn_gain = gains_sum[:, 0]
    grad_ffn_gain = gains_mine[:, 1]
    grad_heads = gains_sum[:gain_count, 2].reshape(2, gain_count // 2)
    pieces = [ring.total(own, others) for own, others in outer_got]
    grad_gateup = jnp.concatenate(pieces, axis=1).reshape(depth, 2, hidden)
    grad_down = grad_down.astype(f32).T
    input_grad = (d_mid + rms_back(residual, attn_scale, attn_weight, d_normed, 1)).astype(bf16)
    return (
        output,
        input_grad,
        grad_query,
        grad_keyval,
        grad_out,
        grad_gateup,
        grad_down,
        grad_attn_gain,
        grad_ffn_gain,
        grad_heads,
    )


def solution(mesh):
    in_specs = (
        P("dp", None),
        P("dp", "tensor"),
        P("dp", None),
        P("tensor", "dp"),
        P("dp", None, "tensor"),
        P("tensor", "dp"),
        P("dp"),
        P("dp"),
        P(None, "dp"),
        P("dp"),
        P("dp"),
        P("dp", None),
    )
    out_specs = (
        P("dp", None),
        P("dp", None),
        P("dp", "tensor"),
        P("dp", None),
        P("tensor", "dp"),
        P("dp", None, "tensor"),
        P("tensor", "dp"),
        P("dp"),
        P("dp"),
        P(None, "dp"),
    )
    return jax.shard_map(shards, mesh=mesh, in_specs=in_specs, out_specs=out_specs, check_vma=False)
```

```python
import functools
import math

import jax
import jax.numpy as jnp
from jax import lax
from jax.experimental import pallas as pl
from jax.experimental.pallas import tpu as pltpu
from jax.sharding import PartitionSpec as P

QH = 24
KVH = 6
HD = 64
GROUP = QH // KVH
WINDOW = 1024
SEQ_LEN = 8192
LANES = 128

EPSILON = 1e-06
SCORE_SCALE = 0.125
MASKED = -1e30
ROPE_BASE = 10000.0
EXP2_SCALE = SCORE_SCALE * math.log2(math.e)
TILE = 256
SUM_ROWS = 16
LINK_SHARE = 0.5

bf16 = jnp.bfloat16
f32 = jnp.float32
ANYWHERE = pl.BlockSpec(memory_space=pl.ANY)


def cost(microseconds):
    return pl.CostEstimate(
        flops=int(microseconds * LINK_SHARE * 1.15e9), bytes_accessed=0, transcendentals=0
    )


def angles_of(positions):
    half_width = HD // 2
    frequency = jnp.exp(
        jnp.arange(half_width, dtype=f32) * (-math.log(ROPE_BASE) / half_width)
    )
    phases = frequency[:, None] * positions.astype(f32)[None, :]
    return jnp.cos(phases)[None], jnp.sin(phases)[None]


def rotate(values, cos_table, sin_table):
    half_width = values.shape[1] // 2
    first_half = values[:, :half_width]
    second_half = values[:, half_width:]
    return jnp.concatenate(
        [
            first_half * cos_table - second_half * sin_table,
            second_half * cos_table + first_half * sin_table,
        ],
        axis=1,
    )


def inverse_rms(values, axis):
    return lax.rsqrt(jnp.mean(values * values, axis=axis, keepdims=True) + EPSILON)


def rms_back(values, scale, weight, d_out, axis):
    weighted = d_out * weight
    pull = jnp.mean(weighted * values, axis=axis, keepdims=True)
    return scale * weighted - values * (scale * scale * scale * pull)


class Ring:
    def __init__(self):
        self.count = lax.axis_size("dp")
        self.index = lax.axis_index("dp")
        self.bits = [1 << at for at in range(self.count.bit_length() - 1)]

    def order(self, bits):
        order = []
        for at in range(self.count - 1, -1, -1):
            flips = sum(bit for place, bit in enumerate(reversed(bits)) if at >> place & 1)
            order.append(self.index ^ flips)
        return jnp.stack(order).astype(jnp.int32)

    def chosen(self, array, bits):
        depth = array.shape[1] // self.count
        if depth % LANES:
            blocks = array.T.reshape(self.count, depth, array.shape[0])
            return jnp.take(blocks, self.order(bits), axis=0).reshape(array.shape[1], array.shape[0])
        return transposed_blocks(self.order(bits), array, depth)


class Scatter:
    def __init__(self, ring, left, right, bits, tail=None):
        self.ring, self.left, self.right, self.bits, self.tail = ring, left, right, bits, tail
        self.got = []

    def rows(self):
        step = len(self.got)
        last = step == len(self.bits)
        size = self.left.shape[0] >> (step if last else step + 1)
        start = self.left.shape[0] - (self.left.shape[0] >> step)
        starts = [self.left.shape[0] - (self.left.shape[0] >> at + 1) for at in range(step)]
        return size, start // size, [(start - first) // size for first in starts]

    def send(self, *after):
        size, block, blocks = self.rows()
        sent = product(
            self.left, self.right, size, block, list(zip(self.got, blocks)), after, self.tail
        )
        bit = self.bits[len(self.got)]
        pairs = [(i, i ^ bit) for i in range(self.ring.count)]
        self.got.append(lax.ppermute(sent, "dp", pairs))
        return sent

    def total(self, *after, transposed=False):
        size, block, blocks = self.rows()
        got = list(zip(self.got, blocks))
        return product(self.left, self.right, size, block, got, after, self.tail, f32, transposed)


def other_tensor(array):
    count = lax.axis_size("tensor")
    return lax.ppermute(array, "tensor", [(i, (i + 1) % count) for i in range(count)])


def tensor_sum(partial, *before):
    low = partial.astype(bf16)
    other = other_tensor(low)
    if before:
        other = tie(other, *before)
    return low.astype(f32) + other.astype(f32)


def from_behind(shard, by):
    length = lax.axis_size("dp")
    pairs = [(i, i + by) for i in range(length) if 0 <= i + by < length]
    return lax.ppermute(shard, "dp", pairs)


def tn_dot(left, right):
    return lax.dot_general(left, right, (((0,), (0,)), ((), ())), preferred_element_type=f32)


def nt_dot(left, right):
    return lax.dot_general(left, right, (((1,), (1,)), ((), ())), preferred_element_type=f32)


def nn_dot(left, right):
    return jnp.dot(left, right, preferred_element_type=f32)


def tie(array, *others):
    def kernel(*refs):
        del refs

    return pl.pallas_call(
        kernel,
        in_specs=[pl.BlockSpec(memory_space=pl.ANY)] * (1 + len(others)),
        out_specs=pl.BlockSpec(memory_space=pl.ANY),
        out_shape=jax.ShapeDtypeStruct(array.shape, array.dtype),
        input_output_aliases={0: 0},
        cost_estimate=cost(0),
    )(array, *others)


def corner(array):
    return array[: 2 * 8, :LANES]


def transposed_blocks(order, array, depth):
    tokens, width = array.shape
    step = math.gcd(tokens, LANES)

    def kernel(order_ref, in_ref, out_ref):
        for at in range(width // depth):
            column = pl.multiple_of(order_ref[at] * depth, depth)
            out_ref[at * depth : (at + 1) * depth, :] = in_ref[:, pl.ds(column, depth)].T

    return pl.pallas_call(
        kernel,
        grid_spec=pltpu.PrefetchScalarGridSpec(
            num_scalar_prefetch=1,
            grid=(tokens // step,),
            in_specs=[pl.BlockSpec((step, width), lambda i, order: (i, 0))],
            out_specs=pl.BlockSpec((width, step), lambda i, order: (0, i)),
        ),
        out_shape=jax.ShapeDtypeStruct((width, tokens), array.dtype),
        cost_estimate=cost(4.8),
    )(order, array)


def product(left, right, size, block, adds, after=(), tail=None, out_type=bf16, transposed=False):
    depth, columns = right.shape
    most = max(LANES, min(columns, 512 * 1024 // size))
    tile = max(t for t in range(LANES, most + 1, LANES) if columns % t == 0)
    if tail is not None:
        tile = LANES
    steps = columns // tile

    def kernel(left_ref, right_ref, *refs):
        def put(total):
            for ref in refs[: len(adds)]:
                total = total + ref[...].astype(f32)
            refs[-1][...] = (total.T if transposed else total).astype(out_type)

        if tail is None:
            put(nn_dot(left_ref[...], right_ref[...]))
            return

        @pl.when(pl.program_id(0) < steps)
        def _():
            put(nn_dot(left_ref[...], right_ref[...]))

        @pl.when(pl.program_id(0) == steps)
        def _():
            put(refs[len(adds)][...].astype(f32))

    all_columns = columns
    in_specs = [
        pl.BlockSpec((size, depth), lambda i: (block, 0)),
        pl.BlockSpec((depth, tile), lambda i: (0, jnp.minimum(i, steps - 1))),
    ] + [
        pl.BlockSpec((size, tile), functools.partial(lambda i, row: (row, i), row=row))
        for _, row in adds
    ]
    operands = [left, right, *[array for array, _ in adds]]
    if tail is not None:
        all_columns += LANES
        in_specs.append(pl.BlockSpec((size, LANES), lambda i: (block, 0)))
        operands.append(tail)
    out_shape, out_block, out_map = (size, all_columns), (size, tile), lambda i: (0, i)
    if transposed:
        out_shape, out_block, out_map = (all_columns, size), (tile, size), lambda i: (i, 0)
    return pl.pallas_call(
        kernel,
        grid=(all_columns // tile,),
        in_specs=in_specs + [ANYWHERE] * len(after),
        out_specs=pl.BlockSpec(out_block, out_map),
        out_shape=jax.ShapeDtypeStruct(out_shape, out_type),
        compiler_params=pltpu.CompilerParams(vmem_limit_bytes=40 * 2**20),
        cost_estimate=cost(2 + 2 * size * depth * columns / 0.9e9),
    )(*operands, *after)


def product_tt(left, first, columns, right):
    depth = left.shape[0]
    rows = right.shape[0]
    tile = max(t for t in range(LANES, 384 + 1, LANES) if columns % t == 0 and first % t == 0)

    def kernel(left_ref, right_ref, out_ref):
        out_ref[...] = nt_dot(left_ref[...].T, right_ref[...]).astype(bf16)

    return pl.pallas_call(
        kernel,
        grid=(columns // tile,),
        in_specs=[
            pl.BlockSpec((depth, tile), lambda i: (0, i + first // tile)),
            pl.BlockSpec((rows, depth), lambda i: (0, 0)),
        ],
        out_specs=pl.BlockSpec((tile, rows), lambda i: (i, 0)),
        out_shape=jax.ShapeDtypeStruct((columns, rows), bf16),
        compiler_params=pltpu.CompilerParams(vmem_limit_bytes=40 * 2**20),
        cost_estimate=cost(4.3),
    )(left, right)


def norm_back(values, direct, part, other, gain, *after):
    rows, width = values.shape
    step = math.gcd(rows, 128)

    def kernel(values_ref, direct_ref, part_ref, other_ref, gain_ref, *refs):
        out_ref, low_ref, gain_out_ref = refs[len(after) :]
        value = values_ref[...].astype(f32)
        scale = inverse_rms(value, 1)
        d_out = part_ref[...].astype(f32) + other_ref[...].astype(f32)
        result = direct_ref[...].astype(f32) + rms_back(value, scale, gain_ref[...], d_out, 1)
        out_ref[...] = result
        low_ref[...] = result.astype(bf16)

        @pl.when(pl.program_id(0) == 0)
        def _():
            gain_out_ref[...] = jnp.zeros_like(gain_out_ref)

        gain_out_ref[...] += jnp.sum(d_out * value * scale, axis=0, keepdims=True)

    block = pl.BlockSpec((step, width), lambda i: (i, 0))
    row = pl.BlockSpec((1, width), lambda i: (0, 0))
    return pl.pallas_call(
        kernel,
        grid=(rows // step,),
        in_specs=[block] * 4 + [row] + [ANYWHERE] * len(after),
        out_specs=[block, block, row],
        out_shape=[
            jax.ShapeDtypeStruct((rows, width), f32),
            jax.ShapeDtypeStruct((rows, width), bf16),
            jax.ShapeDtypeStruct((1, width), f32),
        ],
        compiler_params=pltpu.CompilerParams(vmem_limit_bytes=40 * 2**20),
        cost_estimate=cost(7),
    )(values, direct, part, other, gain[None, :], *after)


def add_up(values, part, other, *after):
    rows, width = values.shape
    step = math.gcd(rows, 128)

    def kernel(values_ref, part_ref, other_ref, *refs):
        added = part_ref[...].astype(f32) + other_ref[...].astype(f32)
        refs[-1][...] = (values_ref[...] + added).astype(bf16)

    block = pl.BlockSpec((step, width), lambda i: (i, 0))
    return pl.pallas_call(
        kernel,
        grid=(rows // step,),
        in_specs=[block] * 3 + [ANYWHERE] * len(after),
        out_specs=block,
        out_shape=jax.ShapeDtypeStruct((rows, width), bf16),
        cost_estimate=cost(3),
    )(values, part, other, *after)


def turn_back(d_rotated, raw, cos_table, sin_table, gain):
    half_width = HD // 2
    first, second = d_rotated[:half_width], d_rotated[half_width:]
    d_normed = jnp.concatenate(
        [first * cos_table + second * sin_table, second * cos_table - first * sin_table], axis=0
    )
    scale = inverse_rms(raw, 0)
    return rms_back(raw, scale, gain, d_normed, 0), d_normed * raw * scale


def query_back(d_query, raw, cos_table, sin_table, gain, *after):
    width, rows = d_query.shape
    step = GROUP * HD

    def kernel(d_ref, raw_ref, cos_ref, sin_ref, gain_ref, *refs):
        out_ref, gain_out_ref = refs[len(after) :]
        results = []
        d_gain = jnp.zeros((HD, rows), f32)
        for head in range(GROUP):
            of = slice(head * HD, (head + 1) * HD)
            result, by_token = turn_back(
                d_ref[of, :] * SCORE_SCALE, raw_ref[of, :], cos_ref[...], sin_ref[...], gain_ref[...]
            )
            results.append(result)
            d_gain = d_gain + by_token
        out_ref[...] = jnp.concatenate(results, axis=0).astype(bf16).T

        @pl.when(pl.program_id(0) == 0)
        def _():
            gain_out_ref[...] = jnp.zeros_like(gain_out_ref)

        gain_out_ref[...] += jnp.sum(d_gain, axis=1, keepdims=True)

    block = pl.BlockSpec((step, rows), lambda i: (i, 0))
    table = pl.BlockSpec((HD // 2, rows), lambda i: (0, 0))
    column = pl.BlockSpec((HD, 1), lambda i: (0, 0))
    return pl.pallas_call(
        kernel,
        grid=(width // step,),
        in_specs=[block, block, table, table, column] + [ANYWHERE] * len(after),
        out_specs=[pl.BlockSpec((rows, step), lambda i: (0, i)), column],
        out_shape=[
            jax.ShapeDtypeStruct((rows, width), bf16),
            jax.ShapeDtypeStruct((HD, 1), f32),
        ],
        compiler_params=pltpu.CompilerParams(vmem_limit_bytes=40 * 2**20),
        cost_estimate=cost(1.6),
    )(d_query, raw, cos_table, sin_table, gain, *after)


def halo_parts(d_keys, d_values, rows, *after):
    width, count = d_keys.shape
    parts = count // rows - 1

    def kernel(d_keys_ref, d_values_ref, *refs):
        for at, ref in enumerate(refs[len(after) :]):
            of = slice(at * rows, (at + 1) * rows)
            ref[:width, :] = d_keys_ref[:, of].astype(bf16)
            ref[width:, :] = d_values_ref[:, of].astype(bf16)

    whole = pl.BlockSpec((width, count), lambda i: (0, 0))
    return pl.pallas_call(
        kernel,
        grid=(1,),
        in_specs=[whole, whole] + [ANYWHERE] * len(after),
        out_specs=[pl.BlockSpec((2 * width, rows), lambda i: (0, 0))] * parts,
        out_shape=[jax.ShapeDtypeStruct((2 * width, rows), bf16)] * parts,
        compiler_params=pltpu.CompilerParams(vmem_limit_bytes=40 * 2**20),
        cost_estimate=cost(1),
    )(d_keys, d_values, *after)


def key_back(d_keys, d_values, got, raw, first, cos_table, sin_table, gain, *after):
    width, count = d_keys.shape
    rows = got[0].shape[1]
    own = pl.BlockSpec((width, rows), lambda i: (0, count // rows - 1))
    heads = width // HD

    def kernel(d_keys_ref, d_values_ref, raw_ref, cos_ref, sin_ref, gain_ref, *refs):
        out_ref, gain_out_ref = refs[len(got) + len(after) :]
        d_key = d_keys_ref[...]
        d_value = d_values_ref[...]
        for ref in refs[: len(got)]:
            d_key = d_key + ref[:width, :].astype(f32)
            d_value = d_value + ref[width:, :].astype(f32)
        results = []
        d_gain = jnp.zeros((HD, rows), f32)
        for head in range(heads):
            of = slice(head * HD, (head + 1) * HD)
            result, by_token = turn_back(
                d_key[of] * SCORE_SCALE, raw_ref[of, :], cos_ref[...], sin_ref[...], gain_ref[...]
            )
            results.append(result)
            d_gain = d_gain + by_token
        out_ref[...] = jnp.concatenate(results + [d_value], axis=0).astype(bf16).T
        gain_out_ref[...] = jnp.sum(d_gain, axis=1, keepdims=True)

    table = pl.BlockSpec((HD // 2, rows), lambda i: (0, 0))
    column = pl.BlockSpec((HD, 1), lambda i: (0, 0))
    return pl.pallas_call(
        kernel,
        grid=(1,),
        in_specs=[
            own,
            own,
            pl.BlockSpec((width, rows), lambda i: (first // width, 0)),
            table,
            table,
            column,
        ]
        + [pl.BlockSpec((2 * width, rows), lambda i: (0, 0))] * len(got)
        + [ANYWHERE] * len(after),
        out_specs=[pl.BlockSpec((rows, 2 * width), lambda i: (0, 0)), column],
        out_shape=[
            jax.ShapeDtypeStruct((rows, 2 * width), bf16),
            jax.ShapeDtypeStruct((HD, 1), f32),
        ],
        compiler_params=pltpu.CompilerParams(vmem_limit_bytes=40 * 2**20),
        cost_estimate=cost(1.6),
    )(d_keys, d_values, raw, cos_table, sin_table, gain, *got, *after)


def input_back(d_query, d_keyval, weights, values, scale, *after):
    rows, query_width = d_query.shape
    qkv_width = query_width + d_keyval.shape[1]
    width = weights.shape[0]
    tile = math.gcd(width, 256)

    def kernel(d_query_ref, d_keyval_ref, weights_ref, values_ref, scale_ref, *refs):
        out_ref, gain_out_ref = refs[len(after) :]
        part = nt_dot(d_query_ref[...], weights_ref[:, :query_width]) + nt_dot(
            d_keyval_ref[...], weights_ref[:, query_width:]
        )
        out_ref[...] = part.astype(bf16)
        product_sum = part * values_ref[...].astype(f32) * scale_ref[...]
        gain_out_ref[...] = jnp.sum(product_sum, axis=0, keepdims=True)

    out = pl.BlockSpec((rows, tile), lambda i: (0, i))
    return pl.pallas_call(
        kernel,
        grid=(width // tile,),
        in_specs=[
            pl.BlockSpec((rows, query_width), lambda i: (0, 0)),
            pl.BlockSpec((rows, qkv_width - query_width), lambda i: (0, 0)),
            pl.BlockSpec((tile, qkv_width), lambda i: (i, 0)),
            out,
            pl.BlockSpec((rows, 1), lambda i: (0, 0)),
        ]
        + [ANYWHERE] * len(after),
        out_specs=[out, pl.BlockSpec((1, tile), lambda i: (0, i))],
        out_shape=[
            jax.ShapeDtypeStruct((rows, width), bf16),
            jax.ShapeDtypeStruct((1, width), f32),
        ],
        compiler_params=pltpu.CompilerParams(vmem_limit_bytes=40 * 2**20),
        cost_estimate=cost(8),
    )(d_query, d_keyval, weights, values, scale, *after)


def gain_block(d_attn, d_ffn, d_query, d_key, places, *after):
    width = d_attn.shape[1]

    def kernel(d_attn_ref, d_ffn_ref, d_query_ref, d_key_ref, places_ref, *refs):
        out_ref = refs[-1]
        out_ref[...] = jnp.zeros_like(out_ref)
        heads = jnp.sum(
            d_query_ref[...] * places_ref[:HD, :].astype(f32)
            + d_key_ref[...] * places_ref[HD:, :].astype(f32),
            axis=0,
            keepdims=True,
        )
        out_ref[0:1, :] = d_attn_ref[...].astype(bf16)
        out_ref[1:2, :] = d_ffn_ref[...].astype(bf16)
        out_ref[2:3, :] = heads.astype(bf16)

    return pl.pallas_call(
        kernel,
        in_specs=[pl.BlockSpec(memory_space=pltpu.VMEM)] * 5 + [ANYWHERE] * len(after),
        out_shape=jax.ShapeDtypeStruct((LANES, width), bf16),
        cost_estimate=cost(1),
    )(d_attn, d_ffn, d_query, d_key, places, *after)


def side_by_side(first, second):
    rows, columns = first.shape
    step = math.gcd(rows, 32)

    def kernel(first_ref, second_ref, out_ref):
        out_ref[:, 0, :] = first_ref[...]
        out_ref[:, 1, :] = second_ref[...]

    return pl.pallas_call(
        kernel,
        grid=(rows // step,),
        in_specs=[pl.BlockSpec((step, columns), lambda i: (i, 0))] * 2,
        out_specs=pl.BlockSpec((step, 2, columns), lambda i: (i, 0, 0)),
        out_shape=jax.ShapeDtypeStruct((rows, 2, columns), first.dtype),
        cost_estimate=cost(4),
    )(first, second)


def attend_kernel(shift, q_ref, k_ref, v_ref, bias_ref, out_ref, inverse_ref):
    rows = q_ref.shape[1]
    for first in range(0, rows, TILE):
        at = slice(first, first + TILE)
        for head in range(GROUP):
            of = slice(head * HD, (head + 1) * HD)
            query = q_ref[of, at]
            total = jnp.zeros((HD + SUM_ROWS, TILE), f32)
            for start in range(first + shift, first + shift + WINDOW + TILE, TILE):
                near = slice(start, start + TILE)
                scores = nn_dot(k_ref[0, near, :], query)
                weight = jnp.exp2(scores * EXP2_SCALE + bias_ref[near, at]).astype(bf16)
                total = total + nn_dot(v_ref[0, :, near], weight)
            inverse = 1.0 / total[HD : HD + 1]
            out_ref[of, at] = (total[:HD] * inverse).astype(bf16)
            inverse_ref[0, head : head + 1, at] = inverse


def attend_back_kernel(shift, operands, *refs):
    q_ref, k_ref, kt_ref, v_ref, d_ref, o_ref, inverse_ref, bias_ref = refs[:8]
    dq_ref, dk_ref, dv_ref = refs[operands:]
    rows = q_ref.shape[1]
    dk_ref[...] = jnp.zeros_like(dk_ref)
    dv_ref[...] = jnp.zeros_like(dv_ref)
    for first in range(0, rows, TILE):
        at = slice(first, first + TILE)
        deltas = []
        for head in range(GROUP):
            of = slice(head * HD, (head + 1) * HD)
            product = d_ref[of, at].astype(f32) * o_ref[of, at].astype(f32)
            deltas.append(jnp.sum(product, axis=0, keepdims=True))
        d_query = [jnp.zeros((HD, TILE), f32) for _ in range(GROUP)]
        for start in range(first + shift, first + shift + WINDOW + TILE, TILE):
            near = slice(start, start + TILE)
            d_key = jnp.zeros((HD, TILE), f32)
            d_value = jnp.zeros((HD, TILE), f32)
            for head in range(GROUP):
                of = slice(head * HD, (head + 1) * HD)
                query = q_ref[of, at]
                d_out = d_ref[of, at]
                scores = nn_dot(k_ref[0, near, :], query)
                weight = jnp.exp2(scores * EXP2_SCALE + bias_ref[near, at])
                prob = weight * inverse_ref[0, head : head + 1, at]
                d_prob = nn_dot(v_ref[0, near, :], d_out)
                d_scores = (prob * (d_prob - deltas[head])).astype(bf16)
                d_query[head] = d_query[head] + nn_dot(kt_ref[:, near], d_scores)
                d_key = d_key + nt_dot(query, d_scores)
                d_value = d_value + nt_dot(d_out, prob.astype(bf16))
            dk_ref[:, near] += d_key
            dv_ref[:, near] += d_value
        for head in range(GROUP):
            dq_ref[head * HD : (head + 1) * HD, at] = d_query[head]


def attend(q_t, k, v_t, bias):
    kv, keys, _ = k.shape
    rows = q_t.shape[1]
    ones = jnp.ones((kv, SUM_ROWS, keys), bf16)
    v_ones = jnp.concatenate([v_t.reshape(kv, HD, keys), ones], axis=1)
    return pl.pallas_call(
        functools.partial(attend_kernel, keys - rows - WINDOW),
        grid=(kv,),
        in_specs=[
            pl.BlockSpec((GROUP * HD, rows), lambda h: (h, 0)),
            pl.BlockSpec((1, keys, HD), lambda h: (h, 0, 0)),
            pl.BlockSpec((1, HD + SUM_ROWS, keys), lambda h: (h, 0, 0)),
            pl.BlockSpec((keys, rows), lambda h: (0, 0)),
        ],
        out_specs=[
            pl.BlockSpec((GROUP * HD, rows), lambda h: (h, 0)),
            pl.BlockSpec((1, 8, rows), lambda h: (h, 0, 0)),
        ],
        out_shape=[jax.ShapeDtypeStruct((kv * GROUP * HD, rows), bf16), jax.ShapeDtypeStruct((kv, 8, rows), f32)],
        compiler_params=pltpu.CompilerParams(vmem_limit_bytes=40 * 2**20),
        cost_estimate=cost(13),
    )(q_t, k, v_ones, bias)


def attend_back(at, so_far, after, q_t, k, k_t, v, d_t, o_t, inverse, bias):
    kv, keys, _ = k.shape
    rows = q_t.shape[1]
    head_block = pl.BlockSpec((GROUP * HD, rows), lambda i: (at, 0))
    key_block = pl.BlockSpec((1, keys, HD), lambda i: (at, 0, 0))
    key_t_block = pl.BlockSpec((HD, keys), lambda i: (at, 0))
    waits = [*so_far, *after]
    operands = 8 + len(waits)
    return pl.pallas_call(
        functools.partial(attend_back_kernel, keys - rows - WINDOW, operands),
        grid=(1,),
        in_specs=[
            head_block,
            key_block,
            key_t_block,
            key_block,
            head_block,
            head_block,
            pl.BlockSpec((1, 8, rows), lambda i: (at, 0, 0)),
            pl.BlockSpec((keys, rows), lambda i: (0, 0)),
        ]
        + [pl.BlockSpec(memory_space=pl.ANY)] * len(waits),
        out_specs=[head_block, key_t_block, key_t_block],
        out_shape=[
            jax.ShapeDtypeStruct((kv * GROUP * HD, rows), f32),
            jax.ShapeDtypeStruct((kv * HD, keys), f32),
            jax.ShapeDtypeStruct((kv * HD, keys), f32),
        ],
        input_output_aliases={8 + i: i for i in range(len(so_far))},
        compiler_params=pltpu.CompilerParams(vmem_limit_bytes=40 * 2**20),
        cost_estimate=cost(11),
    )(q_t, k, k_t, v, d_t, o_t, inverse, bias, *waits)


def feed_kernel(n_ref, d_act_ref, gate_ref, up_ref, *refs):
    act_ref, d_gate_ref, d_up_ref = refs[-3:]
    normed = n_ref[...]
    gate = nn_dot(normed, gate_ref[...])
    up = nn_dot(normed, up_ref[...])
    sigmoid = 1.0 / (1.0 + jnp.exp(-gate))
    silu = gate * sigmoid
    act_ref[...] = (silu * up).astype(bf16)
    d_act = d_act_ref[...]
    d_gate_ref[...] = (d_act * up * sigmoid * (1.0 + gate * (1.0 - sigmoid))).astype(bf16)
    d_up_ref[...] = (d_act * silu).astype(bf16)


def feed(normed, d_act, gateup, *after):
    rows, width = normed.shape
    hidden = d_act.shape[1]
    tile = math.gcd(hidden, 512)
    steps = hidden // tile
    hidden_block = pl.BlockSpec((rows, tile), lambda i: (0, i))
    return pl.pallas_call(
        feed_kernel,
        grid=(steps,),
        in_specs=[
            pl.BlockSpec((rows, width), lambda i: (0, 0)),
            hidden_block,
            pl.BlockSpec((width, tile), lambda i: (0, i)),
            pl.BlockSpec((width, tile), lambda i: (0, i + steps)),
        ]
        + [ANYWHERE] * len(after),
        out_specs=[hidden_block] * 3,
        out_shape=[jax.ShapeDtypeStruct((rows, hidden), bf16)] * 3,
        compiler_params=pltpu.CompilerParams(vmem_limit_bytes=56 * 2**20),
        cost_estimate=cost(19.5),
    )(normed, d_act, gateup, gateup, *after)


def feed_back(d_gate, d_up, gateup, *after):
    rows, hidden = d_gate.shape
    width = gateup.shape[0]
    tile = math.gcd(width, 256)

    def kernel(d_gate_ref, d_up_ref, gate_ref, up_ref, *refs):
        total = nt_dot(d_gate_ref[...], gate_ref[...]) + nt_dot(d_up_ref[...], up_ref[...])
        refs[-1][...] = total.astype(bf16)

    whole = pl.BlockSpec((rows, hidden), lambda i: (0, 0))
    return pl.pallas_call(
        kernel,
        grid=(width // tile,),
        in_specs=[
            whole,
            whole,
            pl.BlockSpec((tile, hidden), lambda i: (i, 0)),
            pl.BlockSpec((tile, hidden), lambda i: (i, 1)),
        ]
        + [ANYWHERE] * len(after),
        out_specs=pl.BlockSpec((rows, tile), lambda i: (0, i)),
        out_shape=jax.ShapeDtypeStruct((rows, width), bf16),
        compiler_params=pltpu.CompilerParams(vmem_limit_bytes=56 * 2**20),
        cost_estimate=cost(17),
    )(d_gate, d_up, gateup, gateup, *after)


def feed_out(act, downs, down_start, *after):
    rows, hidden = act.shape
    width, columns = downs.shape
    tile = math.gcd(width, 256)

    def kernel(act_ref, down_ref, *refs):
        refs[-1][...] = nt_dot(act_ref[...], down_ref[:, down_start:]).astype(bf16)

    return pl.pallas_call(
        kernel,
        grid=(width // tile,),
        in_specs=[
            pl.BlockSpec((rows, hidden), lambda i: (0, 0)),
            pl.BlockSpec((tile, columns), lambda i: (i, 0)),
        ]
        + [ANYWHERE] * len(after),
        out_specs=pl.BlockSpec((rows, tile), lambda i: (0, i)),
        out_shape=jax.ShapeDtypeStruct((rows, width), bf16),
        compiler_params=pltpu.CompilerParams(vmem_limit_bytes=56 * 2**20),
        cost_estimate=cost(9),
    )(act, downs, *after)


def shards(
    tokens,
    w_query,
    w_keyval,
    w_out,
    w_gateup,
    w_down,
    attn_gain,
    ffn_gain,
    qk_gain,
    segments,
    positions,
    cotangent,
):
    ring = Ring()
    row_count = tokens.shape[0]
    depth = w_query.shape[0]
    model = tokens.shape[1]
    hidden = w_gateup.shape[2]
    tensor = lax.axis_index("tensor")
    query_width = w_query.shape[1]
    local_heads = query_width // HD
    local_kv = local_heads // GROUP
    kv_width = local_kv * HD
    all_kv = w_keyval.shape[1] // 2
    qkv_width = query_width + 2 * kv_width
    gain_count = 2 * qk_gain.shape[1]

    own_keyval = lax.dynamic_index_in_dim(
        w_keyval.reshape(depth, 2, all_kv // kv_width, kv_width), tensor, 2, keepdims=False
    ).reshape(depth, 2 * kv_width)
    head_gain_column = jnp.pad(qk_gain.reshape(gain_count), (0, depth - gain_count))
    gains = jnp.stack([attn_gain, ffn_gain, head_gain_column], axis=1)
    gains = jnp.pad(gains, ((0, 0), (0, LANES - gains.shape[1])))
    first_pack = jnp.concatenate([w_query, own_keyval, w_out.T, gains, w_down.T], axis=1)
    first_full = lax.all_gather(first_pack.astype(bf16), "dp", axis=0, tiled=True)
    gateup_full = lax.all_gather(
        w_gateup.reshape(depth, 2 * hidden).astype(bf16), "dp", axis=0, tiled=True
    )
    qkv_full = first_full[:, :qkv_width]
    gain_start = qkv_width + query_width
    out_full = first_full[:, qkv_width:gain_start]
    down_full = first_full[:, gain_start + LANES :]
    gain_columns = first_full[:, gain_start : gain_start + 3].astype(f32)
    attn_weight = gain_columns[:, 0]
    ffn_weight = gain_columns[:, 1]
    head_gains = gain_columns[:, 2].reshape(ring.count, depth)[:, :gain_count]
    head_gains = head_gains.reshape(ring.count, 2, qk_gain.shape[1]).transpose(1, 0, 2).reshape(2, HD)
    gain_query = head_gains[0][:, None]
    gain_key = head_gains[1][:, None]

    marks = (segments + 1).astype(bf16)
    seq_devices = min(SEQ_LEN // row_count, ring.count)
    own_sequence = ring.index // seq_devices
    reach_count = -(-WINDOW // row_count)
    halo_marks = []
    for step_back in range(reach_count, 0, -1):
        same_sequence = ((ring.index - step_back) // seq_devices == own_sequence).astype(bf16)
        halo_marks.append(from_behind(marks, step_back) * same_sequence)
    key_marks = jnp.concatenate(halo_marks + [marks], axis=0)
    key_count = key_marks.shape[0]
    distance = (jnp.arange(row_count, dtype=jnp.int32) + reach_count * row_count)[
        None, :
    ] - jnp.arange(key_count, dtype=jnp.int32)[:, None]
    allowed = (distance >= 0) & (distance < WINDOW) & (key_marks[:, None] == marks[None, :])
    bias = jnp.where(allowed, 0.0, MASKED).astype(f32)
    cos_table, sin_table = angles_of(positions)

    residual = tokens.astype(f32)
    attn_scale = inverse_rms(residual, 1)

    normed_low = (residual * attn_scale * attn_weight).astype(bf16)
    qkv_raw = lax.dot_general(
        qkv_full, normed_low, (((0,), (1,)), ((), ())), preferred_element_type=f32
    )
    query_raw = qkv_raw[:query_width].reshape(local_heads, HD, row_count)
    key_raw = qkv_raw[query_width : query_width + kv_width].reshape(local_kv, HD, row_count)
    query_scale = inverse_rms(query_raw, 1)
    key_scale = inverse_rms(key_raw, 1)
    query_low = rotate(query_raw * query_scale * gain_query, cos_table, sin_table).astype(bf16)
    key_low = rotate(key_raw * key_scale * gain_key, cos_table, sin_table).astype(bf16)
    query_low = query_low.reshape(query_width, row_count)
    keyval_low = jnp.concatenate(
        [key_low.reshape(kv_width, row_count), qkv_raw[query_width + kv_width :].astype(bf16)], axis=0
    )
    halo = [from_behind(keyval_low, step_back) for step_back in range(reach_count, 0, -1)]
    key_keyval = jnp.concatenate(halo + [keyval_low], axis=1)
    keys_t = key_keyval[:kv_width]
    values_t = key_keyval[kv_width:]
    keys = keys_t.reshape(local_kv, HD, key_count).transpose(0, 2, 1)
    values = values_t.reshape(local_kv, HD, key_count).transpose(0, 2, 1)
    attended, inverse_total = attend(query_low, keys, values_t, bias)
    mid_part = lax.dot_general(
        attended, out_full, (((0,), (1,)), ((), ())), preferred_element_type=f32
    )
    near_first = ring.bits
    far_first = [1, 4, 2] + ring.bits[3:]
    normed_rows = ring.chosen(normed_low, near_first)
    cotangent_rows = ring.chosen(cotangent, far_first)
    attended_back = attended.T
    mid = residual + tensor_sum(
        mid_part, corner(normed_rows), corner(cotangent_rows), corner(attended_back)
    )

    d_act = nn_dot(cotangent, down_full)
    ffn_scale = inverse_rms(mid, 1)
    normed2_low = (mid * ffn_scale * ffn_weight).astype(bf16)
    normed2_rows = ring.chosen(normed2_low, near_first)
    act_low, d_gate, d_up = feed(normed2_low, d_act, gateup_full, normed2_rows)
    gate_sum = Scatter(ring, normed2_rows, d_gate, near_first)
    up_sum = Scatter(ring, normed2_rows, d_up, near_first)
    down_sum = Scatter(ring, cotangent_rows, act_low, far_first)
    before = gate_sum.send()
    d_normed2_low = feed_back(d_gate, d_up, gateup_full, before)
    d_normed2_other = other_tensor(d_normed2_low)
    before = gate_sum.send(d_normed2_low)
    before = up_sum.send(before)
    before = down_sum.send(before)
    result_low = feed_out(act_low, first_full, gain_start + LANES, before)
    before = up_sum.send(result_low)
    before = down_sum.send(before)
    d_mid, d_mid_low, d_ffn_weight = norm_back(
        mid, cotangent, d_normed2_low, d_normed2_other, ffn_weight, before
    )
    result_low = tie(result_low, d_normed2_other)
    result_other = other_tensor(result_low)

    d_attended = product_tt(first_full, qkv_width, query_width, d_mid_low)
    grads = ()
    for at in range(local_kv):
        grads = attend_back(
            at, grads, (), query_low, keys, keys_t, values, d_attended, attended, inverse_total, bias
        )
    d_query, d_keys, d_values = grads
    parts = halo_parts(d_keys, d_values, row_count)
    got = [from_behind(part, at - reach_count) for at, part in enumerate(parts)]
    before = gate_sum.send(parts[0])
    d_query_low, d_gain_query = query_back(
        d_query, qkv_raw, cos_table[0], sin_table[0], gain_query, before
    )
    query_sum = Scatter(ring, normed_rows, d_query_low, near_first)
    before = query_sum.send()
    before = down_sum.send(before)
    d_mid_rows = ring.chosen(tie(d_mid_low, before), near_first)
    out_sum = Scatter(ring, d_mid_rows, attended_back, near_first)
    before = out_sum.send()
    d_keyval_low, d_gain_key = key_back(
        d_keys, d_values, got, qkv_raw, query_width, cos_table[0], sin_table[0], gain_key, before
    )
    d_normed_low, d_attn_part = input_back(
        d_query_low, d_keyval_low, first_full, tokens, attn_scale
    )
    d_normed_other = other_tensor(d_normed_low)
    places = jnp.arange(2 * HD, dtype=jnp.int32)
    per_device = gain_count // 2
    places = places % HD // per_device * depth + places // HD * per_device + places % per_device
    places = (places[:, None] == jnp.arange(model, dtype=jnp.int32)[None, :]).astype(bf16)
    gain_grads = gain_block(d_attn_part, d_ffn_weight, d_gain_query, d_gain_key, places)
    gain_rows = ring.chosen(gain_grads, near_first)
    shared_sum = Scatter(ring, normed_rows, d_keyval_low, near_first, gain_rows)
    before = shared_sum.send()
    before = up_sum.send(before)
    before = query_sum.send(before)
    before = out_sum.send(before)
    before = shared_sum.send(before)
    before = gate_sum.send(before)
    output = add_up(mid, result_low, result_other, before)
    before = down_sum.send(output)
    before = query_sum.send(before)
    before = out_sum.send(before)
    before = shared_sum.send(before)
    before = up_sum.send(before)
    before = query_sum.send(before)
    before = out_sum.send(before)
    before = shared_sum.send(before)
    for rest in (down_sum, gate_sum, up_sum, query_sum, out_sum, shared_sum):
        while len(rest.got) < len(rest.bits):
            before = rest.send(before)
    grad_down = down_sum.total(before, transposed=True)
    gate_total = gate_sum.total(grad_down)
    grad_query = query_sum.total(gate_total)
    grad_out = out_sum.total(grad_query, transposed=True)
    shared = shared_sum.total(grad_out).astype(bf16)
    _, input_grad, _ = norm_back(
        tokens, d_mid, d_normed_low, d_normed_other, attn_weight, shared
    )
    grad_gateup = side_by_side(gate_total, up_sum.total(input_grad))
    shared_other = other_tensor(shared).astype(f32)
    shared = shared.astype(f32)
    first = tensor == 0
    keyval_mine = shared[:, : 2 * kv_width].reshape(depth, 2, 1, kv_width)
    keyval_theirs = shared_other[:, : 2 * kv_width].reshape(depth, 2, 1, kv_width)
    grad_keyval = jnp.concatenate(
        [
            jnp.where(first, keyval_mine, keyval_theirs),
            jnp.where(first, keyval_theirs, keyval_mine),
        ],
        axis=2,
    ).reshape(depth, 2 * all_kv)
    gains_mine = shared[:, 2 * kv_width :]
    gains_sum = gains_mine + shared_other[:, 2 * kv_width :]
    grad_attn_gain = gains_sum[:, 0]
    grad_ffn_gain = gains_mine[:, 1]
    grad_heads = gains_sum[:gain_count, 2].reshape(2, gain_count // 2)
    return (
        output,
        input_grad,
        grad_query,
        grad_keyval,
        grad_out,
        grad_gateup,
        grad_down,
        grad_attn_gain,
        grad_ffn_gain,
        grad_heads,
    )


def solution(mesh):
    in_specs = (
        P("dp", None),
        P("dp", "tensor"),
        P("dp", None),
        P("tensor", "dp"),
        P("dp", None, "tensor"),
        P("tensor", "dp"),
        P("dp"),
        P("dp"),
        P(None, "dp"),
        P("dp"),
        P("dp"),
        P("dp", None),
    )
    out_specs = (
        P("dp", None),
        P("dp", None),
        P("dp", "tensor"),
        P("dp", None),
        P("tensor", "dp"),
        P("dp", None, "tensor"),
        P("tensor", "dp"),
        P("dp"),
        P("dp"),
        P(None, "dp"),
    )
    return jax.shard_map(shards, mesh=mesh, in_specs=in_specs, out_specs=out_specs, check_vma=False)
```

```python
import functools
import math

import jax
import jax.numpy as jnp
from jax import lax
from jax.experimental import pallas as pl
from jax.experimental.pallas import tpu as pltpu
from jax.sharding import PartitionSpec as P

QH = 24
KVH = 6
HD = 64
GROUP = QH // KVH
WINDOW = 1024
SEQ_LEN = 8192
LANES = 128

EPSILON = 1e-06
SCORE_SCALE = 0.125
MASKED = -1e30
ROPE_BASE = 10000.0
EXP2_SCALE = SCORE_SCALE * math.log2(math.e)
TILE = 256
SUM_ROWS = 16
PARTS = 4
ORDER = (
    "D", "G", "FB", "U", "G", "FO", "U", "NB", "DA", "H", "H", "G",
    "H", "HP", "QB", "Q", "OP", "O", "G", "Q", "O", "KB", "U", "IB",
    "G", "Q", "O", "GB", "K", "K", "U", "Q", "O", "K", "IG", "K",
    "AD", "D", "U", "Q", "O", "K",
)
LINK_SHARE = 0.35

bf16 = jnp.bfloat16
f32 = jnp.float32
ANYWHERE = pl.BlockSpec(memory_space=pl.ANY)


def cost(microseconds):
    return pl.CostEstimate(
        flops=int(microseconds * LINK_SHARE * 1.15e9), bytes_accessed=0, transcendentals=0
    )


def angles_of(positions):
    half_width = HD // 2
    frequency = jnp.exp(
        jnp.arange(half_width, dtype=f32) * (-math.log(ROPE_BASE) / half_width)
    )
    phases = frequency[:, None] * positions.astype(f32)[None, :]
    return jnp.cos(phases)[None], jnp.sin(phases)[None]


def rotate(values, cos_table, sin_table):
    half_width = values.shape[1] // 2
    first_half = values[:, :half_width]
    second_half = values[:, half_width:]
    return jnp.concatenate(
        [
            first_half * cos_table - second_half * sin_table,
            second_half * cos_table + first_half * sin_table,
        ],
        axis=1,
    )


def inverse_rms(values, axis):
    return lax.rsqrt(jnp.mean(values * values, axis=axis, keepdims=True) + EPSILON)


def rms_back(values, scale, weight, d_out, axis):
    weighted = d_out * weight
    pull = jnp.mean(weighted * values, axis=axis, keepdims=True)
    return scale * weighted - values * (scale * scale * scale * pull)


class Ring:
    def __init__(self):
        self.count = lax.axis_size("dp")
        self.index = lax.axis_index("dp")
        self.bits = [1 << at for at in range(self.count.bit_length() - 1)]

    def order(self, bits):
        order = []
        for at in range(self.count - 1, -1, -1):
            flips = sum(bit for place, bit in enumerate(reversed(bits)) if at >> place & 1)
            order.append(self.index ^ flips)
        return jnp.stack(order).astype(jnp.int32)

    def chosen(self, array, bits):
        depth = array.shape[1] // self.count
        if depth % LANES:
            blocks = array.T.reshape(self.count, depth, array.shape[0])
            return jnp.take(blocks, self.order(bits), axis=0).reshape(array.shape[1], array.shape[0])
        return transposed_blocks(self.order(bits), array, depth)


class Scatter:
    def __init__(self, ring, left, right, bits, tail=None):
        self.ring, self.left, self.right, self.bits, self.tail = ring, left, right, bits, tail
        self.got = []

    def rows(self):
        step = len(self.got)
        last = step == len(self.bits)
        size = self.left.shape[0] >> (step if last else step + 1)
        start = self.left.shape[0] - (self.left.shape[0] >> step)
        adds = []
        for at, parts in enumerate(self.got):
            first = start - self.left.shape[0] + (self.left.shape[0] >> at + 1)
            height = parts[0].shape[0]
            if height >= size:
                adds.append([(parts[first // height], first % height // size)])
            else:
                adds.append([(part, 0) for part in parts[first // height : (first + size) // height]])
        return size, start // size, adds

    def send(self, *after, parts=1):
        size, block, adds = self.rows()
        sent = product(
            self.left, self.right, size, block, adds, after, self.tail, parts=parts
        )
        bit = self.bits[len(self.got)]
        pairs = [(i, i ^ bit) for i in range(self.ring.count)]
        self.got.append([lax.ppermute(part, "dp", pairs) for part in sent])
        return sent[0]

    def total(self, *after, transposed=False):
        while len(self.got) < len(self.bits):
            after = (self.send(*after),)
        size, block, adds = self.rows()
        return product(self.left, self.right, size, block, adds, after, self.tail, f32, transposed)[0]


def other_tensor(array):
    count = lax.axis_size("tensor")
    return lax.ppermute(array, "tensor", [(i, (i + 1) % count) for i in range(count)])


def tensor_sum(partial, *before):
    low = partial.astype(bf16)
    other = other_tensor(low)
    if before:
        other = tie(other, *before)
    return low.astype(f32) + other.astype(f32)


def from_behind(shard, by):
    length = lax.axis_size("dp")
    pairs = [(i, i + by) for i in range(length) if 0 <= i + by < length]
    return lax.ppermute(shard, "dp", pairs)


def tn_dot(left, right):
    return lax.dot_general(left, right, (((0,), (0,)), ((), ())), preferred_element_type=f32)


def nt_dot(left, right):
    return lax.dot_general(left, right, (((1,), (1,)), ((), ())), preferred_element_type=f32)


def nn_dot(left, right):
    return jnp.dot(left, right, preferred_element_type=f32)


def tie(array, *others):
    def kernel(*refs):
        del refs

    return pl.pallas_call(
        kernel,
        in_specs=[pl.BlockSpec(memory_space=pl.ANY)] * (1 + len(others)),
        out_specs=pl.BlockSpec(memory_space=pl.ANY),
        out_shape=jax.ShapeDtypeStruct(array.shape, array.dtype),
        input_output_aliases={0: 0},
        cost_estimate=cost(0),
    )(array, *others)


def corner(array):
    return array[: 2 * 8, :LANES]


def transposed(array, *after):
    tokens, width = array.shape
    step = math.gcd(tokens, LANES)

    def kernel(in_ref, *refs):
        refs[-1][...] = in_ref[...].T

    return pl.pallas_call(
        kernel,
        grid=(tokens // step,),
        in_specs=[pl.BlockSpec((step, width), lambda i: (i, 0))] + [ANYWHERE] * len(after),
        out_specs=pl.BlockSpec((width, step), lambda i: (0, i)),
        out_shape=jax.ShapeDtypeStruct((width, tokens), array.dtype),
        cost_estimate=cost(4.8),
    )(array, *after)


def transposed_blocks(order, array, depth):
    tokens, width = array.shape
    step = math.gcd(tokens, LANES)

    def kernel(order_ref, in_ref, out_ref):
        for at in range(width // depth):
            column = pl.multiple_of(order_ref[at] * depth, depth)
            out_ref[at * depth : (at + 1) * depth, :] = in_ref[:, pl.ds(column, depth)].T

    return pl.pallas_call(
        kernel,
        grid_spec=pltpu.PrefetchScalarGridSpec(
            num_scalar_prefetch=1,
            grid=(tokens // step,),
            in_specs=[pl.BlockSpec((step, width), lambda i, order: (i, 0))],
            out_specs=pl.BlockSpec((width, step), lambda i, order: (0, i)),
        ),
        out_shape=jax.ShapeDtypeStruct((width, tokens), array.dtype),
        cost_estimate=cost(4.8),
    )(order, array)


def product(
    left, right, size, block, adds, after=(), tail=None, out_type=bf16, transposed=False, parts=1
):
    depth, columns = right.shape
    most = max(LANES, min(columns, 512 * 1024 // size))
    tile = max(t for t in range(LANES, most + 1, LANES) if columns % t == 0)
    if tail is not None:
        tile = LANES
    steps = columns // tile
    flat = [(array, row, size // len(add)) for add in adds for array, row in add]

    def kernel(left_ref, right_ref, *refs):
        def put(total):
            at = 0
            for add in adds:
                pieces = [ref[...].astype(f32) for ref in refs[at : at + len(add)]]
                total = total + (pieces[0] if len(add) == 1 else jnp.concatenate(pieces, axis=0))
                at += len(add)
            total = (total.T if transposed else total).astype(out_type)
            height = total.shape[0] // parts
            for at, ref in enumerate(refs[len(refs) - parts :]):
                ref[...] = total[at * height : (at + 1) * height]

        if tail is None:
            put(nn_dot(left_ref[...], right_ref[...]))
            return

        @pl.when(pl.program_id(0) < steps)
        def _():
            put(nn_dot(left_ref[...], right_ref[...]))

        @pl.when(pl.program_id(0) == steps)
        def _():
            put(refs[len(flat)][...].astype(f32))

    all_columns = columns
    in_specs = [
        pl.BlockSpec((size, depth), lambda i: (block, 0)),
        pl.BlockSpec((depth, tile), lambda i: (0, jnp.minimum(i, steps - 1))),
    ] + [
        pl.BlockSpec((height, tile), functools.partial(lambda i, row: (row, i), row=row))
        for _, row, height in flat
    ]
    operands = [left, right, *[array for array, _, _ in flat]]
    if tail is not None:
        all_columns += LANES
        in_specs.append(pl.BlockSpec((size, LANES), lambda i: (block, 0)))
        operands.append(tail)
    height = size // parts
    out_shape, out_block, out_map = (height, all_columns), (height, tile), lambda i: (0, i)
    if transposed:
        out_shape, out_block, out_map = (all_columns, height), (tile, height), lambda i: (i, 0)
    return pl.pallas_call(
        kernel,
        grid=(all_columns // tile,),
        in_specs=in_specs + [ANYWHERE] * len(after),
        out_specs=[pl.BlockSpec(out_block, out_map)] * parts,
        out_shape=[jax.ShapeDtypeStruct(out_shape, out_type)] * parts,
        compiler_params=pltpu.CompilerParams(vmem_limit_bytes=40 * 2**20),
        cost_estimate=cost(2 + 2 * size * depth * columns / 0.9e9),
    )(*operands, *after)


def product_tt(left, first, columns, right):
    depth = left.shape[0]
    rows = right.shape[0]
    tile = max(t for t in range(LANES, 384 + 1, LANES) if columns % t == 0 and first % t == 0)

    def kernel(left_ref, right_ref, out_ref):
        out_ref[...] = nt_dot(left_ref[...].T, right_ref[...]).astype(bf16)

    return pl.pallas_call(
        kernel,
        grid=(columns // tile,),
        in_specs=[
            pl.BlockSpec((depth, tile), lambda i: (0, i + first // tile)),
            pl.BlockSpec((rows, depth), lambda i: (0, 0)),
        ],
        out_specs=pl.BlockSpec((tile, rows), lambda i: (i, 0)),
        out_shape=jax.ShapeDtypeStruct((columns, rows), bf16),
        compiler_params=pltpu.CompilerParams(vmem_limit_bytes=40 * 2**20),
        cost_estimate=cost(4.3),
    )(left, right)


def norm_back(values, direct, part, other, gain, *after):
    rows, width = values.shape
    step = math.gcd(rows, 128)

    def kernel(values_ref, direct_ref, part_ref, other_ref, gain_ref, *refs):
        out_ref, low_ref, gain_out_ref = refs[len(after) :]
        value = values_ref[...].astype(f32)
        scale = inverse_rms(value, 1)
        d_out = part_ref[...].astype(f32) + other_ref[...].astype(f32)
        result = direct_ref[...].astype(f32) + rms_back(value, scale, gain_ref[...], d_out, 1)
        out_ref[...] = result
        low_ref[...] = result.astype(bf16)

        @pl.when(pl.program_id(0) == 0)
        def _():
            gain_out_ref[...] = jnp.zeros_like(gain_out_ref)

        gain_out_ref[...] += jnp.sum(d_out * value * scale, axis=0, keepdims=True)

    block = pl.BlockSpec((step, width), lambda i: (i, 0))
    row = pl.BlockSpec((1, width), lambda i: (0, 0))
    return pl.pallas_call(
        kernel,
        grid=(rows // step,),
        in_specs=[block] * 4 + [row] + [ANYWHERE] * len(after),
        out_specs=[block, block, row],
        out_shape=[
            jax.ShapeDtypeStruct((rows, width), f32),
            jax.ShapeDtypeStruct((rows, width), bf16),
            jax.ShapeDtypeStruct((1, width), f32),
        ],
        compiler_params=pltpu.CompilerParams(vmem_limit_bytes=40 * 2**20),
        cost_estimate=cost(7),
    )(values, direct, part, other, gain[None, :], *after)


def add_up(values, part, other, *after):
    rows, width = values.shape
    step = math.gcd(rows, 128)

    def kernel(values_ref, part_ref, other_ref, *refs):
        added = part_ref[...].astype(f32) + other_ref[...].astype(f32)
        refs[-1][...] = (values_ref[...] + added).astype(bf16)

    block = pl.BlockSpec((step, width), lambda i: (i, 0))
    return pl.pallas_call(
        kernel,
        grid=(rows // step,),
        in_specs=[block] * 3 + [ANYWHERE] * len(after),
        out_specs=block,
        out_shape=jax.ShapeDtypeStruct((rows, width), bf16),
        cost_estimate=cost(3),
    )(values, part, other, *after)


def turn_back(d_rotated, raw, cos_table, sin_table, gain):
    half_width = HD // 2
    first, second = d_rotated[:half_width], d_rotated[half_width:]
    d_normed = jnp.concatenate(
        [first * cos_table + second * sin_table, second * cos_table - first * sin_table], axis=0
    )
    scale = inverse_rms(raw, 0)
    return rms_back(raw, scale, gain, d_normed, 0), d_normed * raw * scale


def query_back(d_query, raw, cos_table, sin_table, gain, *after):
    width, rows = d_query.shape
    step = GROUP * HD

    def kernel(d_ref, raw_ref, cos_ref, sin_ref, gain_ref, *refs):
        out_ref, gain_out_ref = refs[len(after) :]
        results = []
        d_gain = jnp.zeros((HD, rows), f32)
        for head in range(GROUP):
            of = slice(head * HD, (head + 1) * HD)
            result, by_token = turn_back(
                d_ref[of, :] * SCORE_SCALE, raw_ref[of, :], cos_ref[...], sin_ref[...], gain_ref[...]
            )
            results.append(result)
            d_gain = d_gain + by_token
        out_ref[...] = jnp.concatenate(results, axis=0).astype(bf16).T

        @pl.when(pl.program_id(0) == 0)
        def _():
            gain_out_ref[...] = jnp.zeros_like(gain_out_ref)

        gain_out_ref[...] += jnp.sum(d_gain, axis=1, keepdims=True)

    block = pl.BlockSpec((step, rows), lambda i: (i, 0))
    table = pl.BlockSpec((HD // 2, rows), lambda i: (0, 0))
    column = pl.BlockSpec((HD, 1), lambda i: (0, 0))
    return pl.pallas_call(
        kernel,
        grid=(width // step,),
        in_specs=[block, block, table, table, column] + [ANYWHERE] * len(after),
        out_specs=[pl.BlockSpec((rows, step), lambda i: (0, i)), column],
        out_shape=[
            jax.ShapeDtypeStruct((rows, width), bf16),
            jax.ShapeDtypeStruct((HD, 1), f32),
        ],
        compiler_params=pltpu.CompilerParams(vmem_limit_bytes=40 * 2**20),
        cost_estimate=cost(1.6),
    )(d_query, raw, cos_table, sin_table, gain, *after)


def halo_parts(d_keys, d_values, rows, *after):
    width, count = d_keys.shape
    parts = count // rows - 1

    def kernel(d_keys_ref, d_values_ref, *refs):
        for at, ref in enumerate(refs[len(after) :]):
            of = slice(at * rows, (at + 1) * rows)
            ref[:width, :] = d_keys_ref[:, of].astype(bf16)
            ref[width:, :] = d_values_ref[:, of].astype(bf16)

    whole = pl.BlockSpec((width, count), lambda i: (0, 0))
    return pl.pallas_call(
        kernel,
        grid=(1,),
        in_specs=[whole, whole] + [ANYWHERE] * len(after),
        out_specs=[pl.BlockSpec((2 * width, rows), lambda i: (0, 0))] * parts,
        out_shape=[jax.ShapeDtypeStruct((2 * width, rows), bf16)] * parts,
        compiler_params=pltpu.CompilerParams(vmem_limit_bytes=40 * 2**20),
        cost_estimate=cost(1),
    )(d_keys, d_values, *after)


def key_back(d_keys, d_values, got, raw, first, cos_table, sin_table, gain, *after):
    width, count = d_keys.shape
    rows = got[0].shape[1]
    own = pl.BlockSpec((width, rows), lambda i: (0, count // rows - 1))
    heads = width // HD

    def kernel(d_keys_ref, d_values_ref, raw_ref, cos_ref, sin_ref, gain_ref, *refs):
        out_ref, gain_out_ref = refs[len(got) + len(after) :]
        d_key = d_keys_ref[...]
        d_value = d_values_ref[...]
        for ref in refs[: len(got)]:
            d_key = d_key + ref[:width, :].astype(f32)
            d_value = d_value + ref[width:, :].astype(f32)
        results = []
        d_gain = jnp.zeros((HD, rows), f32)
        for head in range(heads):
            of = slice(head * HD, (head + 1) * HD)
            result, by_token = turn_back(
                d_key[of] * SCORE_SCALE, raw_ref[of, :], cos_ref[...], sin_ref[...], gain_ref[...]
            )
            results.append(result)
            d_gain = d_gain + by_token
        out_ref[...] = jnp.concatenate(results + [d_value], axis=0).astype(bf16).T
        gain_out_ref[...] = jnp.sum(d_gain, axis=1, keepdims=True)

    table = pl.BlockSpec((HD // 2, rows), lambda i: (0, 0))
    column = pl.BlockSpec((HD, 1), lambda i: (0, 0))
    return pl.pallas_call(
        kernel,
        grid=(1,),
        in_specs=[
            own,
            own,
            pl.BlockSpec((width, rows), lambda i: (first // width, 0)),
            table,
            table,
            column,
        ]
        + [pl.BlockSpec((2 * width, rows), lambda i: (0, 0))] * len(got)
        + [ANYWHERE] * len(after),
        out_specs=[pl.BlockSpec((rows, 2 * width), lambda i: (0, 0)), column],
        out_shape=[
            jax.ShapeDtypeStruct((rows, 2 * width), bf16),
            jax.ShapeDtypeStruct((HD, 1), f32),
        ],
        compiler_params=pltpu.CompilerParams(vmem_limit_bytes=40 * 2**20),
        cost_estimate=cost(1.6),
    )(d_keys, d_values, raw, cos_table, sin_table, gain, *got, *after)


def input_back(d_query, d_keyval, weights, values, scale, *after):
    rows, query_width = d_query.shape
    qkv_width = query_width + d_keyval.shape[1]
    width = weights.shape[0]
    tile = math.gcd(width, 256)

    def kernel(d_query_ref, d_keyval_ref, weights_ref, values_ref, scale_ref, *refs):
        out_ref, gain_out_ref = refs[len(after) :]
        part = nt_dot(d_query_ref[...], weights_ref[:, :query_width]) + nt_dot(
            d_keyval_ref[...], weights_ref[:, query_width:]
        )
        out_ref[...] = part.astype(bf16)
        product_sum = part * values_ref[...].astype(f32) * scale_ref[...]
        gain_out_ref[...] = jnp.sum(product_sum, axis=0, keepdims=True)

    out = pl.BlockSpec((rows, tile), lambda i: (0, i))
    return pl.pallas_call(
        kernel,
        grid=(width // tile,),
        in_specs=[
            pl.BlockSpec((rows, query_width), lambda i: (0, 0)),
            pl.BlockSpec((rows, qkv_width - query_width), lambda i: (0, 0)),
            pl.BlockSpec((tile, qkv_width), lambda i: (i, 0)),
            out,
            pl.BlockSpec((rows, 1), lambda i: (0, 0)),
        ]
        + [ANYWHERE] * len(after),
        out_specs=[out, pl.BlockSpec((1, tile), lambda i: (0, i))],
        out_shape=[
            jax.ShapeDtypeStruct((rows, width), bf16),
            jax.ShapeDtypeStruct((1, width), f32),
        ],
        compiler_params=pltpu.CompilerParams(vmem_limit_bytes=40 * 2**20),
        cost_estimate=cost(8),
    )(d_query, d_keyval, weights, values, scale, *after)


def gain_block(d_attn, d_ffn, d_query, d_key, places, *after):
    width = d_attn.shape[1]

    def kernel(d_attn_ref, d_ffn_ref, d_query_ref, d_key_ref, places_ref, *refs):
        out_ref = refs[-1]
        out_ref[...] = jnp.zeros_like(out_ref)
        heads = jnp.sum(
            d_query_ref[...] * places_ref[:HD, :].astype(f32)
            + d_key_ref[...] * places_ref[HD:, :].astype(f32),
            axis=0,
            keepdims=True,
        )
        out_ref[0:1, :] = d_attn_ref[...].astype(bf16)
        out_ref[1:2, :] = d_ffn_ref[...].astype(bf16)
        out_ref[2:3, :] = heads.astype(bf16)

    return pl.pallas_call(
        kernel,
        in_specs=[pl.BlockSpec(memory_space=pltpu.VMEM)] * 5 + [ANYWHERE] * len(after),
        out_shape=jax.ShapeDtypeStruct((LANES, width), bf16),
        cost_estimate=cost(1),
    )(d_attn, d_ffn, d_query, d_key, places, *after)


def turned(array, *after):
    rows, columns = array.shape
    tile = math.gcd(columns, 512)

    def kernel(in_ref, *refs):
        refs[-1][...] = in_ref[...].astype(f32).T

    return pl.pallas_call(
        kernel,
        grid=(columns // tile,),
        in_specs=[pl.BlockSpec((rows, tile), lambda i: (0, i))] + [ANYWHERE] * len(after),
        out_specs=pl.BlockSpec((tile, rows), lambda i: (i, 0)),
        out_shape=jax.ShapeDtypeStruct((columns, rows), f32),
        cost_estimate=cost(2),
    )(array, *after)


def both_tensors(mine, theirs, tensor, width):
    rows = mine.shape[0]

    def kernel(tensor_ref, mine_ref, theirs_ref, out_ref, gains_ref):
        own = mine_ref[...].astype(f32)
        other = theirs_ref[...].astype(f32)
        first = tensor_ref[0] == 0
        low = jnp.where(first, own, other)
        high = jnp.where(first, other, own)
        out_ref[...] = jnp.concatenate(
            [low[:, :width], high[:, :width], low[:, width : 2 * width], high[:, width : 2 * width]],
            axis=1,
        )
        column = lax.broadcasted_iota(jnp.int32, (rows, LANES), 1)
        own_gains = own[:, 2 * width :]
        gains = own_gains + jnp.where(column == 1, 0.0, other[:, 2 * width :])
        gains_ref[...] = gains.T[:8, :]

    return pl.pallas_call(
        kernel,
        in_specs=[pl.BlockSpec(memory_space=pltpu.SMEM)]
        + [pl.BlockSpec(memory_space=pltpu.VMEM)] * 2,
        out_shape=[
            jax.ShapeDtypeStruct((rows, 4 * width), f32),
            jax.ShapeDtypeStruct((8, rows), f32),
        ],
        cost_estimate=cost(2),
    )(tensor.reshape(1).astype(jnp.int32), mine, theirs)


def side_by_side(first, second):
    rows, columns = first.shape
    step = math.gcd(rows, 32)

    def kernel(first_ref, second_ref, out_ref):
        out_ref[:, 0, :] = first_ref[...]
        out_ref[:, 1, :] = second_ref[...]

    return pl.pallas_call(
        kernel,
        grid=(rows // step,),
        in_specs=[pl.BlockSpec((step, columns), lambda i: (i, 0))] * 2,
        out_specs=pl.BlockSpec((step, 2, columns), lambda i: (i, 0, 0)),
        out_shape=jax.ShapeDtypeStruct((rows, 2, columns), first.dtype),
        cost_estimate=cost(4),
    )(first, second)


def attend_kernel(shift, q_ref, k_ref, v_ref, bias_ref, out_ref, inverse_ref):
    rows = q_ref.shape[1]
    for first in range(0, rows, TILE):
        at = slice(first, first + TILE)
        for head in range(GROUP):
            of = slice(head * HD, (head + 1) * HD)
            query = q_ref[of, at]
            total = jnp.zeros((HD + SUM_ROWS, TILE), f32)
            for start in range(first + shift, first + shift + WINDOW + TILE, TILE):
                near = slice(start, start + TILE)
                scores = nn_dot(k_ref[0, near, :], query)
                weight = jnp.exp2(scores * EXP2_SCALE + bias_ref[near, at]).astype(bf16)
                total = total + nn_dot(v_ref[0, :, near], weight)
            inverse = 1.0 / total[HD : HD + 1]
            out_ref[of, at] = (total[:HD] * inverse).astype(bf16)
            inverse_ref[0, head : head + 1, at] = inverse


def attend_back_kernel(shift, operands, *refs):
    q_ref, k_ref, kt_ref, v_ref, d_ref, o_ref, inverse_ref, bias_ref = refs[:8]
    dq_ref, dk_ref, dv_ref = refs[operands:]
    rows = q_ref.shape[1]
    dk_ref[...] = jnp.zeros_like(dk_ref)
    dv_ref[...] = jnp.zeros_like(dv_ref)
    for first in range(0, rows, TILE):
        at = slice(first, first + TILE)
        deltas = []
        for head in range(GROUP):
            of = slice(head * HD, (head + 1) * HD)
            product = d_ref[of, at].astype(f32) * o_ref[of, at].astype(f32)
            deltas.append(jnp.sum(product, axis=0, keepdims=True))
        d_query = [jnp.zeros((HD, TILE), f32) for _ in range(GROUP)]
        for start in range(first + shift, first + shift + WINDOW + TILE, TILE):
            near = slice(start, start + TILE)
            d_key = jnp.zeros((HD, TILE), f32)
            d_value = jnp.zeros((HD, TILE), f32)
            for head in range(GROUP):
                of = slice(head * HD, (head + 1) * HD)
                query = q_ref[of, at]
                d_out = d_ref[of, at]
                scores = nn_dot(k_ref[0, near, :], query)
                weight = jnp.exp2(scores * EXP2_SCALE + bias_ref[near, at])
                prob = weight * inverse_ref[0, head : head + 1, at]
                d_prob = nn_dot(v_ref[0, near, :], d_out)
                d_scores = (prob * (d_prob - deltas[head])).astype(bf16)
                d_query[head] = d_query[head] + nn_dot(kt_ref[:, near], d_scores)
                d_key = d_key + nt_dot(query, d_scores)
                d_value = d_value + nt_dot(d_out, prob.astype(bf16))
            dk_ref[:, near] += d_key
            dv_ref[:, near] += d_value
        for head in range(GROUP):
            dq_ref[head * HD : (head + 1) * HD, at] = d_query[head]


def attend(q_t, k, v_t, bias):
    kv, keys, _ = k.shape
    rows = q_t.shape[1]
    ones = jnp.ones((kv, SUM_ROWS, keys), bf16)
    v_ones = jnp.concatenate([v_t.reshape(kv, HD, keys), ones], axis=1)
    return pl.pallas_call(
        functools.partial(attend_kernel, keys - rows - WINDOW),
        grid=(kv,),
        in_specs=[
            pl.BlockSpec((GROUP * HD, rows), lambda h: (h, 0)),
            pl.BlockSpec((1, keys, HD), lambda h: (h, 0, 0)),
            pl.BlockSpec((1, HD + SUM_ROWS, keys), lambda h: (h, 0, 0)),
            pl.BlockSpec((keys, rows), lambda h: (0, 0)),
        ],
        out_specs=[
            pl.BlockSpec((GROUP * HD, rows), lambda h: (h, 0)),
            pl.BlockSpec((1, 8, rows), lambda h: (h, 0, 0)),
        ],
        out_shape=[jax.ShapeDtypeStruct((kv * GROUP * HD, rows), bf16), jax.ShapeDtypeStruct((kv, 8, rows), f32)],
        compiler_params=pltpu.CompilerParams(vmem_limit_bytes=40 * 2**20),
        cost_estimate=cost(13),
    )(q_t, k, v_ones, bias)


def attend_back(at, so_far, after, q_t, k, k_t, v, d_t, o_t, inverse, bias):
    kv, keys, _ = k.shape
    rows = q_t.shape[1]
    head_block = pl.BlockSpec((GROUP * HD, rows), lambda i: (at, 0))
    key_block = pl.BlockSpec((1, keys, HD), lambda i: (at, 0, 0))
    key_t_block = pl.BlockSpec((HD, keys), lambda i: (at, 0))
    waits = [*so_far, *after]
    operands = 8 + len(waits)
    return pl.pallas_call(
        functools.partial(attend_back_kernel, keys - rows - WINDOW, operands),
        grid=(1,),
        in_specs=[
            head_block,
            key_block,
            key_t_block,
            key_block,
            head_block,
            head_block,
            pl.BlockSpec((1, 8, rows), lambda i: (at, 0, 0)),
            pl.BlockSpec((keys, rows), lambda i: (0, 0)),
        ]
        + [pl.BlockSpec(memory_space=pl.ANY)] * len(waits),
        out_specs=[head_block, key_t_block, key_t_block],
        out_shape=[
            jax.ShapeDtypeStruct((kv * GROUP * HD, rows), f32),
            jax.ShapeDtypeStruct((kv * HD, keys), f32),
            jax.ShapeDtypeStruct((kv * HD, keys), f32),
        ],
        input_output_aliases={8 + i: i for i in range(len(so_far))},
        compiler_params=pltpu.CompilerParams(vmem_limit_bytes=40 * 2**20),
        cost_estimate=cost(11),
    )(q_t, k, k_t, v, d_t, o_t, inverse, bias, *waits)


def feed_kernel(n_ref, d_act_ref, gate_ref, up_ref, *refs):
    act_ref, d_gate_ref, d_up_ref = refs[-3:]
    normed = n_ref[...]
    gate = nn_dot(normed, gate_ref[...])
    up = nn_dot(normed, up_ref[...])
    sigmoid = 1.0 / (1.0 + jnp.exp(-gate))
    silu = gate * sigmoid
    act_ref[...] = (silu * up).astype(bf16)
    d_act = d_act_ref[...]
    d_gate_ref[...] = (d_act * up * sigmoid * (1.0 + gate * (1.0 - sigmoid))).astype(bf16)
    d_up_ref[...] = (d_act * silu).astype(bf16)


def feed(normed, d_act, gateup, *after):
    rows, width = normed.shape
    hidden = d_act.shape[1]
    tile = math.gcd(hidden, 512)
    steps = hidden // tile
    hidden_block = pl.BlockSpec((rows, tile), lambda i: (0, i))
    return pl.pallas_call(
        feed_kernel,
        grid=(steps,),
        in_specs=[
            pl.BlockSpec((rows, width), lambda i: (0, 0)),
            hidden_block,
            pl.BlockSpec((width, tile), lambda i: (0, i)),
            pl.BlockSpec((width, tile), lambda i: (0, i + steps)),
        ]
        + [ANYWHERE] * len(after),
        out_specs=[hidden_block] * 3,
        out_shape=[jax.ShapeDtypeStruct((rows, hidden), bf16)] * 3,
        compiler_params=pltpu.CompilerParams(vmem_limit_bytes=56 * 2**20),
        cost_estimate=cost(19.5),
    )(normed, d_act, gateup, gateup, *after)


def feed_back(d_gate, d_up, gateup, *after):
    rows, hidden = d_gate.shape
    width = gateup.shape[0]
    tile = math.gcd(width, 256)

    def kernel(d_gate_ref, d_up_ref, gate_ref, up_ref, *refs):
        total = nt_dot(d_gate_ref[...], gate_ref[...]) + nt_dot(d_up_ref[...], up_ref[...])
        refs[-1][...] = total.astype(bf16)

    whole = pl.BlockSpec((rows, hidden), lambda i: (0, 0))
    return pl.pallas_call(
        kernel,
        grid=(width // tile,),
        in_specs=[
            whole,
            whole,
            pl.BlockSpec((tile, hidden), lambda i: (i, 0)),
            pl.BlockSpec((tile, hidden), lambda i: (i, 1)),
        ]
        + [ANYWHERE] * len(after),
        out_specs=pl.BlockSpec((rows, tile), lambda i: (0, i)),
        out_shape=jax.ShapeDtypeStruct((rows, width), bf16),
        compiler_params=pltpu.CompilerParams(vmem_limit_bytes=56 * 2**20),
        cost_estimate=cost(17),
    )(d_gate, d_up, gateup, gateup, *after)


def feed_out(act, downs, down_start, *after):
    rows, hidden = act.shape
    width = downs.shape[0]
    tile = math.gcd(width, 256)
    step = math.gcd(math.gcd(hidden, down_start), 512)
    count = hidden // step

    def kernel(act_ref, *refs):
        total = jnp.zeros((rows, tile), f32)
        for at, ref in enumerate(refs[:count]):
            total = total + nt_dot(act_ref[:, at * step : (at + 1) * step], ref[...])
        refs[-1][...] = total.astype(bf16)

    return pl.pallas_call(
        kernel,
        grid=(width // tile,),
        in_specs=[pl.BlockSpec((rows, hidden), lambda i: (0, 0))]
        + [
            pl.BlockSpec((tile, step), functools.partial(lambda i, at: (i, at), at=at))
            for at in range(down_start // step, down_start // step + count)
        ]
        + [ANYWHERE] * len(after),
        out_specs=pl.BlockSpec((rows, tile), lambda i: (0, i)),
        out_shape=jax.ShapeDtypeStruct((rows, width), bf16),
        compiler_params=pltpu.CompilerParams(vmem_limit_bytes=56 * 2**20),
        cost_estimate=cost(9),
    )(act, *[downs] * count, *after)


def shards(
    tokens,
    w_query,
    w_keyval,
    w_out,
    w_gateup,
    w_down,
    attn_gain,
    ffn_gain,
    qk_gain,
    segments,
    positions,
    cotangent,
):
    ring = Ring()
    row_count = tokens.shape[0]
    depth = w_query.shape[0]
    model = tokens.shape[1]
    hidden = w_gateup.shape[2]
    tensor = lax.axis_index("tensor")
    query_width = w_query.shape[1]
    local_heads = query_width // HD
    local_kv = local_heads // GROUP
    kv_width = local_kv * HD
    all_kv = w_keyval.shape[1] // 2
    qkv_width = query_width + 2 * kv_width
    gain_count = 2 * qk_gain.shape[1]

    own_keyval = lax.dynamic_index_in_dim(
        w_keyval.reshape(depth, 2, all_kv // kv_width, kv_width), tensor, 2, keepdims=False
    ).reshape(depth, 2 * kv_width)
    head_gain_column = jnp.pad(qk_gain.reshape(gain_count), (0, depth - gain_count))
    gains = jnp.stack([attn_gain, ffn_gain, head_gain_column], axis=1)
    gains = jnp.pad(gains, ((0, 0), (0, LANES - gains.shape[1])))
    first_pack = jnp.concatenate([w_query, own_keyval, w_out.T, gains, w_down.T], axis=1)
    first_full = lax.all_gather(first_pack.astype(bf16), "dp", axis=0, tiled=True)
    gateup_full = lax.all_gather(
        w_gateup.reshape(depth, 2 * hidden).astype(bf16), "dp", axis=0, tiled=True
    )
    qkv_full = first_full[:, :qkv_width]
    gain_start = qkv_width + query_width
    out_full = first_full[:, qkv_width:gain_start]
    down_full = first_full[:, gain_start + LANES :]
    gain_columns = first_full[:, gain_start : gain_start + 3].astype(f32)
    attn_weight = gain_columns[:, 0]
    ffn_weight = gain_columns[:, 1]
    head_gains = gain_columns[:, 2].reshape(ring.count, depth)[:, :gain_count]
    head_gains = head_gains.reshape(ring.count, 2, qk_gain.shape[1]).transpose(1, 0, 2).reshape(2, HD)
    gain_query = head_gains[0][:, None]
    gain_key = head_gains[1][:, None]

    marks = (segments + 1).astype(bf16)
    seq_devices = min(SEQ_LEN // row_count, ring.count)
    own_sequence = ring.index // seq_devices
    reach_count = -(-WINDOW // row_count)
    halo_marks = []
    for step_back in range(reach_count, 0, -1):
        same_sequence = ((ring.index - step_back) // seq_devices == own_sequence).astype(bf16)
        halo_marks.append(from_behind(marks, step_back) * same_sequence)
    key_marks = jnp.concatenate(halo_marks + [marks], axis=0)
    key_count = key_marks.shape[0]
    distance = (jnp.arange(row_count, dtype=jnp.int32) + reach_count * row_count)[
        None, :
    ] - jnp.arange(key_count, dtype=jnp.int32)[:, None]
    allowed = (distance >= 0) & (distance < WINDOW) & (key_marks[:, None] == marks[None, :])
    bias = jnp.where(allowed, 0.0, MASKED).astype(f32)
    cos_table, sin_table = angles_of(positions)

    residual = tokens.astype(f32)
    attn_scale = inverse_rms(residual, 1)

    normed_low = (residual * attn_scale * attn_weight).astype(bf16)
    qkv_raw = lax.dot_general(
        qkv_full, normed_low, (((0,), (1,)), ((), ())), preferred_element_type=f32
    )
    query_raw = qkv_raw[:query_width].reshape(local_heads, HD, row_count)
    key_raw = qkv_raw[query_width : query_width + kv_width].reshape(local_kv, HD, row_count)
    query_scale = inverse_rms(query_raw, 1)
    key_scale = inverse_rms(key_raw, 1)
    query_low = rotate(query_raw * query_scale * gain_query, cos_table, sin_table).astype(bf16)
    key_low = rotate(key_raw * key_scale * gain_key, cos_table, sin_table).astype(bf16)
    query_low = query_low.reshape(query_width, row_count)
    keyval_low = jnp.concatenate(
        [key_low.reshape(kv_width, row_count), qkv_raw[query_width + kv_width :].astype(bf16)], axis=0
    )
    halo = [from_behind(keyval_low, step_back) for step_back in range(reach_count, 0, -1)]
    key_keyval = jnp.concatenate(halo + [keyval_low], axis=1)
    keys_t = key_keyval[:kv_width]
    values_t = key_keyval[kv_width:]
    keys = keys_t.reshape(local_kv, HD, key_count).transpose(0, 2, 1)
    values = values_t.reshape(local_kv, HD, key_count).transpose(0, 2, 1)
    attended, inverse_total = attend(query_low, keys, values_t, bias)
    mid_part = lax.dot_general(
        attended, out_full, (((0,), (1,)), ((), ())), preferred_element_type=f32
    )
    near_first = ring.bits
    normed_rows = ring.chosen(normed_low, near_first)
    cotangent_rows = transposed(cotangent)
    attended_back = attended.T
    mid = residual + tensor_sum(
        mid_part, corner(normed_rows), corner(cotangent_rows), corner(attended_back)
    )

    d_act = nn_dot(cotangent, down_full)
    ffn_scale = inverse_rms(mid, 1)
    normed2_low = (mid * ffn_scale * ffn_weight).astype(bf16)
    normed2_rows = ring.chosen(normed2_low, near_first)
    act_low, d_gate, d_up = feed(normed2_low, d_act, gateup_full, normed2_rows)
    gate_sum = Scatter(ring, normed2_rows, d_gate, near_first)
    up_sum = Scatter(ring, normed2_rows, d_up, near_first)
    sums = {"G": gate_sum, "U": up_sum}
    totals = {}
    heads = 0
    grads = ()
    down_low = None
    before = None
    for step in ORDER:
        after = () if before is None else (before,)
        if step in sums:
            one = sums[step]
            if len(one.got) < len(one.bits) and step not in totals:
                before = one.send(*after, parts=PARTS if step in "OQK" and not one.got else 1)
                if len(one.got) == 4:
                    while len(one.got) < len(one.bits):
                        before = one.send(before)
            else:
                before = totals[step] = one.total(*after, transposed=step == "O")
        elif step == "D":
            if down_low is None:
                before = product(cotangent_rows, act_low, model, 0, [], after)[0]
                down_low = lax.psum_scatter(before, "dp", scatter_dimension=0, tiled=True)
            else:
                before = totals["D"] = turned(down_low, *after)
        elif step == "FB":
            before = d_normed2_low = feed_back(d_gate, d_up, gateup_full, *after)
            d_normed2_other = other_tensor(d_normed2_low)
        elif step == "FO":
            before = result_low = feed_out(act_low, first_full, gain_start + LANES, *after)
        elif step == "NB":
            d_mid, d_mid_low, d_ffn_weight = norm_back(
                mid, cotangent, d_normed2_low, d_normed2_other, ffn_weight, *after
            )
            before = d_mid_low
            result_other = other_tensor(tie(result_low, d_normed2_other))
        elif step == "DA":
            before = d_attended = product_tt(first_full, qkv_width, query_width, d_mid_low)
        elif step == "H":
            grads = attend_back(
                heads,
                grads,
                after,
                query_low,
                keys,
                keys_t,
                values,
                d_attended,
                attended,
                inverse_total,
                bias,
            )
            heads += 1
            d_query, d_keys, d_values = grads
            before = d_keys
        elif step == "HP":
            halo_grads = halo_parts(d_keys, d_values, row_count, *after)
            got = [from_behind(part, at - reach_count) for at, part in enumerate(halo_grads)]
            before = halo_grads[0]
        elif step == "QB":
            d_query_low, d_gain_query = query_back(
                d_query, qkv_raw, cos_table[0], sin_table[0], gain_query, *after
            )
            before = d_query_low
            sums["Q"] = Scatter(ring, normed_rows, d_query_low, near_first)
        elif step == "OP":
            before = d_mid_rows = ring.chosen(tie(d_mid_low, *after), near_first)
            sums["O"] = Scatter(ring, d_mid_rows, attended_back, near_first)
        elif step == "KB":
            d_keyval_low, d_gain_key = key_back(
                d_keys,
                d_values,
                got,
                qkv_raw,
                query_width,
                cos_table[0],
                sin_table[0],
                gain_key,
                *after,
            )
            before = d_keyval_low
        elif step == "IB":
            d_normed_low, d_attn_part = input_back(
                d_query_low, d_keyval_low, first_full, tokens, attn_scale, *after
            )
            d_normed_other = other_tensor(d_normed_low)
            before = d_normed_low
        elif step == "GB":
            places = jnp.arange(2 * HD, dtype=jnp.int32)
            per_device = gain_count // 2
            places = (
                places % HD // per_device * depth
                + places // HD * per_device
                + places % per_device
            )
            places = (places[:, None] == jnp.arange(model, dtype=jnp.int32)[None, :]).astype(bf16)
            gain_grads = gain_block(
                d_attn_part, d_ffn_weight, d_gain_query, d_gain_key, places, *after
            )
            before = gain_rows = ring.chosen(gain_grads, near_first)
            sums["K"] = Scatter(ring, normed_rows, d_keyval_low, near_first, gain_rows)
        elif step == "AD":
            before = output = add_up(mid, result_low, result_other, *after)
        elif step == "IG":
            _, input_grad, _ = norm_back(
                tokens, d_mid, d_normed_low, d_normed_other, attn_weight, *after
            )
            before = input_grad
    grad_down, grad_out, grad_query = totals["D"], totals["O"], totals["Q"]
    grad_gateup = side_by_side(totals["G"], totals["U"])
    shared = totals["K"].astype(bf16)
    grad_keyval, gains_t = both_tensors(shared, other_tensor(shared), tensor, kv_width)
    grad_attn_gain = gains_t[0]
    grad_ffn_gain = gains_t[1]
    grad_heads = gains_t[2, :gain_count].reshape(2, gain_count // 2)
    return (
        output,
        input_grad,
        grad_query,
        grad_keyval,
        grad_out,
        grad_gateup,
        grad_down,
        grad_attn_gain,
        grad_ffn_gain,
        grad_heads,
    )


def solution(mesh):
    in_specs = (
        P("dp", None),
        P("dp", "tensor"),
        P("dp", None),
        P("tensor", "dp"),
        P("dp", None, "tensor"),
        P("tensor", "dp"),
        P("dp"),
        P("dp"),
        P(None, "dp"),
        P("dp"),
        P("dp"),
        P("dp", None),
    )
    out_specs = (
        P("dp", None),
        P("dp", None),
        P("dp", "tensor"),
        P("dp", None),
        P("tensor", "dp"),
        P("dp", None, "tensor"),
        P("tensor", "dp"),
        P("dp"),
        P("dp"),
        P(None, "dp"),
    )
    return jax.shard_map(shards, mesh=mesh, in_specs=in_specs, out_specs=out_specs, check_vma=False)
```

```python
import functools
import math

import jax
import jax.numpy as jnp
from jax import lax
from jax.experimental import pallas as pl
from jax.experimental.pallas import tpu as pltpu
from jax.sharding import PartitionSpec as P

QH = 24
KVH = 6
HD = 64
GROUP = QH // KVH
WINDOW = 1024
SEQ_LEN = 8192
LANES = 128

EPSILON = 1e-06
SCORE_SCALE = 0.125
MASKED = -1e30
ROPE_BASE = 10000.0
EXP2_SCALE = SCORE_SCALE * math.log2(math.e)
TILE = 256
SUM_ROWS = 16
PARTS = 4
ORDER = (
    "G", "D", "FB", "U", "G", "FO", "U", "NB", "DA", "H", "H", "G",
    "H", "HP", "QB", "Q", "OP", "O", "G", "Q", "O", "KB", "U", "IB",
    "G", "Q", "O", "GB", "K", "K", "U", "Q", "O", "K", "IG", "K",
    "AD", "D", "U", "Q", "O", "K",
)
LINK_SHARE = 0.35

bf16 = jnp.bfloat16
f32 = jnp.float32
ANYWHERE = pl.BlockSpec(memory_space=pl.ANY)


def cost(microseconds):
    return pl.CostEstimate(
        flops=int(microseconds * LINK_SHARE * 1.15e9), bytes_accessed=0, transcendentals=0
    )


def angles_of(positions):
    half_width = HD // 2
    frequency = jnp.exp(
        jnp.arange(half_width, dtype=f32) * (-math.log(ROPE_BASE) / half_width)
    )
    phases = frequency[:, None] * positions.astype(f32)[None, :]
    return jnp.cos(phases)[None], jnp.sin(phases)[None]


def rotate(values, cos_table, sin_table):
    half_width = values.shape[1] // 2
    first_half = values[:, :half_width]
    second_half = values[:, half_width:]
    return jnp.concatenate(
        [
            first_half * cos_table - second_half * sin_table,
            second_half * cos_table + first_half * sin_table,
        ],
        axis=1,
    )


def inverse_rms(values, axis):
    return lax.rsqrt(jnp.mean(values * values, axis=axis, keepdims=True) + EPSILON)


def rms_back(values, scale, weight, d_out, axis):
    weighted = d_out * weight
    pull = jnp.mean(weighted * values, axis=axis, keepdims=True)
    return scale * weighted - values * (scale * scale * scale * pull)


class Ring:
    def __init__(self):
        self.count = lax.axis_size("dp")
        self.index = lax.axis_index("dp")
        self.bits = [1 << at for at in range(self.count.bit_length() - 1)]

    def order(self, bits):
        order = []
        for at in range(self.count - 1, -1, -1):
            flips = sum(bit for place, bit in enumerate(reversed(bits)) if at >> place & 1)
            order.append(self.index ^ flips)
        return jnp.stack(order).astype(jnp.int32)

    def chosen(self, array, bits):
        depth = array.shape[1] // self.count
        if depth % LANES:
            blocks = array.T.reshape(self.count, depth, array.shape[0])
            return jnp.take(blocks, self.order(bits), axis=0).reshape(array.shape[1], array.shape[0])
        return transposed_blocks(self.order(bits), array, depth)


class Scatter:
    def __init__(self, ring, left, right, bits, tail=None):
        self.ring, self.left, self.right, self.bits, self.tail = ring, left, right, bits, tail
        self.got = []

    def rows(self):
        step = len(self.got)
        last = step == len(self.bits)
        size = self.left.shape[0] >> (step if last else step + 1)
        start = self.left.shape[0] - (self.left.shape[0] >> step)
        adds = []
        for at, parts in enumerate(self.got):
            first = start - self.left.shape[0] + (self.left.shape[0] >> at + 1)
            height = parts[0].shape[0]
            if height >= size:
                adds.append([(parts[first // height], first % height // size)])
            else:
                adds.append([(part, 0) for part in parts[first // height : (first + size) // height]])
        return size, start // size, adds

    def send(self, *after, parts=1):
        size, block, adds = self.rows()
        sent = product(
            self.left, self.right, size, block, adds, after, self.tail, parts=parts
        )
        bit = self.bits[len(self.got)]
        pairs = [(i, i ^ bit) for i in range(self.ring.count)]
        self.got.append([lax.ppermute(part, "dp", pairs) for part in sent])
        return sent[0]

    def total(self, *after, transposed=False):
        while len(self.got) < len(self.bits):
            after = (self.send(*after),)
        size, block, adds = self.rows()
        return product(self.left, self.right, size, block, adds, after, self.tail, f32, transposed)[0]


def other_tensor(array):
    count = lax.axis_size("tensor")
    return lax.ppermute(array, "tensor", [(i, (i + 1) % count) for i in range(count)])


def tensor_sum(partial, *before):
    low = partial.astype(bf16)
    other = other_tensor(low)
    if before:
        other = tie(other, *before)
    return low.astype(f32) + other.astype(f32)


def from_behind(shard, by):
    length = lax.axis_size("dp")
    pairs = [(i, i + by) for i in range(length) if 0 <= i + by < length]
    return lax.ppermute(shard, "dp", pairs)


def tn_dot(left, right):
    return lax.dot_general(left, right, (((0,), (0,)), ((), ())), preferred_element_type=f32)


def nt_dot(left, right):
    return lax.dot_general(left, right, (((1,), (1,)), ((), ())), preferred_element_type=f32)


def nn_dot(left, right):
    return jnp.dot(left, right, preferred_element_type=f32)


def tie(array, *others):
    def kernel(*refs):
        del refs

    return pl.pallas_call(
        kernel,
        in_specs=[pl.BlockSpec(memory_space=pl.ANY)] * (1 + len(others)),
        out_specs=pl.BlockSpec(memory_space=pl.ANY),
        out_shape=jax.ShapeDtypeStruct(array.shape, array.dtype),
        input_output_aliases={0: 0},
        cost_estimate=cost(0),
    )(array, *others)


def corner(array):
    return array[: 2 * 8, :LANES]


def transposed(array, *after):
    tokens, width = array.shape
    step = math.gcd(tokens, LANES)

    def kernel(in_ref, *refs):
        refs[-1][...] = in_ref[...].T

    return pl.pallas_call(
        kernel,
        grid=(tokens // step,),
        in_specs=[pl.BlockSpec((step, width), lambda i: (i, 0))] + [ANYWHERE] * len(after),
        out_specs=pl.BlockSpec((width, step), lambda i: (0, i)),
        out_shape=jax.ShapeDtypeStruct((width, tokens), array.dtype),
        cost_estimate=cost(4.8),
    )(array, *after)


def transposed_blocks(order, array, depth):
    tokens, width = array.shape
    step = math.gcd(tokens, LANES)

    def kernel(order_ref, in_ref, out_ref):
        for at in range(width // depth):
            column = pl.multiple_of(order_ref[at] * depth, depth)
            out_ref[at * depth : (at + 1) * depth, :] = in_ref[:, pl.ds(column, depth)].T

    return pl.pallas_call(
        kernel,
        grid_spec=pltpu.PrefetchScalarGridSpec(
            num_scalar_prefetch=1,
            grid=(tokens // step,),
            in_specs=[pl.BlockSpec((step, width), lambda i, order: (i, 0))],
            out_specs=pl.BlockSpec((width, step), lambda i, order: (0, i)),
        ),
        out_shape=jax.ShapeDtypeStruct((width, tokens), array.dtype),
        cost_estimate=cost(4.8),
    )(order, array)


def product(
    left, right, size, block, adds, after=(), tail=None, out_type=bf16, transposed=False, parts=1
):
    depth, columns = right.shape
    most = max(LANES, min(columns, 512 * 1024 // size))
    tile = max(t for t in range(LANES, most + 1, LANES) if columns % t == 0)
    if tail is not None:
        tile = LANES
    steps = columns // tile
    flat = [(array, row, size // len(add)) for add in adds for array, row in add]

    def kernel(left_ref, right_ref, *refs):
        def put(total):
            at = 0
            for add in adds:
                pieces = [ref[...].astype(f32) for ref in refs[at : at + len(add)]]
                total = total + (pieces[0] if len(add) == 1 else jnp.concatenate(pieces, axis=0))
                at += len(add)
            total = (total.T if transposed else total).astype(out_type)
            height = total.shape[0] // parts
            for at, ref in enumerate(refs[len(refs) - parts :]):
                ref[...] = total[at * height : (at + 1) * height]

        if tail is None:
            put(nn_dot(left_ref[...], right_ref[...]))
            return

        @pl.when(pl.program_id(0) < steps)
        def _():
            put(nn_dot(left_ref[...], right_ref[...]))

        @pl.when(pl.program_id(0) == steps)
        def _():
            put(refs[len(flat)][...].astype(f32))

    all_columns = columns
    in_specs = [
        pl.BlockSpec((size, depth), lambda i: (block, 0)),
        pl.BlockSpec((depth, tile), lambda i: (0, jnp.minimum(i, steps - 1))),
    ] + [
        pl.BlockSpec((height, tile), functools.partial(lambda i, row: (row, i), row=row))
        for _, row, height in flat
    ]
    operands = [left, right, *[array for array, _, _ in flat]]
    if tail is not None:
        all_columns += LANES
        in_specs.append(pl.BlockSpec((size, LANES), lambda i: (block, 0)))
        operands.append(tail)
    height = size // parts
    out_shape, out_block, out_map = (height, all_columns), (height, tile), lambda i: (0, i)
    if transposed:
        out_shape, out_block, out_map = (all_columns, height), (tile, height), lambda i: (i, 0)
    return pl.pallas_call(
        kernel,
        grid=(all_columns // tile,),
        in_specs=in_specs + [ANYWHERE] * len(after),
        out_specs=[pl.BlockSpec(out_block, out_map)] * parts,
        out_shape=[jax.ShapeDtypeStruct(out_shape, out_type)] * parts,
        compiler_params=pltpu.CompilerParams(vmem_limit_bytes=40 * 2**20),
        cost_estimate=cost(2 + 2 * size * depth * columns / 0.9e9),
    )(*operands, *after)


def product_tt(left, first, columns, right):
    depth = left.shape[0]
    rows = right.shape[0]
    tile = max(t for t in range(LANES, 384 + 1, LANES) if columns % t == 0 and first % t == 0)

    def kernel(left_ref, right_ref, out_ref):
        out_ref[...] = nt_dot(left_ref[...].T, right_ref[...]).astype(bf16)

    return pl.pallas_call(
        kernel,
        grid=(columns // tile,),
        in_specs=[
            pl.BlockSpec((depth, tile), lambda i: (0, i + first // tile)),
            pl.BlockSpec((rows, depth), lambda i: (0, 0)),
        ],
        out_specs=pl.BlockSpec((tile, rows), lambda i: (i, 0)),
        out_shape=jax.ShapeDtypeStruct((columns, rows), bf16),
        compiler_params=pltpu.CompilerParams(vmem_limit_bytes=40 * 2**20),
        cost_estimate=cost(4.3),
    )(left, right)


def norm_back(values, direct, part, other, gain, *after):
    rows, width = values.shape
    step = math.gcd(rows, 128)

    def kernel(values_ref, direct_ref, part_ref, other_ref, gain_ref, *refs):
        out_ref, low_ref, gain_out_ref = refs[len(after) :]
        value = values_ref[...].astype(f32)
        scale = inverse_rms(value, 1)
        d_out = part_ref[...].astype(f32) + other_ref[...].astype(f32)
        result = direct_ref[...].astype(f32) + rms_back(value, scale, gain_ref[...], d_out, 1)
        out_ref[...] = result
        low_ref[...] = result.astype(bf16)

        @pl.when(pl.program_id(0) == 0)
        def _():
            gain_out_ref[...] = jnp.zeros_like(gain_out_ref)

        gain_out_ref[...] += jnp.sum(d_out * value * scale, axis=0, keepdims=True)

    block = pl.BlockSpec((step, width), lambda i: (i, 0))
    row = pl.BlockSpec((1, width), lambda i: (0, 0))
    return pl.pallas_call(
        kernel,
        grid=(rows // step,),
        in_specs=[block] * 4 + [row] + [ANYWHERE] * len(after),
        out_specs=[block, block, row],
        out_shape=[
            jax.ShapeDtypeStruct((rows, width), f32),
            jax.ShapeDtypeStruct((rows, width), bf16),
            jax.ShapeDtypeStruct((1, width), f32),
        ],
        compiler_params=pltpu.CompilerParams(vmem_limit_bytes=40 * 2**20),
        cost_estimate=cost(7),
    )(values, direct, part, other, gain[None, :], *after)


def add_up(values, part, other, *after):
    rows, width = values.shape
    step = math.gcd(rows, 128)

    def kernel(values_ref, part_ref, other_ref, *refs):
        added = part_ref[...].astype(f32) + other_ref[...].astype(f32)
        refs[-1][...] = (values_ref[...] + added).astype(bf16)

    block = pl.BlockSpec((step, width), lambda i: (i, 0))
    return pl.pallas_call(
        kernel,
        grid=(rows // step,),
        in_specs=[block] * 3 + [ANYWHERE] * len(after),
        out_specs=block,
        out_shape=jax.ShapeDtypeStruct((rows, width), bf16),
        cost_estimate=cost(3),
    )(values, part, other, *after)


def turn_back(d_rotated, raw, cos_table, sin_table, gain):
    half_width = HD // 2
    first, second = d_rotated[:half_width], d_rotated[half_width:]
    d_normed = jnp.concatenate(
        [first * cos_table + second * sin_table, second * cos_table - first * sin_table], axis=0
    )
    scale = inverse_rms(raw, 0)
    return rms_back(raw, scale, gain, d_normed, 0), d_normed * raw * scale


def query_back(d_query, raw, cos_table, sin_table, gain, *after):
    width, rows = d_query.shape
    step = GROUP * HD

    def kernel(d_ref, raw_ref, cos_ref, sin_ref, gain_ref, *refs):
        out_ref, gain_out_ref = refs[len(after) :]
        results = []
        d_gain = jnp.zeros((HD, rows), f32)
        for head in range(GROUP):
            of = slice(head * HD, (head + 1) * HD)
            result, by_token = turn_back(
                d_ref[of, :] * SCORE_SCALE, raw_ref[of, :], cos_ref[...], sin_ref[...], gain_ref[...]
            )
            results.append(result)
            d_gain = d_gain + by_token
        out_ref[...] = jnp.concatenate(results, axis=0).astype(bf16).T

        @pl.when(pl.program_id(0) == 0)
        def _():
            gain_out_ref[...] = jnp.zeros_like(gain_out_ref)

        gain_out_ref[...] += jnp.sum(d_gain, axis=1, keepdims=True)

    block = pl.BlockSpec((step, rows), lambda i: (i, 0))
    table = pl.BlockSpec((HD // 2, rows), lambda i: (0, 0))
    column = pl.BlockSpec((HD, 1), lambda i: (0, 0))
    return pl.pallas_call(
        kernel,
        grid=(width // step,),
        in_specs=[block, block, table, table, column] + [ANYWHERE] * len(after),
        out_specs=[pl.BlockSpec((rows, step), lambda i: (0, i)), column],
        out_shape=[
            jax.ShapeDtypeStruct((rows, width), bf16),
            jax.ShapeDtypeStruct((HD, 1), f32),
        ],
        compiler_params=pltpu.CompilerParams(vmem_limit_bytes=40 * 2**20),
        cost_estimate=cost(1.6),
    )(d_query, raw, cos_table, sin_table, gain, *after)


def halo_parts(d_keys, d_values, rows, *after):
    width, count = d_keys.shape
    parts = count // rows - 1

    def kernel(d_keys_ref, d_values_ref, *refs):
        for at, ref in enumerate(refs[len(after) :]):
            of = slice(at * rows, (at + 1) * rows)
            ref[:width, :] = d_keys_ref[:, of].astype(bf16)
            ref[width:, :] = d_values_ref[:, of].astype(bf16)

    whole = pl.BlockSpec((width, count), lambda i: (0, 0))
    return pl.pallas_call(
        kernel,
        grid=(1,),
        in_specs=[whole, whole] + [ANYWHERE] * len(after),
        out_specs=[pl.BlockSpec((2 * width, rows), lambda i: (0, 0))] * parts,
        out_shape=[jax.ShapeDtypeStruct((2 * width, rows), bf16)] * parts,
        compiler_params=pltpu.CompilerParams(vmem_limit_bytes=40 * 2**20),
        cost_estimate=cost(1),
    )(d_keys, d_values, *after)


def key_back(d_keys, d_values, got, raw, first, cos_table, sin_table, gain, *after):
    width, count = d_keys.shape
    rows = got[0].shape[1]
    own = pl.BlockSpec((width, rows), lambda i: (0, count // rows - 1))
    heads = width // HD

    def kernel(d_keys_ref, d_values_ref, raw_ref, cos_ref, sin_ref, gain_ref, *refs):
        out_ref, gain_out_ref = refs[len(got) + len(after) :]
        d_key = d_keys_ref[...]
        d_value = d_values_ref[...]
        for ref in refs[: len(got)]:
            d_key = d_key + ref[:width, :].astype(f32)
            d_value = d_value + ref[width:, :].astype(f32)
        results = []
        d_gain = jnp.zeros((HD, rows), f32)
        for head in range(heads):
            of = slice(head * HD, (head + 1) * HD)
            result, by_token = turn_back(
                d_key[of] * SCORE_SCALE, raw_ref[of, :], cos_ref[...], sin_ref[...], gain_ref[...]
            )
            results.append(result)
            d_gain = d_gain + by_token
        out_ref[...] = jnp.concatenate(results + [d_value], axis=0).astype(bf16).T
        gain_out_ref[...] = jnp.sum(d_gain, axis=1, keepdims=True)

    table = pl.BlockSpec((HD // 2, rows), lambda i: (0, 0))
    column = pl.BlockSpec((HD, 1), lambda i: (0, 0))
    return pl.pallas_call(
        kernel,
        grid=(1,),
        in_specs=[
            own,
            own,
            pl.BlockSpec((width, rows), lambda i: (first // width, 0)),
            table,
            table,
            column,
        ]
        + [pl.BlockSpec((2 * width, rows), lambda i: (0, 0))] * len(got)
        + [ANYWHERE] * len(after),
        out_specs=[pl.BlockSpec((rows, 2 * width), lambda i: (0, 0)), column],
        out_shape=[
            jax.ShapeDtypeStruct((rows, 2 * width), bf16),
            jax.ShapeDtypeStruct((HD, 1), f32),
        ],
        compiler_params=pltpu.CompilerParams(vmem_limit_bytes=40 * 2**20),
        cost_estimate=cost(1.6),
    )(d_keys, d_values, raw, cos_table, sin_table, gain, *got, *after)


def input_back(d_query, d_keyval, weights, values, scale, *after):
    rows, query_width = d_query.shape
    qkv_width = query_width + d_keyval.shape[1]
    width = weights.shape[0]
    tile = math.gcd(width, 256)

    def kernel(d_query_ref, d_keyval_ref, weights_ref, values_ref, scale_ref, *refs):
        out_ref, gain_out_ref = refs[len(after) :]
        part = nt_dot(d_query_ref[...], weights_ref[:, :query_width]) + nt_dot(
            d_keyval_ref[...], weights_ref[:, query_width:]
        )
        out_ref[...] = part.astype(bf16)
        product_sum = part * values_ref[...].astype(f32) * scale_ref[...]
        gain_out_ref[...] = jnp.sum(product_sum, axis=0, keepdims=True)

    out = pl.BlockSpec((rows, tile), lambda i: (0, i))
    return pl.pallas_call(
        kernel,
        grid=(width // tile,),
        in_specs=[
            pl.BlockSpec((rows, query_width), lambda i: (0, 0)),
            pl.BlockSpec((rows, qkv_width - query_width), lambda i: (0, 0)),
            pl.BlockSpec((tile, qkv_width), lambda i: (i, 0)),
            out,
            pl.BlockSpec((rows, 1), lambda i: (0, 0)),
        ]
        + [ANYWHERE] * len(after),
        out_specs=[out, pl.BlockSpec((1, tile), lambda i: (0, i))],
        out_shape=[
            jax.ShapeDtypeStruct((rows, width), bf16),
            jax.ShapeDtypeStruct((1, width), f32),
        ],
        compiler_params=pltpu.CompilerParams(vmem_limit_bytes=40 * 2**20),
        cost_estimate=cost(8),
    )(d_query, d_keyval, weights, values, scale, *after)


def gain_block(d_attn, d_ffn, d_query, d_key, places, *after):
    width = d_attn.shape[1]

    def kernel(d_attn_ref, d_ffn_ref, d_query_ref, d_key_ref, places_ref, *refs):
        out_ref = refs[-1]
        out_ref[...] = jnp.zeros_like(out_ref)
        heads = jnp.sum(
            d_query_ref[...] * places_ref[:HD, :].astype(f32)
            + d_key_ref[...] * places_ref[HD:, :].astype(f32),
            axis=0,
            keepdims=True,
        )
        out_ref[0:1, :] = d_attn_ref[...].astype(bf16)
        out_ref[1:2, :] = d_ffn_ref[...].astype(bf16)
        out_ref[2:3, :] = heads.astype(bf16)

    return pl.pallas_call(
        kernel,
        in_specs=[pl.BlockSpec(memory_space=pltpu.VMEM)] * 5 + [ANYWHERE] * len(after),
        out_shape=jax.ShapeDtypeStruct((LANES, width), bf16),
        cost_estimate=cost(1),
    )(d_attn, d_ffn, d_query, d_key, places, *after)


def turned(array, *after):
    rows, columns = array.shape
    tile = math.gcd(columns, 512)

    def kernel(in_ref, *refs):
        refs[-1][...] = in_ref[...].astype(f32).T

    return pl.pallas_call(
        kernel,
        grid=(columns // tile,),
        in_specs=[pl.BlockSpec((rows, tile), lambda i: (0, i))] + [ANYWHERE] * len(after),
        out_specs=pl.BlockSpec((tile, rows), lambda i: (i, 0)),
        out_shape=jax.ShapeDtypeStruct((columns, rows), f32),
        cost_estimate=cost(2),
    )(array, *after)


def both_tensors(mine, theirs, tensor, width):
    rows = mine.shape[0]

    def kernel(tensor_ref, mine_ref, theirs_ref, out_ref, gains_ref):
        own = mine_ref[...].astype(f32)
        other = theirs_ref[...].astype(f32)
        first = tensor_ref[0] == 0
        low = jnp.where(first, own, other)
        high = jnp.where(first, other, own)
        out_ref[...] = jnp.concatenate(
            [low[:, :width], high[:, :width], low[:, width : 2 * width], high[:, width : 2 * width]],
            axis=1,
        )
        column = lax.broadcasted_iota(jnp.int32, (rows, LANES), 1)
        own_gains = own[:, 2 * width :]
        gains = own_gains + jnp.where(column == 1, 0.0, other[:, 2 * width :])
        gains_ref[...] = gains.T[:8, :]

    return pl.pallas_call(
        kernel,
        in_specs=[pl.BlockSpec(memory_space=pltpu.SMEM)]
        + [pl.BlockSpec(memory_space=pltpu.VMEM)] * 2,
        out_shape=[
            jax.ShapeDtypeStruct((rows, 4 * width), f32),
            jax.ShapeDtypeStruct((8, rows), f32),
        ],
        cost_estimate=cost(2),
    )(tensor.reshape(1).astype(jnp.int32), mine, theirs)


def side_by_side(first, second):
    rows, columns = first.shape
    step = math.gcd(rows, 32)

    def kernel(first_ref, second_ref, out_ref):
        out_ref[:, 0, :] = first_ref[...]
        out_ref[:, 1, :] = second_ref[...]

    return pl.pallas_call(
        kernel,
        grid=(rows // step,),
        in_specs=[pl.BlockSpec((step, columns), lambda i: (i, 0))] * 2,
        out_specs=pl.BlockSpec((step, 2, columns), lambda i: (i, 0, 0)),
        out_shape=jax.ShapeDtypeStruct((rows, 2, columns), first.dtype),
        cost_estimate=cost(4),
    )(first, second)


def attend_kernel(shift, q_ref, k_ref, v_ref, bias_ref, out_ref, inverse_ref):
    rows = q_ref.shape[1]
    for first in range(0, rows, TILE):
        at = slice(first, first + TILE)
        for head in range(GROUP):
            of = slice(head * HD, (head + 1) * HD)
            query = q_ref[of, at]
            total = jnp.zeros((HD + SUM_ROWS, TILE), f32)
            for start in range(first + shift, first + shift + WINDOW + TILE, TILE):
                near = slice(start, start + TILE)
                scores = nn_dot(k_ref[0, near, :], query)
                weight = jnp.exp2(scores * EXP2_SCALE + bias_ref[near, at]).astype(bf16)
                total = total + nn_dot(v_ref[0, :, near], weight)
            inverse = 1.0 / total[HD : HD + 1]
            out_ref[of, at] = (total[:HD] * inverse).astype(bf16)
            inverse_ref[0, head : head + 1, at] = inverse


def attend_back_kernel(shift, operands, *refs):
    q_ref, k_ref, kt_ref, v_ref, d_ref, o_ref, inverse_ref, bias_ref = refs[:8]
    dq_ref, dk_ref, dv_ref = refs[operands:]
    rows = q_ref.shape[1]
    dk_ref[...] = jnp.zeros_like(dk_ref)
    dv_ref[...] = jnp.zeros_like(dv_ref)
    for first in range(0, rows, TILE):
        at = slice(first, first + TILE)
        deltas = []
        for head in range(GROUP):
            of = slice(head * HD, (head + 1) * HD)
            product = d_ref[of, at].astype(f32) * o_ref[of, at].astype(f32)
            deltas.append(jnp.sum(product, axis=0, keepdims=True))
        d_query = [jnp.zeros((HD, TILE), f32) for _ in range(GROUP)]
        for start in range(first + shift, first + shift + WINDOW + TILE, TILE):
            near = slice(start, start + TILE)
            d_key = jnp.zeros((HD, TILE), f32)
            d_value = jnp.zeros((HD, TILE), f32)
            for head in range(GROUP):
                of = slice(head * HD, (head + 1) * HD)
                query = q_ref[of, at]
                d_out = d_ref[of, at]
                scores = nn_dot(k_ref[0, near, :], query)
                weight = jnp.exp2(scores * EXP2_SCALE + bias_ref[near, at])
                prob = weight * inverse_ref[0, head : head + 1, at]
                d_prob = nn_dot(v_ref[0, near, :], d_out)
                d_scores = (prob * (d_prob - deltas[head])).astype(bf16)
                d_query[head] = d_query[head] + nn_dot(kt_ref[:, near], d_scores)
                d_key = d_key + nt_dot(query, d_scores)
                d_value = d_value + nt_dot(d_out, prob.astype(bf16))
            dk_ref[:, near] += d_key
            dv_ref[:, near] += d_value
        for head in range(GROUP):
            dq_ref[head * HD : (head + 1) * HD, at] = d_query[head]


def attend(q_t, k, v_t, bias):
    kv, keys, _ = k.shape
    rows = q_t.shape[1]
    ones = jnp.ones((kv, SUM_ROWS, keys), bf16)
    v_ones = jnp.concatenate([v_t.reshape(kv, HD, keys), ones], axis=1)
    return pl.pallas_call(
        functools.partial(attend_kernel, keys - rows - WINDOW),
        grid=(kv,),
        in_specs=[
            pl.BlockSpec((GROUP * HD, rows), lambda h: (h, 0)),
            pl.BlockSpec((1, keys, HD), lambda h: (h, 0, 0)),
            pl.BlockSpec((1, HD + SUM_ROWS, keys), lambda h: (h, 0, 0)),
            pl.BlockSpec((keys, rows), lambda h: (0, 0)),
        ],
        out_specs=[
            pl.BlockSpec((GROUP * HD, rows), lambda h: (h, 0)),
            pl.BlockSpec((1, 8, rows), lambda h: (h, 0, 0)),
        ],
        out_shape=[jax.ShapeDtypeStruct((kv * GROUP * HD, rows), bf16), jax.ShapeDtypeStruct((kv, 8, rows), f32)],
        compiler_params=pltpu.CompilerParams(vmem_limit_bytes=40 * 2**20),
        cost_estimate=cost(13),
    )(q_t, k, v_ones, bias)


def attend_back(at, so_far, after, q_t, k, k_t, v, d_t, o_t, inverse, bias):
    kv, keys, _ = k.shape
    rows = q_t.shape[1]
    head_block = pl.BlockSpec((GROUP * HD, rows), lambda i: (at, 0))
    key_block = pl.BlockSpec((1, keys, HD), lambda i: (at, 0, 0))
    key_t_block = pl.BlockSpec((HD, keys), lambda i: (at, 0))
    waits = [*so_far, *after]
    operands = 8 + len(waits)
    return pl.pallas_call(
        functools.partial(attend_back_kernel, keys - rows - WINDOW, operands),
        grid=(1,),
        in_specs=[
            head_block,
            key_block,
            key_t_block,
            key_block,
            head_block,
            head_block,
            pl.BlockSpec((1, 8, rows), lambda i: (at, 0, 0)),
            pl.BlockSpec((keys, rows), lambda i: (0, 0)),
        ]
        + [pl.BlockSpec(memory_space=pl.ANY)] * len(waits),
        out_specs=[head_block, key_t_block, key_t_block],
        out_shape=[
            jax.ShapeDtypeStruct((kv * GROUP * HD, rows), f32),
            jax.ShapeDtypeStruct((kv * HD, keys), f32),
            jax.ShapeDtypeStruct((kv * HD, keys), f32),
        ],
        input_output_aliases={8 + i: i for i in range(len(so_far))},
        compiler_params=pltpu.CompilerParams(vmem_limit_bytes=40 * 2**20),
        cost_estimate=cost(11),
    )(q_t, k, k_t, v, d_t, o_t, inverse, bias, *waits)


def feed_kernel(n_ref, d_act_ref, gate_ref, up_ref, *refs):
    act_ref, d_gate_ref, d_up_ref = refs[-3:]
    normed = n_ref[...]
    gate = nn_dot(normed, gate_ref[...])
    up = nn_dot(normed, up_ref[...])
    sigmoid = 1.0 / (1.0 + jnp.exp(-gate))
    silu = gate * sigmoid
    act_ref[...] = (silu * up).astype(bf16)
    d_act = d_act_ref[...]
    d_gate_ref[...] = (d_act * up * sigmoid * (1.0 + gate * (1.0 - sigmoid))).astype(bf16)
    d_up_ref[...] = (d_act * silu).astype(bf16)


def feed(normed, d_act, gateup, *after):
    rows, width = normed.shape
    hidden = d_act.shape[1]
    tile = math.gcd(hidden, 512)
    steps = hidden // tile
    hidden_block = pl.BlockSpec((rows, tile), lambda i: (0, i))
    return pl.pallas_call(
        feed_kernel,
        grid=(steps,),
        in_specs=[
            pl.BlockSpec((rows, width), lambda i: (0, 0)),
            hidden_block,
            pl.BlockSpec((width, tile), lambda i: (0, i)),
            pl.BlockSpec((width, tile), lambda i: (0, i + steps)),
        ]
        + [ANYWHERE] * len(after),
        out_specs=[hidden_block] * 3,
        out_shape=[jax.ShapeDtypeStruct((rows, hidden), bf16)] * 3,
        compiler_params=pltpu.CompilerParams(vmem_limit_bytes=56 * 2**20),
        cost_estimate=cost(19.5),
    )(normed, d_act, gateup, gateup, *after)


def feed_back(d_gate, d_up, gateup, *after):
    rows, hidden = d_gate.shape
    width = gateup.shape[0]
    tile = math.gcd(width, 256)

    def kernel(d_gate_ref, d_up_ref, gate_ref, up_ref, *refs):
        total = nt_dot(d_gate_ref[...], gate_ref[...]) + nt_dot(d_up_ref[...], up_ref[...])
        refs[-1][...] = total.astype(bf16)

    whole = pl.BlockSpec((rows, hidden), lambda i: (0, 0))
    return pl.pallas_call(
        kernel,
        grid=(width // tile,),
        in_specs=[
            whole,
            whole,
            pl.BlockSpec((tile, hidden), lambda i: (i, 0)),
            pl.BlockSpec((tile, hidden), lambda i: (i, 1)),
        ]
        + [ANYWHERE] * len(after),
        out_specs=pl.BlockSpec((rows, tile), lambda i: (0, i)),
        out_shape=jax.ShapeDtypeStruct((rows, width), bf16),
        compiler_params=pltpu.CompilerParams(vmem_limit_bytes=56 * 2**20),
        cost_estimate=cost(17),
    )(d_gate, d_up, gateup, gateup, *after)


def feed_out(act, downs, down_start, *after):
    rows, hidden = act.shape
    width = downs.shape[0]
    tile = math.gcd(width, 256)
    step = math.gcd(math.gcd(hidden, down_start), 512)
    count = hidden // step

    def kernel(act_ref, *refs):
        total = jnp.zeros((rows, tile), f32)
        for at, ref in enumerate(refs[:count]):
            total = total + nt_dot(act_ref[:, at * step : (at + 1) * step], ref[...])
        refs[-1][...] = total.astype(bf16)

    return pl.pallas_call(
        kernel,
        grid=(width // tile,),
        in_specs=[pl.BlockSpec((rows, hidden), lambda i: (0, 0))]
        + [
            pl.BlockSpec((tile, step), functools.partial(lambda i, at: (i, at), at=at))
            for at in range(down_start // step, down_start // step + count)
        ]
        + [ANYWHERE] * len(after),
        out_specs=pl.BlockSpec((rows, tile), lambda i: (0, i)),
        out_shape=jax.ShapeDtypeStruct((rows, width), bf16),
        compiler_params=pltpu.CompilerParams(vmem_limit_bytes=56 * 2**20),
        cost_estimate=cost(9),
    )(act, *[downs] * count, *after)


def shards(
    tokens,
    w_query,
    w_keyval,
    w_out,
    w_gateup,
    w_down,
    attn_gain,
    ffn_gain,
    qk_gain,
    segments,
    positions,
    cotangent,
):
    ring = Ring()
    row_count = tokens.shape[0]
    depth = w_query.shape[0]
    model = tokens.shape[1]
    hidden = w_gateup.shape[2]
    tensor = lax.axis_index("tensor")
    query_width = w_query.shape[1]
    local_heads = query_width // HD
    local_kv = local_heads // GROUP
    kv_width = local_kv * HD
    all_kv = w_keyval.shape[1] // 2
    qkv_width = query_width + 2 * kv_width
    gain_count = 2 * qk_gain.shape[1]

    own_keyval = lax.dynamic_index_in_dim(
        w_keyval.reshape(depth, 2, all_kv // kv_width, kv_width), tensor, 2, keepdims=False
    ).reshape(depth, 2 * kv_width)
    head_gain_column = jnp.pad(qk_gain.reshape(gain_count), (0, depth - gain_count))
    gains = jnp.stack([attn_gain, ffn_gain, head_gain_column], axis=1)
    gains = jnp.pad(gains, ((0, 0), (0, LANES - gains.shape[1])))
    first_pack = jnp.concatenate([w_query, own_keyval, w_out.T, gains, w_down.T], axis=1)
    first_full = lax.all_gather(first_pack.astype(bf16), "dp", axis=0, tiled=True)
    gateup_full = lax.all_gather(
        w_gateup.reshape(depth, 2 * hidden).astype(bf16), "dp", axis=0, tiled=True
    )
    qkv_full = first_full[:, :qkv_width]
    gain_start = qkv_width + query_width
    out_full = first_full[:, qkv_width:gain_start]
    down_full = first_full[:, gain_start + LANES :]
    gain_columns = first_full[:, gain_start : gain_start + 3].astype(f32)
    attn_weight = gain_columns[:, 0]
    ffn_weight = gain_columns[:, 1]
    head_gains = gain_columns[:, 2].reshape(ring.count, depth)[:, :gain_count]
    head_gains = head_gains.reshape(ring.count, 2, qk_gain.shape[1]).transpose(1, 0, 2).reshape(2, HD)
    gain_query = head_gains[0][:, None]
    gain_key = head_gains[1][:, None]

    marks = (segments + 1).astype(bf16)
    seq_devices = min(SEQ_LEN // row_count, ring.count)
    own_sequence = ring.index // seq_devices
    reach_count = -(-WINDOW // row_count)
    halo_marks = []
    for step_back in range(reach_count, 0, -1):
        same_sequence = ((ring.index - step_back) // seq_devices == own_sequence).astype(bf16)
        halo_marks.append(from_behind(marks, step_back) * same_sequence)
    key_marks = jnp.concatenate(halo_marks + [marks], axis=0)
    key_count = key_marks.shape[0]
    distance = (jnp.arange(row_count, dtype=jnp.int32) + reach_count * row_count)[
        None, :
    ] - jnp.arange(key_count, dtype=jnp.int32)[:, None]
    allowed = (distance >= 0) & (distance < WINDOW) & (key_marks[:, None] == marks[None, :])
    bias = jnp.where(allowed, 0.0, MASKED).astype(f32)
    cos_table, sin_table = angles_of(positions)

    residual = tokens.astype(f32)
    attn_scale = inverse_rms(residual, 1)

    normed_low = (residual * attn_scale * attn_weight).astype(bf16)
    qkv_raw = lax.dot_general(
        qkv_full, normed_low, (((0,), (1,)), ((), ())), preferred_element_type=f32
    )
    query_raw = qkv_raw[:query_width].reshape(local_heads, HD, row_count)
    key_raw = qkv_raw[query_width : query_width + kv_width].reshape(local_kv, HD, row_count)
    query_scale = inverse_rms(query_raw, 1)
    key_scale = inverse_rms(key_raw, 1)
    query_low = rotate(query_raw * query_scale * gain_query, cos_table, sin_table).astype(bf16)
    key_low = rotate(key_raw * key_scale * gain_key, cos_table, sin_table).astype(bf16)
    query_low = query_low.reshape(query_width, row_count)
    keyval_low = jnp.concatenate(
        [key_low.reshape(kv_width, row_count), qkv_raw[query_width + kv_width :].astype(bf16)], axis=0
    )
    halo = [from_behind(keyval_low, step_back) for step_back in range(reach_count, 0, -1)]
    key_keyval = jnp.concatenate(halo + [keyval_low], axis=1)
    keys_t = key_keyval[:kv_width]
    values_t = key_keyval[kv_width:]
    keys = keys_t.reshape(local_kv, HD, key_count).transpose(0, 2, 1)
    values = values_t.reshape(local_kv, HD, key_count).transpose(0, 2, 1)
    attended, inverse_total = attend(query_low, keys, values_t, bias)
    mid_part = lax.dot_general(
        attended, out_full, (((0,), (1,)), ((), ())), preferred_element_type=f32
    )
    near_first = ring.bits
    normed_rows = ring.chosen(normed_low, near_first)
    cotangent_rows = transposed(cotangent)
    attended_back = attended.T
    mid = residual + tensor_sum(
        mid_part, corner(normed_rows), corner(cotangent_rows), corner(attended_back)
    )

    d_act = nn_dot(cotangent, down_full)
    ffn_scale = inverse_rms(mid, 1)
    normed2_low = (mid * ffn_scale * ffn_weight).astype(bf16)
    normed2_rows = ring.chosen(normed2_low, near_first)
    act_low, d_gate, d_up = feed(normed2_low, d_act, gateup_full, normed2_rows)
    gate_sum = Scatter(ring, normed2_rows, d_gate, near_first)
    up_sum = Scatter(ring, normed2_rows, d_up, near_first)
    sums = {"G": gate_sum, "U": up_sum}
    totals = {}
    heads = 0
    grads = ()
    down_low = None
    before = None
    for step in ORDER:
        after = () if before is None else (before,)
        if step in sums:
            one = sums[step]
            if len(one.got) < len(one.bits) and step not in totals:
                before = one.send(*after, parts=PARTS if step in "OQK" and not one.got else 1)
                if len(one.got) == 4:
                    while len(one.got) < len(one.bits):
                        before = one.send(before)
            else:
                before = totals[step] = one.total(*after, transposed=step == "O")
        elif step == "D":
            if down_low is None:
                before = product(cotangent_rows, act_low, model, 0, [], after)[0]
                down_low = lax.psum_scatter(before, "dp", scatter_dimension=0, tiled=True)
            else:
                before = totals["D"] = turned(down_low, *after)
        elif step == "FB":
            before = d_normed2_low = feed_back(d_gate, d_up, gateup_full, *after)
            d_normed2_other = other_tensor(d_normed2_low)
        elif step == "FO":
            before = result_low = feed_out(act_low, first_full, gain_start + LANES, *after)
        elif step == "NB":
            d_mid, d_mid_low, d_ffn_weight = norm_back(
                mid, cotangent, d_normed2_low, d_normed2_other, ffn_weight, *after
            )
            before = d_mid_low
            result_other = other_tensor(tie(result_low, d_normed2_other))
        elif step == "DA":
            before = d_attended = product_tt(first_full, qkv_width, query_width, d_mid_low)
        elif step == "H":
            grads = attend_back(
                heads,
                grads,
                after,
                query_low,
                keys,
                keys_t,
                values,
                d_attended,
                attended,
                inverse_total,
                bias,
            )
            heads += 1
            d_query, d_keys, d_values = grads
            before = d_keys
        elif step == "HP":
            halo_grads = halo_parts(d_keys, d_values, row_count, *after)
            got = [from_behind(part, at - reach_count) for at, part in enumerate(halo_grads)]
            before = halo_grads[0]
        elif step == "QB":
            d_query_low, d_gain_query = query_back(
                d_query, qkv_raw, cos_table[0], sin_table[0], gain_query, *after
            )
            before = d_query_low
            sums["Q"] = Scatter(ring, normed_rows, d_query_low, near_first)
        elif step == "OP":
            before = d_mid_rows = ring.chosen(tie(d_mid_low, *after), near_first)
            sums["O"] = Scatter(ring, d_mid_rows, attended_back, near_first)
        elif step == "KB":
            d_keyval_low, d_gain_key = key_back(
                d_keys,
                d_values,
                got,
                qkv_raw,
                query_width,
                cos_table[0],
                sin_table[0],
                gain_key,
                *after,
            )
            before = d_keyval_low
        elif step == "IB":
            d_normed_low, d_attn_part = input_back(
                d_query_low, d_keyval_low, first_full, tokens, attn_scale, *after
            )
            d_normed_other = other_tensor(d_normed_low)
            before = d_normed_low
        elif step == "GB":
            places = jnp.arange(2 * HD, dtype=jnp.int32)
            per_device = gain_count // 2
            places = (
                places % HD // per_device * depth
                + places // HD * per_device
                + places % per_device
            )
            places = (places[:, None] == jnp.arange(model, dtype=jnp.int32)[None, :]).astype(bf16)
            gain_grads = gain_block(
                d_attn_part, d_ffn_weight, d_gain_query, d_gain_key, places, *after
            )
            before = gain_rows = ring.chosen(gain_grads, near_first)
            sums["K"] = Scatter(ring, normed_rows, d_keyval_low, near_first, gain_rows)
        elif step == "AD":
            before = output = add_up(mid, result_low, result_other, *after)
        elif step == "IG":
            _, input_grad, _ = norm_back(
                tokens, d_mid, d_normed_low, d_normed_other, attn_weight, *after
            )
            before = input_grad
    grad_down, grad_out, grad_query = totals["D"], totals["O"], totals["Q"]
    grad_gateup = side_by_side(totals["G"], totals["U"])
    shared = totals["K"].astype(bf16)
    grad_keyval, gains_t = both_tensors(shared, other_tensor(shared), tensor, kv_width)
    grad_attn_gain = gains_t[0]
    grad_ffn_gain = gains_t[1]
    grad_heads = gains_t[2, :gain_count].reshape(2, gain_count // 2)
    return (
        output,
        input_grad,
        grad_query,
        grad_keyval,
        grad_out,
        grad_gateup,
        grad_down,
        grad_attn_gain,
        grad_ffn_gain,
        grad_heads,
    )


def solution(mesh):
    in_specs = (
        P("dp", None),
        P("dp", "tensor"),
        P("dp", None),
        P("tensor", "dp"),
        P("dp", None, "tensor"),
        P("tensor", "dp"),
        P("dp"),
        P("dp"),
        P(None, "dp"),
        P("dp"),
        P("dp"),
        P("dp", None),
    )
    out_specs = (
        P("dp", None),
        P("dp", None),
        P("dp", "tensor"),
        P("dp", None),
        P("tensor", "dp"),
        P("dp", None, "tensor"),
        P("tensor", "dp"),
        P("dp"),
        P("dp"),
        P(None, "dp"),
    )
    return jax.shard_map(shards, mesh=mesh, in_specs=in_specs, out_specs=out_specs, check_vma=False)
```

```python
import functools
import math

import jax
import jax.numpy as jnp
from jax import lax
from jax.experimental import pallas as pl
from jax.experimental.pallas import tpu as pltpu
from jax.sharding import PartitionSpec as P

QH = 24
KVH = 6
HD = 64
GROUP = QH // KVH
WINDOW = 1024
SEQ_LEN = 8192
LANES = 128

EPSILON = 1e-06
SCORE_SCALE = 0.125
MASKED = -1e30
ROPE_BASE = 10000.0
EXP2_SCALE = SCORE_SCALE * math.log2(math.e)
TILE = 256
SUM_ROWS = 16
PARTS = 4
ORDER = (
    "G", "D", "FB", "G", "U", "FO", "U", "NB", "DA", "H", "H", "G",
    "H", "HP", "QB", "Q", "OP", "O", "G", "Q", "O", "KB", "U", "IB",
    "G", "Q", "O", "GB", "K", "K", "U", "Q", "O", "K", "IG", "K",
    "AD", "D", "U", "Q", "O", "K",
)
LINK_SHARE = 0.35

bf16 = jnp.bfloat16
f32 = jnp.float32
ANYWHERE = pl.BlockSpec(memory_space=pl.ANY)


def cost(microseconds):
    return pl.CostEstimate(
        flops=int(microseconds * LINK_SHARE * 1.15e9), bytes_accessed=0, transcendentals=0
    )


def angles_of(positions):
    half_width = HD // 2
    frequency = jnp.exp(
        jnp.arange(half_width, dtype=f32) * (-math.log(ROPE_BASE) / half_width)
    )
    phases = frequency[:, None] * positions.astype(f32)[None, :]
    return jnp.cos(phases)[None], jnp.sin(phases)[None]


def rotate(values, cos_table, sin_table):
    half_width = values.shape[1] // 2
    first_half = values[:, :half_width]
    second_half = values[:, half_width:]
    return jnp.concatenate(
        [
            first_half * cos_table - second_half * sin_table,
            second_half * cos_table + first_half * sin_table,
        ],
        axis=1,
    )


def inverse_rms(values, axis):
    return lax.rsqrt(jnp.mean(values * values, axis=axis, keepdims=True) + EPSILON)


def rms_back(values, scale, weight, d_out, axis):
    weighted = d_out * weight
    pull = jnp.mean(weighted * values, axis=axis, keepdims=True)
    return scale * weighted - values * (scale * scale * scale * pull)


class Ring:
    def __init__(self):
        self.count = lax.axis_size("dp")
        self.index = lax.axis_index("dp")
        self.bits = [1 << at for at in range(self.count.bit_length() - 1)]

    def order(self, bits):
        order = []
        for at in range(self.count - 1, -1, -1):
            flips = sum(bit for place, bit in enumerate(reversed(bits)) if at >> place & 1)
            order.append(self.index ^ flips)
        return jnp.stack(order).astype(jnp.int32)

    def chosen(self, array, bits):
        depth = array.shape[1] // self.count
        if depth % LANES:
            blocks = array.T.reshape(self.count, depth, array.shape[0])
            return jnp.take(blocks, self.order(bits), axis=0).reshape(array.shape[1], array.shape[0])
        return transposed_blocks(self.order(bits), array, depth)


class Scatter:
    def __init__(self, ring, left, right, bits, tail=None):
        self.ring, self.left, self.right, self.bits, self.tail = ring, left, right, bits, tail
        self.got = []

    def rows(self):
        step = len(self.got)
        last = step == len(self.bits)
        size = self.left.shape[0] >> (step if last else step + 1)
        start = self.left.shape[0] - (self.left.shape[0] >> step)
        adds = []
        for at, parts in enumerate(self.got):
            first = start - self.left.shape[0] + (self.left.shape[0] >> at + 1)
            height = parts[0].shape[0]
            if height >= size:
                adds.append([(parts[first // height], first % height // size)])
            else:
                adds.append([(part, 0) for part in parts[first // height : (first + size) // height]])
        return size, start // size, adds

    def send(self, *after, parts=1):
        size, block, adds = self.rows()
        sent = product(
            self.left, self.right, size, block, adds, after, self.tail, parts=parts
        )
        bit = self.bits[len(self.got)]
        pairs = [(i, i ^ bit) for i in range(self.ring.count)]
        self.got.append([lax.ppermute(part, "dp", pairs) for part in sent])
        return sent[0]

    def total(self, *after, transposed=False):
        while len(self.got) < len(self.bits):
            after = (self.send(*after),)
        size, block, adds = self.rows()
        return product(self.left, self.right, size, block, adds, after, self.tail, f32, transposed)[0]


def other_tensor(array):
    count = lax.axis_size("tensor")
    return lax.ppermute(array, "tensor", [(i, (i + 1) % count) for i in range(count)])


def tensor_sum(partial, *before):
    low = partial.astype(bf16)
    other = other_tensor(low)
    if before:
        other = tie(other, *before)
    return low.astype(f32) + other.astype(f32)


def from_behind(shard, by):
    length = lax.axis_size("dp")
    pairs = [(i, i + by) for i in range(length) if 0 <= i + by < length]
    return lax.ppermute(shard, "dp", pairs)


def tn_dot(left, right):
    return lax.dot_general(left, right, (((0,), (0,)), ((), ())), preferred_element_type=f32)


def nt_dot(left, right):
    return lax.dot_general(left, right, (((1,), (1,)), ((), ())), preferred_element_type=f32)


def nn_dot(left, right):
    return jnp.dot(left, right, preferred_element_type=f32)


def tie(array, *others):
    def kernel(*refs):
        del refs

    return pl.pallas_call(
        kernel,
        in_specs=[pl.BlockSpec(memory_space=pl.ANY)] * (1 + len(others)),
        out_specs=pl.BlockSpec(memory_space=pl.ANY),
        out_shape=jax.ShapeDtypeStruct(array.shape, array.dtype),
        input_output_aliases={0: 0},
        cost_estimate=cost(0),
    )(array, *others)


def corner(array):
    return array[: 2 * 8, :LANES]


def transposed(array, *after):
    tokens, width = array.shape
    step = math.gcd(tokens, LANES)

    def kernel(in_ref, *refs):
        refs[-1][...] = in_ref[...].T

    return pl.pallas_call(
        kernel,
        grid=(tokens // step,),
        in_specs=[pl.BlockSpec((step, width), lambda i: (i, 0))] + [ANYWHERE] * len(after),
        out_specs=pl.BlockSpec((width, step), lambda i: (0, i)),
        out_shape=jax.ShapeDtypeStruct((width, tokens), array.dtype),
        cost_estimate=cost(4.8),
    )(array, *after)


def transposed_blocks(order, array, depth):
    tokens, width = array.shape
    step = math.gcd(tokens, LANES)

    def kernel(order_ref, in_ref, out_ref):
        for at in range(width // depth):
            column = pl.multiple_of(order_ref[at] * depth, depth)
            out_ref[at * depth : (at + 1) * depth, :] = in_ref[:, pl.ds(column, depth)].T

    return pl.pallas_call(
        kernel,
        grid_spec=pltpu.PrefetchScalarGridSpec(
            num_scalar_prefetch=1,
            grid=(tokens // step,),
            in_specs=[pl.BlockSpec((step, width), lambda i, order: (i, 0))],
            out_specs=pl.BlockSpec((width, step), lambda i, order: (0, i)),
        ),
        out_shape=jax.ShapeDtypeStruct((width, tokens), array.dtype),
        cost_estimate=cost(4.8),
    )(order, array)


def product(
    left, right, size, block, adds, after=(), tail=None, out_type=bf16, transposed=False, parts=1
):
    depth, columns = right.shape
    most = max(LANES, min(columns, 512 * 1024 // size))
    tile = max(t for t in range(LANES, most + 1, LANES) if columns % t == 0)
    if tail is not None:
        tile = LANES
    steps = columns // tile
    flat = [(array, row, size // len(add)) for add in adds for array, row in add]

    def kernel(left_ref, right_ref, *refs):
        def put(total):
            at = 0
            for add in adds:
                pieces = [ref[...].astype(f32) for ref in refs[at : at + len(add)]]
                total = total + (pieces[0] if len(add) == 1 else jnp.concatenate(pieces, axis=0))
                at += len(add)
            total = (total.T if transposed else total).astype(out_type)
            height = total.shape[0] // parts
            for at, ref in enumerate(refs[len(refs) - parts :]):
                ref[...] = total[at * height : (at + 1) * height]

        if tail is None:
            put(nn_dot(left_ref[...], right_ref[...]))
            return

        @pl.when(pl.program_id(0) < steps)
        def _():
            put(nn_dot(left_ref[...], right_ref[...]))

        @pl.when(pl.program_id(0) == steps)
        def _():
            put(refs[len(flat)][...].astype(f32))

    all_columns = columns
    in_specs = [
        pl.BlockSpec((size, depth), lambda i: (block, 0)),
        pl.BlockSpec((depth, tile), lambda i: (0, jnp.minimum(i, steps - 1))),
    ] + [
        pl.BlockSpec((height, tile), functools.partial(lambda i, row: (row, i), row=row))
        for _, row, height in flat
    ]
    operands = [left, right, *[array for array, _, _ in flat]]
    if tail is not None:
        all_columns += LANES
        in_specs.append(pl.BlockSpec((size, LANES), lambda i: (block, 0)))
        operands.append(tail)
    height = size // parts
    out_shape, out_block, out_map = (height, all_columns), (height, tile), lambda i: (0, i)
    if transposed:
        out_shape, out_block, out_map = (all_columns, height), (tile, height), lambda i: (i, 0)
    return pl.pallas_call(
        kernel,
        grid=(all_columns // tile,),
        in_specs=in_specs + [ANYWHERE] * len(after),
        out_specs=[pl.BlockSpec(out_block, out_map)] * parts,
        out_shape=[jax.ShapeDtypeStruct(out_shape, out_type)] * parts,
        compiler_params=pltpu.CompilerParams(vmem_limit_bytes=40 * 2**20),
        cost_estimate=cost(2 + 2 * size * depth * columns / 0.9e9),
    )(*operands, *after)


def product_tt(left, first, columns, right):
    depth = left.shape[0]
    rows = right.shape[0]
    tile = max(t for t in range(LANES, 384 + 1, LANES) if columns % t == 0 and first % t == 0)

    def kernel(left_ref, right_ref, out_ref):
        out_ref[...] = nt_dot(left_ref[...].T, right_ref[...]).astype(bf16)

    return pl.pallas_call(
        kernel,
        grid=(columns // tile,),
        in_specs=[
            pl.BlockSpec((depth, tile), lambda i: (0, i + first // tile)),
            pl.BlockSpec((rows, depth), lambda i: (0, 0)),
        ],
        out_specs=pl.BlockSpec((tile, rows), lambda i: (i, 0)),
        out_shape=jax.ShapeDtypeStruct((columns, rows), bf16),
        compiler_params=pltpu.CompilerParams(vmem_limit_bytes=40 * 2**20),
        cost_estimate=cost(4.3),
    )(left, right)


def norm_back(values, direct, part, other, gain, *after):
    rows, width = values.shape
    step = math.gcd(rows, 128)

    def kernel(values_ref, direct_ref, part_ref, other_ref, gain_ref, *refs):
        out_ref, low_ref, gain_out_ref = refs[len(after) :]
        value = values_ref[...].astype(f32)
        scale = inverse_rms(value, 1)
        d_out = part_ref[...].astype(f32) + other_ref[...].astype(f32)
        result = direct_ref[...].astype(f32) + rms_back(value, scale, gain_ref[...], d_out, 1)
        out_ref[...] = result
        low_ref[...] = result.astype(bf16)

        @pl.when(pl.program_id(0) == 0)
        def _():
            gain_out_ref[...] = jnp.zeros_like(gain_out_ref)

        gain_out_ref[...] += jnp.sum(d_out * value * scale, axis=0, keepdims=True)

    block = pl.BlockSpec((step, width), lambda i: (i, 0))
    row = pl.BlockSpec((1, width), lambda i: (0, 0))
    return pl.pallas_call(
        kernel,
        grid=(rows // step,),
        in_specs=[block] * 4 + [row] + [ANYWHERE] * len(after),
        out_specs=[block, block, row],
        out_shape=[
            jax.ShapeDtypeStruct((rows, width), f32),
            jax.ShapeDtypeStruct((rows, width), bf16),
            jax.ShapeDtypeStruct((1, width), f32),
        ],
        compiler_params=pltpu.CompilerParams(vmem_limit_bytes=40 * 2**20),
        cost_estimate=cost(7),
    )(values, direct, part, other, gain[None, :], *after)


def add_up(values, part, other, *after):
    rows, width = values.shape
    step = math.gcd(rows, 128)

    def kernel(values_ref, part_ref, other_ref, *refs):
        added = part_ref[...].astype(f32) + other_ref[...].astype(f32)
        refs[-1][...] = (values_ref[...] + added).astype(bf16)

    block = pl.BlockSpec((step, width), lambda i: (i, 0))
    return pl.pallas_call(
        kernel,
        grid=(rows // step,),
        in_specs=[block] * 3 + [ANYWHERE] * len(after),
        out_specs=block,
        out_shape=jax.ShapeDtypeStruct((rows, width), bf16),
        cost_estimate=cost(3),
    )(values, part, other, *after)


def turn_back(d_rotated, raw, cos_table, sin_table, gain):
    half_width = HD // 2
    first, second = d_rotated[:half_width], d_rotated[half_width:]
    d_normed = jnp.concatenate(
        [first * cos_table + second * sin_table, second * cos_table - first * sin_table], axis=0
    )
    scale = inverse_rms(raw, 0)
    return rms_back(raw, scale, gain, d_normed, 0), d_normed * raw * scale


def query_back(d_query, raw, cos_table, sin_table, gain, *after):
    width, rows = d_query.shape
    step = GROUP * HD

    def kernel(d_ref, raw_ref, cos_ref, sin_ref, gain_ref, *refs):
        out_ref, gain_out_ref = refs[len(after) :]
        results = []
        d_gain = jnp.zeros((HD, rows), f32)
        for head in range(GROUP):
            of = slice(head * HD, (head + 1) * HD)
            result, by_token = turn_back(
                d_ref[of, :] * SCORE_SCALE, raw_ref[of, :], cos_ref[...], sin_ref[...], gain_ref[...]
            )
            results.append(result)
            d_gain = d_gain + by_token
        out_ref[...] = jnp.concatenate(results, axis=0).astype(bf16).T

        @pl.when(pl.program_id(0) == 0)
        def _():
            gain_out_ref[...] = jnp.zeros_like(gain_out_ref)

        gain_out_ref[...] += jnp.sum(d_gain, axis=1, keepdims=True)

    block = pl.BlockSpec((step, rows), lambda i: (i, 0))
    table = pl.BlockSpec((HD // 2, rows), lambda i: (0, 0))
    column = pl.BlockSpec((HD, 1), lambda i: (0, 0))
    return pl.pallas_call(
        kernel,
        grid=(width // step,),
        in_specs=[block, block, table, table, column] + [ANYWHERE] * len(after),
        out_specs=[pl.BlockSpec((rows, step), lambda i: (0, i)), column],
        out_shape=[
            jax.ShapeDtypeStruct((rows, width), bf16),
            jax.ShapeDtypeStruct((HD, 1), f32),
        ],
        compiler_params=pltpu.CompilerParams(vmem_limit_bytes=40 * 2**20),
        cost_estimate=cost(1.6),
    )(d_query, raw, cos_table, sin_table, gain, *after)


def halo_parts(d_keys, d_values, rows, *after):
    width, count = d_keys.shape
    parts = count // rows - 1

    def kernel(d_keys_ref, d_values_ref, *refs):
        for at, ref in enumerate(refs[len(after) :]):
            of = slice(at * rows, (at + 1) * rows)
            ref[:width, :] = d_keys_ref[:, of].astype(bf16)
            ref[width:, :] = d_values_ref[:, of].astype(bf16)

    whole = pl.BlockSpec((width, count), lambda i: (0, 0))
    return pl.pallas_call(
        kernel,
        grid=(1,),
        in_specs=[whole, whole] + [ANYWHERE] * len(after),
        out_specs=[pl.BlockSpec((2 * width, rows), lambda i: (0, 0))] * parts,
        out_shape=[jax.ShapeDtypeStruct((2 * width, rows), bf16)] * parts,
        compiler_params=pltpu.CompilerParams(vmem_limit_bytes=40 * 2**20),
        cost_estimate=cost(1),
    )(d_keys, d_values, *after)


def key_back(d_keys, d_values, got, raw, first, cos_table, sin_table, gain, *after):
    width, count = d_keys.shape
    rows = got[0].shape[1]
    own = pl.BlockSpec((width, rows), lambda i: (0, count // rows - 1))
    heads = width // HD

    def kernel(d_keys_ref, d_values_ref, raw_ref, cos_ref, sin_ref, gain_ref, *refs):
        out_ref, gain_out_ref = refs[len(got) + len(after) :]
        d_key = d_keys_ref[...]
        d_value = d_values_ref[...]
        for ref in refs[: len(got)]:
            d_key = d_key + ref[:width, :].astype(f32)
            d_value = d_value + ref[width:, :].astype(f32)
        results = []
        d_gain = jnp.zeros((HD, rows), f32)
        for head in range(heads):
            of = slice(head * HD, (head + 1) * HD)
            result, by_token = turn_back(
                d_key[of] * SCORE_SCALE, raw_ref[of, :], cos_ref[...], sin_ref[...], gain_ref[...]
            )
            results.append(result)
            d_gain = d_gain + by_token
        out_ref[...] = jnp.concatenate(results + [d_value], axis=0).astype(bf16).T
        gain_out_ref[...] = jnp.sum(d_gain, axis=1, keepdims=True)

    table = pl.BlockSpec((HD // 2, rows), lambda i: (0, 0))
    column = pl.BlockSpec((HD, 1), lambda i: (0, 0))
    return pl.pallas_call(
        kernel,
        grid=(1,),
        in_specs=[
            own,
            own,
            pl.BlockSpec((width, rows), lambda i: (first // width, 0)),
            table,
            table,
            column,
        ]
        + [pl.BlockSpec((2 * width, rows), lambda i: (0, 0))] * len(got)
        + [ANYWHERE] * len(after),
        out_specs=[pl.BlockSpec((rows, 2 * width), lambda i: (0, 0)), column],
        out_shape=[
            jax.ShapeDtypeStruct((rows, 2 * width), bf16),
            jax.ShapeDtypeStruct((HD, 1), f32),
        ],
        compiler_params=pltpu.CompilerParams(vmem_limit_bytes=40 * 2**20),
        cost_estimate=cost(1.6),
    )(d_keys, d_values, raw, cos_table, sin_table, gain, *got, *after)


def input_back(d_query, d_keyval, weights, values, scale, *after):
    rows, query_width = d_query.shape
    qkv_width = query_width + d_keyval.shape[1]
    width = weights.shape[0]
    tile = math.gcd(width, 256)

    def kernel(d_query_ref, d_keyval_ref, weights_ref, values_ref, scale_ref, *refs):
        out_ref, gain_out_ref = refs[len(after) :]
        part = nt_dot(d_query_ref[...], weights_ref[:, :query_width]) + nt_dot(
            d_keyval_ref[...], weights_ref[:, query_width:]
        )
        out_ref[...] = part.astype(bf16)
        product_sum = part * values_ref[...].astype(f32) * scale_ref[...]
        gain_out_ref[...] = jnp.sum(product_sum, axis=0, keepdims=True)

    out = pl.BlockSpec((rows, tile), lambda i: (0, i))
    return pl.pallas_call(
        kernel,
        grid=(width // tile,),
        in_specs=[
            pl.BlockSpec((rows, query_width), lambda i: (0, 0)),
            pl.BlockSpec((rows, qkv_width - query_width), lambda i: (0, 0)),
            pl.BlockSpec((tile, qkv_width), lambda i: (i, 0)),
            out,
            pl.BlockSpec((rows, 1), lambda i: (0, 0)),
        ]
        + [ANYWHERE] * len(after),
        out_specs=[out, pl.BlockSpec((1, tile), lambda i: (0, i))],
        out_shape=[
            jax.ShapeDtypeStruct((rows, width), bf16),
            jax.ShapeDtypeStruct((1, width), f32),
        ],
        compiler_params=pltpu.CompilerParams(vmem_limit_bytes=40 * 2**20),
        cost_estimate=cost(8),
    )(d_query, d_keyval, weights, values, scale, *after)


def gain_block(d_attn, d_ffn, d_query, d_key, places, *after):
    width = d_attn.shape[1]

    def kernel(d_attn_ref, d_ffn_ref, d_query_ref, d_key_ref, places_ref, *refs):
        out_ref = refs[-1]
        out_ref[...] = jnp.zeros_like(out_ref)
        heads = jnp.sum(
            d_query_ref[...] * places_ref[:HD, :].astype(f32)
            + d_key_ref[...] * places_ref[HD:, :].astype(f32),
            axis=0,
            keepdims=True,
        )
        out_ref[0:1, :] = d_attn_ref[...].astype(bf16)
        out_ref[1:2, :] = d_ffn_ref[...].astype(bf16)
        out_ref[2:3, :] = heads.astype(bf16)

    return pl.pallas_call(
        kernel,
        in_specs=[pl.BlockSpec(memory_space=pltpu.VMEM)] * 5 + [ANYWHERE] * len(after),
        out_shape=jax.ShapeDtypeStruct((LANES, width), bf16),
        cost_estimate=cost(1),
    )(d_attn, d_ffn, d_query, d_key, places, *after)


def turned(array, *after):
    rows, columns = array.shape
    tile = math.gcd(columns, 512)

    def kernel(in_ref, *refs):
        refs[-1][...] = in_ref[...].astype(f32).T

    return pl.pallas_call(
        kernel,
        grid=(columns // tile,),
        in_specs=[pl.BlockSpec((rows, tile), lambda i: (0, i))] + [ANYWHERE] * len(after),
        out_specs=pl.BlockSpec((tile, rows), lambda i: (i, 0)),
        out_shape=jax.ShapeDtypeStruct((columns, rows), f32),
        cost_estimate=cost(2),
    )(array, *after)


def both_tensors(mine, theirs, tensor, width):
    rows = mine.shape[0]

    def kernel(tensor_ref, mine_ref, theirs_ref, out_ref, gains_ref):
        own = mine_ref[...].astype(f32)
        other = theirs_ref[...].astype(f32)
        first = tensor_ref[0] == 0
        low = jnp.where(first, own, other)
        high = jnp.where(first, other, own)
        out_ref[...] = jnp.concatenate(
            [low[:, :width], high[:, :width], low[:, width : 2 * width], high[:, width : 2 * width]],
            axis=1,
        )
        column = lax.broadcasted_iota(jnp.int32, (rows, LANES), 1)
        own_gains = own[:, 2 * width :]
        gains = own_gains + jnp.where(column == 1, 0.0, other[:, 2 * width :])
        gains_ref[...] = gains.T[:8, :]

    return pl.pallas_call(
        kernel,
        in_specs=[pl.BlockSpec(memory_space=pltpu.SMEM)]
        + [pl.BlockSpec(memory_space=pltpu.VMEM)] * 2,
        out_shape=[
            jax.ShapeDtypeStruct((rows, 4 * width), f32),
            jax.ShapeDtypeStruct((8, rows), f32),
        ],
        cost_estimate=cost(2),
    )(tensor.reshape(1).astype(jnp.int32), mine, theirs)


def side_by_side(first, second):
    rows, columns = first.shape
    step = math.gcd(rows, 32)

    def kernel(first_ref, second_ref, out_ref):
        out_ref[:, 0, :] = first_ref[...]
        out_ref[:, 1, :] = second_ref[...]

    return pl.pallas_call(
        kernel,
        grid=(rows // step,),
        in_specs=[pl.BlockSpec((step, columns), lambda i: (i, 0))] * 2,
        out_specs=pl.BlockSpec((step, 2, columns), lambda i: (i, 0, 0)),
        out_shape=jax.ShapeDtypeStruct((rows, 2, columns), first.dtype),
        cost_estimate=cost(4),
    )(first, second)


def attend_kernel(shift, q_ref, k_ref, v_ref, bias_ref, out_ref, inverse_ref):
    rows = q_ref.shape[1]
    for first in range(0, rows, TILE):
        at = slice(first, first + TILE)
        for head in range(GROUP):
            of = slice(head * HD, (head + 1) * HD)
            query = q_ref[of, at]
            total = jnp.zeros((HD + SUM_ROWS, TILE), f32)
            for start in range(first + shift, first + shift + WINDOW + TILE, TILE):
                near = slice(start, start + TILE)
                scores = nn_dot(k_ref[0, near, :], query)
                weight = jnp.exp2(scores * EXP2_SCALE + bias_ref[near, at]).astype(bf16)
                total = total + nn_dot(v_ref[0, :, near], weight)
            inverse = 1.0 / total[HD : HD + 1]
            out_ref[of, at] = (total[:HD] * inverse).astype(bf16)
            inverse_ref[0, head : head + 1, at] = inverse


def attend_back_kernel(shift, operands, *refs):
    q_ref, k_ref, kt_ref, v_ref, d_ref, o_ref, inverse_ref, bias_ref = refs[:8]
    dq_ref, dk_ref, dv_ref = refs[operands:]
    rows = q_ref.shape[1]
    dk_ref[...] = jnp.zeros_like(dk_ref)
    dv_ref[...] = jnp.zeros_like(dv_ref)
    for first in range(0, rows, TILE):
        at = slice(first, first + TILE)
        deltas = []
        for head in range(GROUP):
            of = slice(head * HD, (head + 1) * HD)
            product = d_ref[of, at].astype(f32) * o_ref[of, at].astype(f32)
            deltas.append(jnp.sum(product, axis=0, keepdims=True))
        d_query = [jnp.zeros((HD, TILE), f32) for _ in range(GROUP)]
        for start in range(first + shift, first + shift + WINDOW + TILE, TILE):
            near = slice(start, start + TILE)
            d_key = jnp.zeros((HD, TILE), f32)
            d_value = jnp.zeros((HD, TILE), f32)
            for head in range(GROUP):
                of = slice(head * HD, (head + 1) * HD)
                query = q_ref[of, at]
                d_out = d_ref[of, at]
                scores = nn_dot(k_ref[0, near, :], query)
                weight = jnp.exp2(scores * EXP2_SCALE + bias_ref[near, at])
                prob = weight * inverse_ref[0, head : head + 1, at]
                d_prob = nn_dot(v_ref[0, near, :], d_out)
                d_scores = (prob * (d_prob - deltas[head])).astype(bf16)
                d_query[head] = d_query[head] + nn_dot(kt_ref[:, near], d_scores)
                d_key = d_key + nt_dot(query, d_scores)
                d_value = d_value + nt_dot(d_out, prob.astype(bf16))
            dk_ref[:, near] += d_key
            dv_ref[:, near] += d_value
        for head in range(GROUP):
            dq_ref[head * HD : (head + 1) * HD, at] = d_query[head]


def attend(q_t, k, v_t, bias):
    kv, keys, _ = k.shape
    rows = q_t.shape[1]
    ones = jnp.ones((kv, SUM_ROWS, keys), bf16)
    v_ones = jnp.concatenate([v_t.reshape(kv, HD, keys), ones], axis=1)
    return pl.pallas_call(
        functools.partial(attend_kernel, keys - rows - WINDOW),
        grid=(kv,),
        in_specs=[
            pl.BlockSpec((GROUP * HD, rows), lambda h: (h, 0)),
            pl.BlockSpec((1, keys, HD), lambda h: (h, 0, 0)),
            pl.BlockSpec((1, HD + SUM_ROWS, keys), lambda h: (h, 0, 0)),
            pl.BlockSpec((keys, rows), lambda h: (0, 0)),
        ],
        out_specs=[
            pl.BlockSpec((GROUP * HD, rows), lambda h: (h, 0)),
            pl.BlockSpec((1, 8, rows), lambda h: (h, 0, 0)),
        ],
        out_shape=[jax.ShapeDtypeStruct((kv * GROUP * HD, rows), bf16), jax.ShapeDtypeStruct((kv, 8, rows), f32)],
        compiler_params=pltpu.CompilerParams(vmem_limit_bytes=40 * 2**20),
        cost_estimate=cost(13),
    )(q_t, k, v_ones, bias)


def attend_back(at, so_far, after, q_t, k, k_t, v, d_t, o_t, inverse, bias):
    kv, keys, _ = k.shape
    rows = q_t.shape[1]
    head_block = pl.BlockSpec((GROUP * HD, rows), lambda i: (at, 0))
    key_block = pl.BlockSpec((1, keys, HD), lambda i: (at, 0, 0))
    key_t_block = pl.BlockSpec((HD, keys), lambda i: (at, 0))
    waits = [*so_far, *after]
    operands = 8 + len(waits)
    return pl.pallas_call(
        functools.partial(attend_back_kernel, keys - rows - WINDOW, operands),
        grid=(1,),
        in_specs=[
            head_block,
            key_block,
            key_t_block,
            key_block,
            head_block,
            head_block,
            pl.BlockSpec((1, 8, rows), lambda i: (at, 0, 0)),
            pl.BlockSpec((keys, rows), lambda i: (0, 0)),
        ]
        + [pl.BlockSpec(memory_space=pl.ANY)] * len(waits),
        out_specs=[head_block, key_t_block, key_t_block],
        out_shape=[
            jax.ShapeDtypeStruct((kv * GROUP * HD, rows), f32),
            jax.ShapeDtypeStruct((kv * HD, keys), f32),
            jax.ShapeDtypeStruct((kv * HD, keys), f32),
        ],
        input_output_aliases={8 + i: i for i in range(len(so_far))},
        compiler_params=pltpu.CompilerParams(vmem_limit_bytes=40 * 2**20),
        cost_estimate=cost(11),
    )(q_t, k, k_t, v, d_t, o_t, inverse, bias, *waits)


def feed_kernel(n_ref, d_act_ref, gate_ref, up_ref, *refs):
    act_ref, d_gate_ref, d_up_ref = refs[-3:]
    normed = n_ref[...]
    gate = nn_dot(normed, gate_ref[...])
    up = nn_dot(normed, up_ref[...])
    sigmoid = 1.0 / (1.0 + jnp.exp(-gate))
    silu = gate * sigmoid
    act_ref[...] = (silu * up).astype(bf16)
    d_act = d_act_ref[...]
    d_gate_ref[...] = (d_act * up * sigmoid * (1.0 + gate * (1.0 - sigmoid))).astype(bf16)
    d_up_ref[...] = (d_act * silu).astype(bf16)


def feed(normed, d_act, gateup, *after):
    rows, width = normed.shape
    hidden = d_act.shape[1]
    tile = math.gcd(hidden, 512)
    steps = hidden // tile
    hidden_block = pl.BlockSpec((rows, tile), lambda i: (0, i))
    return pl.pallas_call(
        feed_kernel,
        grid=(steps,),
        in_specs=[
            pl.BlockSpec((rows, width), lambda i: (0, 0)),
            hidden_block,
            pl.BlockSpec((width, tile), lambda i: (0, i)),
            pl.BlockSpec((width, tile), lambda i: (0, i + steps)),
        ]
        + [ANYWHERE] * len(after),
        out_specs=[hidden_block] * 3,
        out_shape=[jax.ShapeDtypeStruct((rows, hidden), bf16)] * 3,
        compiler_params=pltpu.CompilerParams(vmem_limit_bytes=56 * 2**20),
        cost_estimate=cost(19.5),
    )(normed, d_act, gateup, gateup, *after)


def feed_back(d_gate, d_up, gateup, *after):
    rows, hidden = d_gate.shape
    width = gateup.shape[0]
    tile = math.gcd(width, 256)

    def kernel(d_gate_ref, d_up_ref, gate_ref, up_ref, *refs):
        total = nt_dot(d_gate_ref[...], gate_ref[...]) + nt_dot(d_up_ref[...], up_ref[...])
        refs[-1][...] = total.astype(bf16)

    whole = pl.BlockSpec((rows, hidden), lambda i: (0, 0))
    return pl.pallas_call(
        kernel,
        grid=(width // tile,),
        in_specs=[
            whole,
            whole,
            pl.BlockSpec((tile, hidden), lambda i: (i, 0)),
            pl.BlockSpec((tile, hidden), lambda i: (i, 1)),
        ]
        + [ANYWHERE] * len(after),
        out_specs=pl.BlockSpec((rows, tile), lambda i: (0, i)),
        out_shape=jax.ShapeDtypeStruct((rows, width), bf16),
        compiler_params=pltpu.CompilerParams(vmem_limit_bytes=56 * 2**20),
        cost_estimate=cost(17),
    )(d_gate, d_up, gateup, gateup, *after)


def feed_out(act, downs, down_start, *after):
    rows, hidden = act.shape
    width = downs.shape[0]
    tile = math.gcd(width, 256)
    step = math.gcd(math.gcd(hidden, down_start), 512)
    count = hidden // step

    def kernel(act_ref, *refs):
        total = jnp.zeros((rows, tile), f32)
        for at, ref in enumerate(refs[:count]):
            total = total + nt_dot(act_ref[:, at * step : (at + 1) * step], ref[...])
        refs[-1][...] = total.astype(bf16)

    return pl.pallas_call(
        kernel,
        grid=(width // tile,),
        in_specs=[pl.BlockSpec((rows, hidden), lambda i: (0, 0))]
        + [
            pl.BlockSpec((tile, step), functools.partial(lambda i, at: (i, at), at=at))
            for at in range(down_start // step, down_start // step + count)
        ]
        + [ANYWHERE] * len(after),
        out_specs=pl.BlockSpec((rows, tile), lambda i: (0, i)),
        out_shape=jax.ShapeDtypeStruct((rows, width), bf16),
        compiler_params=pltpu.CompilerParams(vmem_limit_bytes=56 * 2**20),
        cost_estimate=cost(9),
    )(act, *[downs] * count, *after)


def shards(
    tokens,
    w_query,
    w_keyval,
    w_out,
    w_gateup,
    w_down,
    attn_gain,
    ffn_gain,
    qk_gain,
    segments,
    positions,
    cotangent,
):
    ring = Ring()
    row_count = tokens.shape[0]
    depth = w_query.shape[0]
    model = tokens.shape[1]
    hidden = w_gateup.shape[2]
    tensor = lax.axis_index("tensor")
    query_width = w_query.shape[1]
    local_heads = query_width // HD
    local_kv = local_heads // GROUP
    kv_width = local_kv * HD
    all_kv = w_keyval.shape[1] // 2
    qkv_width = query_width + 2 * kv_width
    gain_count = 2 * qk_gain.shape[1]

    own_keyval = lax.dynamic_index_in_dim(
        w_keyval.reshape(depth, 2, all_kv // kv_width, kv_width), tensor, 2, keepdims=False
    ).reshape(depth, 2 * kv_width)
    head_gain_column = jnp.pad(qk_gain.reshape(gain_count), (0, depth - gain_count))
    gains = jnp.stack([attn_gain, ffn_gain, head_gain_column], axis=1)
    gains = jnp.pad(gains, ((0, 0), (0, LANES - gains.shape[1])))
    first_pack = jnp.concatenate([w_query, own_keyval, w_out.T, gains, w_down.T], axis=1)
    first_full = lax.all_gather(first_pack.astype(bf16), "dp", axis=0, tiled=True)
    gateup_full = lax.all_gather(
        w_gateup.reshape(depth, 2 * hidden).astype(bf16), "dp", axis=0, tiled=True
    )
    qkv_full = first_full[:, :qkv_width]
    gain_start = qkv_width + query_width
    out_full = first_full[:, qkv_width:gain_start]
    down_full = first_full[:, gain_start + LANES :]
    gain_columns = first_full[:, gain_start : gain_start + 3].astype(f32)
    attn_weight = gain_columns[:, 0]
    ffn_weight = gain_columns[:, 1]
    head_gains = gain_columns[:, 2].reshape(ring.count, depth)[:, :gain_count]
    head_gains = head_gains.reshape(ring.count, 2, qk_gain.shape[1]).transpose(1, 0, 2).reshape(2, HD)
    gain_query = head_gains[0][:, None]
    gain_key = head_gains[1][:, None]

    marks = (segments + 1).astype(bf16)
    seq_devices = min(SEQ_LEN // row_count, ring.count)
    own_sequence = ring.index // seq_devices
    reach_count = -(-WINDOW // row_count)
    halo_marks = []
    for step_back in range(reach_count, 0, -1):
        same_sequence = ((ring.index - step_back) // seq_devices == own_sequence).astype(bf16)
        halo_marks.append(from_behind(marks, step_back) * same_sequence)
    key_marks = jnp.concatenate(halo_marks + [marks], axis=0)
    key_count = key_marks.shape[0]
    distance = (jnp.arange(row_count, dtype=jnp.int32) + reach_count * row_count)[
        None, :
    ] - jnp.arange(key_count, dtype=jnp.int32)[:, None]
    allowed = (distance >= 0) & (distance < WINDOW) & (key_marks[:, None] == marks[None, :])
    bias = jnp.where(allowed, 0.0, MASKED).astype(f32)
    cos_table, sin_table = angles_of(positions)

    residual = tokens.astype(f32)
    attn_scale = inverse_rms(residual, 1)

    normed_low = (residual * attn_scale * attn_weight).astype(bf16)
    qkv_raw = lax.dot_general(
        qkv_full, normed_low, (((0,), (1,)), ((), ())), preferred_element_type=f32
    )
    query_raw = qkv_raw[:query_width].reshape(local_heads, HD, row_count)
    key_raw = qkv_raw[query_width : query_width + kv_width].reshape(local_kv, HD, row_count)
    query_scale = inverse_rms(query_raw, 1)
    key_scale = inverse_rms(key_raw, 1)
    query_low = rotate(query_raw * query_scale * gain_query, cos_table, sin_table).astype(bf16)
    key_low = rotate(key_raw * key_scale * gain_key, cos_table, sin_table).astype(bf16)
    query_low = query_low.reshape(query_width, row_count)
    keyval_low = jnp.concatenate(
        [key_low.reshape(kv_width, row_count), qkv_raw[query_width + kv_width :].astype(bf16)], axis=0
    )
    halo = [from_behind(keyval_low, step_back) for step_back in range(reach_count, 0, -1)]
    key_keyval = jnp.concatenate(halo + [keyval_low], axis=1)
    keys_t = key_keyval[:kv_width]
    values_t = key_keyval[kv_width:]
    keys = keys_t.reshape(local_kv, HD, key_count).transpose(0, 2, 1)
    values = values_t.reshape(local_kv, HD, key_count).transpose(0, 2, 1)
    attended, inverse_total = attend(query_low, keys, values_t, bias)
    mid_part = lax.dot_general(
        attended, out_full, (((0,), (1,)), ((), ())), preferred_element_type=f32
    )
    near_first = ring.bits
    normed_rows = ring.chosen(normed_low, near_first)
    cotangent_rows = transposed(cotangent)
    attended_back = attended.T
    mid = residual + tensor_sum(
        mid_part, corner(normed_rows), corner(cotangent_rows), corner(attended_back)
    )

    d_act = nn_dot(cotangent, down_full)
    ffn_scale = inverse_rms(mid, 1)
    normed2_low = (mid * ffn_scale * ffn_weight).astype(bf16)
    normed2_rows = ring.chosen(normed2_low, near_first)
    act_low, d_gate, d_up = feed(normed2_low, d_act, gateup_full, normed2_rows)
    gate_sum = Scatter(ring, normed2_rows, d_gate, near_first)
    up_sum = Scatter(ring, normed2_rows, d_up, near_first)
    sums = {"G": gate_sum, "U": up_sum}
    totals = {}
    heads = 0
    grads = ()
    down_low = None
    before = None
    for step in ORDER:
        after = () if before is None else (before,)
        if step in sums:
            one = sums[step]
            if len(one.got) < len(one.bits) and step not in totals:
                before = one.send(*after, parts=PARTS if step in "OQK" and not one.got else 1)
                if len(one.got) == 4:
                    while len(one.got) < len(one.bits):
                        before = one.send(before)
            else:
                before = totals[step] = one.total(*after, transposed=step == "O")
        elif step == "D":
            if down_low is None:
                before = product(cotangent_rows, act_low, model, 0, [], after)[0]
                down_low = lax.psum_scatter(before, "dp", scatter_dimension=0, tiled=True)
            else:
                before = totals["D"] = turned(down_low, *after)
        elif step == "FB":
            before = d_normed2_low = feed_back(d_gate, d_up, gateup_full, *after)
            d_normed2_other = other_tensor(d_normed2_low)
        elif step == "FO":
            before = result_low = feed_out(act_low, first_full, gain_start + LANES, *after)
        elif step == "NB":
            d_mid, d_mid_low, d_ffn_weight = norm_back(
                mid, cotangent, d_normed2_low, d_normed2_other, ffn_weight, *after
            )
            before = d_mid_low
            result_other = other_tensor(tie(result_low, d_normed2_other))
        elif step == "DA":
            before = d_attended = product_tt(first_full, qkv_width, query_width, d_mid_low)
        elif step == "H":
            grads = attend_back(
                heads,
                grads,
                after,
                query_low,
                keys,
                keys_t,
                values,
                d_attended,
                attended,
                inverse_total,
                bias,
            )
            heads += 1
            d_query, d_keys, d_values = grads
            before = d_keys
        elif step == "HP":
            halo_grads = halo_parts(d_keys, d_values, row_count, *after)
            got = [from_behind(part, at - reach_count) for at, part in enumerate(halo_grads)]
            before = halo_grads[0]
        elif step == "QB":
            d_query_low, d_gain_query = query_back(
                d_query, qkv_raw, cos_table[0], sin_table[0], gain_query, *after
            )
            before = d_query_low
            sums["Q"] = Scatter(ring, normed_rows, d_query_low, near_first)
        elif step == "OP":
            before = d_mid_rows = ring.chosen(tie(d_mid_low, *after), near_first)
            sums["O"] = Scatter(ring, d_mid_rows, attended_back, near_first)
        elif step == "KB":
            d_keyval_low, d_gain_key = key_back(
                d_keys,
                d_values,
                got,
                qkv_raw,
                query_width,
                cos_table[0],
                sin_table[0],
                gain_key,
                *after,
            )
            before = d_keyval_low
        elif step == "IB":
            d_normed_low, d_attn_part = input_back(
                d_query_low, d_keyval_low, first_full, tokens, attn_scale, *after
            )
            d_normed_other = other_tensor(d_normed_low)
            before = d_normed_low
        elif step == "GB":
            places = jnp.arange(2 * HD, dtype=jnp.int32)
            per_device = gain_count // 2
            places = (
                places % HD // per_device * depth
                + places // HD * per_device
                + places % per_device
            )
            places = (places[:, None] == jnp.arange(model, dtype=jnp.int32)[None, :]).astype(bf16)
            gain_grads = gain_block(
                d_attn_part, d_ffn_weight, d_gain_query, d_gain_key, places, *after
            )
            before = gain_rows = ring.chosen(gain_grads, near_first)
            sums["K"] = Scatter(ring, normed_rows, d_keyval_low, near_first, gain_rows)
        elif step == "AD":
            before = output = add_up(mid, result_low, result_other, *after)
        elif step == "IG":
            _, input_grad, _ = norm_back(
                tokens, d_mid, d_normed_low, d_normed_other, attn_weight, *after
            )
            before = input_grad
    grad_down, grad_out, grad_query = totals["D"], totals["O"], totals["Q"]
    grad_gateup = side_by_side(totals["G"], totals["U"])
    shared = totals["K"].astype(bf16)
    grad_keyval, gains_t = both_tensors(shared, other_tensor(shared), tensor, kv_width)
    grad_attn_gain = gains_t[0]
    grad_ffn_gain = gains_t[1]
    grad_heads = gains_t[2, :gain_count].reshape(2, gain_count // 2)
    return (
        output,
        input_grad,
        grad_query,
        grad_keyval,
        grad_out,
        grad_gateup,
        grad_down,
        grad_attn_gain,
        grad_ffn_gain,
        grad_heads,
    )


def solution(mesh):
    in_specs = (
        P("dp", None),
        P("dp", "tensor"),
        P("dp", None),
        P("tensor", "dp"),
        P("dp", None, "tensor"),
        P("tensor", "dp"),
        P("dp"),
        P("dp"),
        P(None, "dp"),
        P("dp"),
        P("dp"),
        P("dp", None),
    )
    out_specs = (
        P("dp", None),
        P("dp", None),
        P("dp", "tensor"),
        P("dp", None),
        P("tensor", "dp"),
        P("dp", None, "tensor"),
        P("tensor", "dp"),
        P("dp"),
        P("dp"),
        P(None, "dp"),
    )
    return jax.shard_map(shards, mesh=mesh, in_specs=in_specs, out_specs=out_specs, check_vma=False)
```
